128 devices in a mesh: view: 16 (over x_lo, y, core), fsdp: 8 (over x_hi, z).
Axes of the slice: x: 4 (x_hi: 2, x_lo: 2; x = x_hi * 2 + x_lo), y: 4, z: 4, core: 2. Of those that a mesh axis runs over, the one named last changes fastest.
Arguments:
- latents: bfloat16 [8, 16, 2, 256, 1024], P('fsdp', 'view'), may hold values from -17 to 17
- w_qkv: bfloat16 [1024, 3072], P('fsdp'), may hold values from -0.1875 to 0.1875
- cycle_links: int32 [8, 16], P('fsdp'), may hold values 0 or 1
- cross_links: int32 [8, 8], P('fsdp'), may hold values 0 or 1
- d_attended: bfloat16 [8, 16, 2, 256, 1024], P('fsdp', 'view'), may hold values from -6 to 6
Outputs:
- attended: bfloat16 [8, 16, 2, 256, 1024], P('fsdp', 'view')
- d_latents: bfloat16 [8, 16, 2, 256, 1024], P('fsdp', 'view')
- d_wqkv: float32 [1024, 3072], P('fsdp')
The draws below stay inside these ranges and needn't reach their ends.
All inputs are finite; a program needn't handle non-finite values. No bound on the sum of `cycle_links` or of `cross_links` on one device may be relied on, other than what follows from the above.
Results may differ from the reference program's by a relative error of at most 0.012.
The reference program's roundings to bfloat16 on the way (of `projected`, `rounded_probs`, `grad_scores` and `grad_proj`) count: a program that leaves them out, or rounds other values in their place, can miss the bound.
Values may be sent and summed in bfloat16 or wider, within the bound.
A program may use at most 128 MiB of HBM per device.

```python
import jax
import jax.numpy as jnp
from jax import lax

D = 1024
HEAD_DIM = 64
TOK = 256
SAMPLES = 2
VIEWS = 16
SCENES = 8


def draw_latents(key, part):
    key = jax.random.fold_in(key, 7)
    base_key = jax.random.fold_in(key, 0)
    full_shape = (SCENES, VIEWS, SAMPLES, TOK, D)
    values = jax.random.truncated_normal(base_key, -6.0, 6.0, full_shape, jnp.float32)
    return values.astype(jnp.bfloat16)


def touch_ends(entries, stream_key, smallest, high):
    longest = entries.shape.index(max(entries.shape))
    spots = []
    for shift in (0, 1):
        where = [jax.random.randint(jax.random.fold_in(stream_key, axis), (), 0, length) for axis, length in enumerate(entries.shape)]
        where[longest] = (where[longest] + shift) % entries.shape[longest]
        spots.append(tuple(where))
    return entries.at[spots[0]].set(smallest).at[spots[1]].set(high)


def block_levels(stream_key, extent, shards, low, top_value):
    level = 1.0
    for axis_at, blocks in shards:
        heights = jax.random.uniform(jax.random.fold_in(jax.random.fold_in(stream_key, 6), axis_at), (blocks,), jnp.float32, low / len(shards), top_value / len(shards))
        level = level * jnp.repeat(jnp.exp(heights), extent[axis_at] // blocks).reshape((-1,) + (1,) * (len(extent) - 1 - axis_at))
    return level


def bell_draw(key, shape, width, reach, pieces=(), kind=jnp.bfloat16):
    result = jax.random.normal(key, shape, jnp.float32) * width
    if len(pieces) > 0:
        result = block_levels(key, shape, pieces, -0.22, 0.18) * result
    return jnp.clip(result, min=-reach, max=reach).astype(kind)


def setup_inputs(seed: int = 0) -> dict:
    splits = jax.random.split(jax.random.key(seed), 6)
    latents = draw_latents(jax.random.fold_in(splits[5], 71), 0)
    w_qkv = bell_draw(splits[1], (D, 3 * D), D ** -0.5, 0.1875, ((0, 8),))
    cycle_links = touch_ends((jax.random.randint(splits[2], (SCENES, VIEWS), 0, 2) < 1).astype(jnp.int32), jax.random.fold_in(splits[2], 1), 0, 1)
    cross_links = touch_ends((jax.random.randint(splits[3], (SCENES, VIEWS // 2), 0, 2) < 1).astype(jnp.int32), jax.random.fold_in(splits[3], 1), 0, 1)
    d_attended = bell_draw(splits[4], (SCENES, VIEWS, SAMPLES, TOK, D), 1.0, 6.0, ((0, 8), (1, 16)))
    return {"latents": latents, "w_qkv": w_qkv, "cycle_links": cycle_links, "cross_links": cross_links, "d_attended": d_attended}


score_scale = 0.125


def rounded(values):
    return lax.optimization_barrier(values.astype(jnp.bfloat16)).astype(jnp.float32)


def scene_pass(latent_scene, w_qkv, cycle_scene, cross_scene, dout_scene):
    view_total = latent_scene.shape[0]
    samples = latent_scene.shape[1]
    tokens_view = latent_scene.shape[2]
    model_width = latent_scene.shape[3]
    head_count = model_width // HEAD_DIM
    half_cycle = view_total // 2
    offsets = (1, -1, 2, -2, half_cycle)
    flat_rows = latent_scene.reshape(-1, model_width)
    projected = rounded(jnp.dot(flat_rows, w_qkv, preferred_element_type=jnp.float32))
    projected = projected.reshape(view_total, samples, tokens_view, 3 * model_width)
    cycle_float = cycle_scene.astype(jnp.float32)
    cross_float = jnp.concatenate([cross_scene, cross_scene]).astype(jnp.float32)
    ones_float = jnp.ones_like(cycle_float)
    link_mask = jnp.stack([ones_float, ones_float, jnp.roll(cycle_float, 2), cycle_float, cross_float], axis=1)

    def view_step(key_grads, view_pos):
        own_rows = projected[view_pos]
        queries = own_rows[:, :, :model_width].reshape(samples, tokens_view, head_count, HEAD_DIM)
        sources = [view_pos] + [(view_pos - offset) % view_total for offset in offsets]
        kv_all = jnp.concatenate([projected[source][:, :, model_width:] for source in sources], axis=1)
        key_part = kv_all[:, :, :model_width].reshape(samples, 6 * tokens_view, head_count, HEAD_DIM)
        value_part = kv_all[:, :, model_width:].reshape(samples, 6 * tokens_view, head_count, HEAD_DIM)
        slot_mask = jnp.concatenate([jnp.ones((1,), jnp.float32), link_mask[view_pos]])
        key_mask = jnp.repeat(slot_mask, tokens_view)
        scores = jnp.einsum('bqhd,bkhd->bhqk', queries, key_part) * score_scale
        masked = jnp.where(key_mask > 0.5, scores, -1e30)
        row_peak = jnp.max(masked, axis=-1, keepdims=True)
        weights_raw = jnp.exp(masked - row_peak)
        denominator = jnp.sum(weights_raw, axis=-1, keepdims=True)
        probabilities = weights_raw / denominator
        rounded_probs = rounded(probabilities)
        output = jnp.einsum('bhqk,bkhd->bqhd', rounded_probs, value_part)
        attended = output.astype(jnp.bfloat16).reshape(samples, tokens_view, model_width)
        grad_out = dout_scene[view_pos].astype(jnp.float32).reshape(samples, tokens_view, head_count, HEAD_DIM)
        row_delta = jnp.transpose(jnp.sum(grad_out * output, axis=-1), (0, 2, 1))[..., None]
        grad_probs = jnp.einsum('bqhd,bkhd->bhqk', grad_out, value_part)
        grad_scores = rounded(probabilities * (grad_probs - row_delta) * score_scale)
        grad_query = jnp.einsum('bhqk,bkhd->bqhd', grad_scores, key_part).reshape(samples, tokens_view, model_width)
        grad_key = jnp.einsum('bhqk,bqhd->bkhd', grad_scores, queries).reshape(samples, 6 * tokens_view, model_width)
        grad_value = jnp.einsum('bhqk,bqhd->bkhd', rounded_probs, grad_out).reshape(samples, 6 * tokens_view, model_width)
        grad_kv = jnp.concatenate([grad_key, grad_value], axis=-1)
        key_grads = key_grads.at[view_pos].add(grad_kv[:, :tokens_view])
        for neighbour in range(5):
            returned = rounded(grad_kv[:, (neighbour + 1) * tokens_view:(neighbour + 2) * tokens_view])
            key_grads = key_grads.at[sources[neighbour + 1]].add(returned)
        return key_grads, (attended, grad_query)

    key_grads = jnp.zeros((view_total, samples, tokens_view, 2 * model_width), jnp.float32)
    key_grads, (attended, grad_query) = lax.scan(view_step, key_grads, jnp.arange(view_total, dtype=jnp.int32))
    grad_proj = jnp.concatenate([grad_query, key_grads], axis=-1).astype(jnp.bfloat16).reshape(-1, 3 * model_width)
    grad_latent = jnp.dot(grad_proj, w_qkv.T, preferred_element_type=jnp.float32).astype(jnp.bfloat16)
    grad_latent = grad_latent.reshape(latent_scene.shape)
    grad_weight = lax.dot_general(flat_rows, grad_proj, (((0,), (0,)), ((), ())), preferred_element_type=jnp.float32)
    return attended, grad_latent, grad_weight


def reference(latents, w_qkv, cycle_links, cross_links, d_attended):
    def one_scene(packed):
        return scene_pass(packed[0], w_qkv, packed[1], packed[2], packed[3])

    attended, grad_latents, grad_weights = lax.map(one_scene, (latents, cycle_links, cross_links, d_attended))
    return attended, grad_latents, jnp.sum(grad_weights, axis=0)
```

```python
import functools

import jax
import jax.numpy as jnp
from jax import lax
from jax.experimental import pallas as pl
from jax.experimental.pallas import tpu as pltpu
from jax.sharding import PartitionSpec as P

BF, F32 = jnp.bfloat16, jnp.float32
MESH = pl.DeviceIdType.MESH
TOK = 256
LOG2E = 1.4426950408889634
SCALE = 0.125
NT = (((1,), (1,)), ((), ()))
NN = (((1,), (0,)), ((), ()))
TN = (((0,), (0,)), ((), ()))
VMEM_LIMIT = 60 * 2**20


class Place:
    def __init__(self):
        v, f = lax.axis_index("view"), lax.axis_index("fsdp")
        self.view, self.fsdp = v, f
        self.ys, self.zs = 4, 4
        self.core = v % 2
        self.y = (v // 2) % 4
        self.x_lo = v // 8
        self.z = f % 4
        self.x_hi = f // 4
        column = self.x_lo * 8 + self.core

        def at(view, fsdp):
            return {"view": view, "fsdp": fsdp}

        self.up = at(column + 2 * ((self.y + 1) % 4), f)
        self.down = at(column + 2 * ((self.y + 3) % 4), f)
        self.over = at(column + 2 * ((self.y + 2) % 4), f)
        self.pair = at((v + 8) % 16, f)
        self.mate = at(v + 1 - 2 * self.core, f)
        self.f_up = self.x_hi * 4 + (self.z + 1) % 4
        self.f_down = self.x_hi * 4 + (self.z + 3) % 4
        self.f_far = self.x_hi * 4 + (self.z + 2) % 4
        self.f_outer = (f + 4) % 8
        self.z_up = at(v, self.f_up)
        self.z_down = at(v, self.f_down)
        self.outer = at((v + 8) % 16, self.f_outer)


def greet(devices):
    barrier = pltpu.get_barrier_semaphore()
    for device in devices:
        pl.semaphore_signal(barrier, inc=1, device_id=device, device_id_type=MESH)
    pl.semaphore_wait(barrier, len(devices))


class Mail:
    def __init__(self, send, recv):
        self.send, self.recv, self.made, self.sent = send, recv, 0, []

    def copy(self, src, dst, to):
        i = self.made
        self.made += 1
        made = self.again(i, src, dst, to)
        self.sent.append(made)
        return made

    def again(self, i, src, dst, to):
        return pltpu.make_async_remote_copy(
            src_ref=src, dst_ref=dst, send_sem=self.send.at[i], recv_sem=self.recv.at[i],
            device_id=to, device_id_type=MESH)

    def finish(self):
        for copy in self.sent:
            copy.wait_send()


def at(start, size):
    return pl.ds(pl.multiple_of(start, size), size)


def dot(a, b, dims=NN):
    return lax.dot_general(a, b, dims, preferred_element_type=F32)


def gather_kernel(lat_ref, w_ref, g_ref, lat_all, w_all, g_all, local, send, recv):
    me = Place()
    c = me.core
    rows = w_ref.shape[0]
    half = w_ref.shape[1] // 6
    samples, toks = lat_ref.shape[0], lat_ref.shape[1]
    chunks = [(s, pl.ds(t * (toks // 2), toks // 2)) for s in range(samples) for t in range(2)]
    own_block, other_block = 3 + c, 4 - c
    locals_ = []
    for k in range(3):
        locals_.append(pltpu.make_async_copy(
            w_ref.at[:, pl.ds(pl.multiple_of((2 * k + c) * half, half), half)],
            w_all.at[pl.ds(pl.multiple_of(me.fsdp * rows, rows), rows), pl.ds(k * half, half)],
            local.at[k]))
    for s in range(samples):
        locals_.append(pltpu.make_async_copy(lat_ref.at[s], lat_all.at[s, own_block], local.at[3 + s]))
        locals_.append(pltpu.make_async_copy(
            g_ref.at[s, :, pl.ds(pl.multiple_of(c * half, half), half)],
            g_all.at[s, pl.ds(pl.multiple_of(c * toks, toks), toks), :], local.at[5 + s]))
    for copy in locals_:
        copy.start()
    greet((me.up, me.down, me.pair, me.mate, me.z_up, me.z_down, me.outer))

    mail = Mail(send, recv)
    remote = mail.copy

    def block(b, chunk):
        s, t = chunk
        return lat_all.at[s, b, t]

    def shard(f, part=None):
        if part is None:
            return w_all.at[pl.ds(pl.multiple_of(f * rows, rows), rows)]
        return w_all.at[pl.ds(pl.multiple_of(f * rows + part * (rows // 2), rows // 2), rows // 2)]

    n = range(len(chunks))
    mine = [lat_ref.at[s, t] for s, t in chunks]
    to_pair = [remote(mine[i], block(7 * c, chunks[i]), me.pair) for i in n]
    to_mate = [remote(mine[i], block(own_block, chunks[i]), me.mate) for i in n]
    up = [remote(mine[i], block(1 + c, chunks[i]), me.up) for i in n]
    down = [remote(mine[i], block(5 + c, chunks[i]), me.down) for i in n]
    up_far = [mail.again(2 * len(chunks) + i, block(7 * c, chunks[i]), block(1 + c, chunks[i]), me.up) for i in n]
    down_far = [mail.again(3 * len(chunks) + i, block(7 * c, chunks[i]), block(5 + c, chunks[i]), me.down) for i in n]
    relay_pair = [remote(block(7 * c, chunks[i]), block(7 * c, chunks[i]), me.mate) for i in n]
    relay_up = [remote(block(1 + c, chunks[i]), block(1 + c, chunks[i]), me.mate) for i in n]
    relay_down = [remote(block(5 + c, chunks[i]), block(5 + c, chunks[i]), me.mate) for i in n]
    g_mate = [remote(
        g_ref.at[s, :, pl.ds(pl.multiple_of((1 - c) * half, half), half)],
        g_all.at[s, pl.ds(pl.multiple_of(c * toks, toks), toks), :], me.mate) for s in range(samples)]

    first, last = me.y == 0, me.y == me.ys - 1
    f0, fz_up, fz_down, f_out = me.fsdp, me.f_up, me.f_down, me.f_outer
    w_up = remote(shard(f0), shard(f0), me.z_up)
    w_down = remote(shard(f0), shard(f0), me.z_down)
    w_out = remote(shard(f0), shard(f0), me.outer)
    w_up2 = remote(shard(fz_down, 0), shard(fz_down, 0), me.z_up)
    w_down2 = remote(shard(fz_up, 1), shard(fz_up, 1), me.z_down)
    o_up = remote(shard(f_out), shard(f_out), me.z_up)
    o_down = remote(shard(f_out), shard(f_out), me.z_down)
    far = me.f_far
    o_far = [remote(shard(far, part), shard(far, part), me.outer) for part in range(2)]

    for i in n:
        to_pair[i].start()
        if i == 0:
            for copy in locals_[:3]:
                copy.wait()
            w_up.start()
            w_down.start()
            w_out.start()

        @pl.when(jnp.logical_not(last))
        def _(i=i):
            up[i].start()

        @pl.when(jnp.logical_not(first))
        def _(i=i):
            down[i].start()
    for i in n:
        to_mate[i].start()
    for copy in g_mate:
        copy.start()

    def pair_in(i):
        to_pair[i].wait_recv()

        @pl.when(last)
        def _():
            up_far[i].start()

        @pl.when(first)
        def _():
            down_far[i].start()
        relay_pair[i].start()

    def y_in(i):
        up[i].wait_recv()
        relay_up[i].start()
        down[i].wait_recv()
        relay_down[i].start()

    pair_in(0)
    w_up.wait_recv()
    w_up2.start()
    w_down.wait_recv()
    w_down2.start()
    w_out.wait_recv()
    o_up.start()
    o_down.start()
    pair_in(1)
    y_in(0)
    w_up2.wait_recv()
    o_far[0].start()
    w_down2.wait_recv()
    o_far[1].start()
    pair_in(2)
    y_in(1)
    pair_in(3)
    y_in(2)
    y_in(3)
    for copy in (o_up, o_down, *o_far):
        copy.wait_recv()
    for copy in (*to_mate, *relay_pair, *relay_up, *relay_down, *g_mate):
        copy.wait_recv()
    mail.finish()
    for copy in locals_[3:]:
        copy.wait()


def view_pass(bias_ref, view, q, g, k_ref, v_ref, kt, vt, gt, st, dp, pb, gs):
    lane = lax.broadcasted_iota(jnp.int32, (1, 128), 1)
    outs, dqs, qms, gms = [], [], [], []
    for h in range(2):
        mine = (lane >= 64) if h else (lane < 64)
        qm = jnp.where(mine, q, jnp.zeros_like(q))
        gm = jnp.where(mine, g, jnp.zeros_like(g))
        qms.append(qm)
        gms.append(gm)
        tops = []
        for j in range(6):
            rows = pl.ds(j * TOK, TOK)
            s = dot(k_ref[pl.ds((2 * view + j) * TOK, TOK), :], qm, NT)
            st[h, rows, :] = s
            tops.append(jnp.max(s, axis=0, keepdims=True) * (SCALE * LOG2E) + bias_ref[view, j])
        top = functools.reduce(jnp.maximum, tops)
        total = jnp.zeros((1, TOK), F32)
        for j in range(6):
            rows = pl.ds(j * TOK, TOK)
            e = jnp.exp2(st[h, rows, :] * (SCALE * LOG2E) - (top - bias_ref[view, j]))
            st[h, rows, :] = e
            total = total + jnp.sum(e, axis=0, keepdims=True)
        inv = 1.0 / total
        for j in range(6):
            rows = pl.ds(j * TOK, TOK)
            p = st[h, rows, :] * inv
            st[h, rows, :] = p
            pb[rows, h * TOK:(h + 1) * TOK] = p.astype(BF)
        ot = dot(vt, pb[:, h * TOK:(h + 1) * TOK])[h * 64:(h + 1) * 64]
        outs.append(ot)
        delta = jnp.sum(gt[h * 64:(h + 1) * 64] * ot, axis=0, keepdims=True)
        for j in range(6):
            rows = pl.ds(j * TOK, TOK)
            d = dot(v_ref[pl.ds((2 * view + j) * TOK, TOK), :], gm, NT)
            gs[rows, h * TOK:(h + 1) * TOK] = (st[h, rows, :] * (d - delta)).astype(BF)
        dqs.append(dot(kt, gs[:, h * TOK:(h + 1) * TOK])[h * 64:(h + 1) * 64])
    return (
        jnp.concatenate(outs, axis=0),
        jnp.concatenate(dqs, axis=0) * SCALE,
        jnp.concatenate(qms, axis=0),
        jnp.concatenate(gms, axis=0),
    )


def attn_kernel(bias_ref, q_ref, g_ref, k_ref, v_ref, att_ref, dq_ref, own_ref, term_ref, st, dp, pb, gs):
    kt = k_ref[0].T
    vt = v_ref[0].T
    k, v = k_ref.at[0], v_ref.at[0]
    held = []
    for view in range(2):
        rows = pl.ds(view * TOK, TOK)
        q, g = q_ref[0, rows, :], g_ref[0, rows, :]
        gt = g.astype(F32).T
        span = slice(2 * view * TOK, (2 * view + 6) * TOK)
        pbv, gsv = pb.at[view], gs.at[view]
        ot, dqt, qm, gm = view_pass(
            bias_ref, view, q, g, k, v, kt[:, span], vt[:, span], gt, st.at[view], dp, pbv, gsv
        )
        att_ref[0, rows, :] = ot.T.astype(BF)
        dq_ref[0, rows, :] = dqt.T.astype(BF)
        held.append((qm, gm))
    for b in range(8):
        parts = []
        for view in range(2):
            j = b - 2 * view
            if 0 <= j < 6:
                qm, gm = held[view]
                rows = pl.ds(j * TOK, TOK)
                dk = dot(gs[view, rows, :], qm) * SCALE
                dv = dot(pb[view, rows, :], gm)
                parts.append((dk, dv))
        dk, dv = parts[0]
        if b in (3, 4):
            own = b - 3
            other = parts[1 - own]
            mine = parts[own]
            rows = pl.ds(own * TOK, TOK)
            own_ref[0, 0, rows, :] = mine[0] + other[0].astype(BF).astype(F32)
            own_ref[1, 0, rows, :] = mine[1] + other[1].astype(BF).astype(F32)
        else:
            if len(parts) == 2:
                dk = dk.astype(BF).astype(F32) + parts[1][0].astype(BF).astype(F32)
                dv = dv.astype(BF).astype(F32) + parts[1][1].astype(BF).astype(F32)
            n, w = {0: (2, 0), 1: (0, 0), 2: (0, 1), 5: (1, 0), 6: (1, 1), 7: (2, 1)}[b]
            rows = pl.ds(w * TOK, TOK)
            term_ref[n, 0, 0, rows, :] = dk.astype(BF)
            term_ref[n, 1, 0, rows, :] = dv.astype(BF)


def attention(bias, q, g, kv):
    S = q.shape[0]
    W = q.shape[2]
    pairs = W // 128
    return pl.pallas_call(
        attn_kernel,
        grid=(pairs, S),
        in_specs=[
            pl.BlockSpec(memory_space=pltpu.SMEM),
            pl.BlockSpec((1, 512, 128), lambda p, s: (s, 0, p)),
            pl.BlockSpec((1, 512, 128), lambda p, s: (s, 0, p)),
            pl.BlockSpec((1, 2048, 128), lambda p, s: (s, 0, p)),
            pl.BlockSpec((1, 2048, 128), lambda p, s: (s, 0, pairs + p)),
        ],
        out_specs=[
            pl.BlockSpec((1, 512, 128), lambda p, s: (s, 0, p)),
            pl.BlockSpec((1, 512, 128), lambda p, s: (s, 0, p)),
            pl.BlockSpec((2, 1, 512, 128), lambda p, s: (0, s, 0, p)),
            pl.BlockSpec((3, 2, 1, 512, 128), lambda p, s: (0, 0, s, 0, p)),
        ],
        out_shape=[
            jax.ShapeDtypeStruct((S, 512, W), BF),
            jax.ShapeDtypeStruct((S, 512, W), BF),
            jax.ShapeDtypeStruct((2, S, 512, W), F32),
            jax.ShapeDtypeStruct((3, 2, S, 512, W), BF),
        ],
        scratch_shapes=[
            pltpu.VMEM((2, 2, 1536, TOK), F32),
            pltpu.VMEM((8, 128), F32),
            pltpu.VMEM((2, 1536, 2 * TOK), BF),
            pltpu.VMEM((2, 1536, 2 * TOK), BF),
        ],
        compiler_params=pltpu.CompilerParams(vmem_limit_bytes=60 * 2**20),
    )(bias, q, g, kv, kv)


def terms_kernel(term_ref, own_ref, dq_ref, att_ref, gp_ref, att_full, inbox, joined, local, send, recv):
    me = Place()
    c = me.core
    mail = Mail(send, recv)
    samples = dq_ref.shape[0]
    width = dq_ref.shape[2]
    parts = [(i, s) for i in range(2) for s in range(samples)]
    greet((me.up, me.down, me.pair, me.mate))
    first, last = me.y == 0, me.y == me.ys - 1
    ups = [mail.copy(term_ref.at[1, i, s], inbox.at[1, i, s], me.up) for i, s in parts]
    downs = [mail.copy(term_ref.at[0, i, s], inbox.at[0, i, s], me.down) for i, s in parts]
    pairs = [mail.copy(term_ref.at[2, i, s], inbox.at[2, i, s], me.pair) for i, s in parts]
    n = len(parts)
    pairs_joined = [mail.again(2 * n + a, joined.at[i, s], inbox.at[2, i, s], me.pair) for a, (i, s) in enumerate(parts)]
    edge = jnp.logical_or(first, last)
    for a in range(n):
        ups[a].start()
        downs[a].start()

        @pl.when(jnp.logical_not(edge))
        def _(a=a):
            pairs[a].start()
    mine = at(c * width, width)
    att_mate = [mail.copy(att_ref.at[s, at((1 - c) * TOK, TOK)], att_full.at[s, :, mine], me.mate) for s in range(samples)]
    for copy in att_mate:
        copy.start()
    att_own = [pltpu.make_async_copy(att_ref.at[s, at(c * TOK, TOK)], att_full.at[s, :, mine], local.at[s]) for s in range(samples)]
    for copy in att_own:
        copy.start()
    gp_ref[:, :, :width] = dq_ref[...]
    for a, (i, s) in enumerate(parts):
        ups[a].wait_recv()
        downs[a].wait_recv()

        @pl.when(first)
        def _(a=a, i=i, s=s):
            joined[i, s] = (term_ref[2, i, s].astype(F32) + inbox[1, i, s].astype(F32)).astype(BF)
            pairs_joined[a].start()

        @pl.when(last)
        def _(a=a, i=i, s=s):
            joined[i, s] = (term_ref[2, i, s].astype(F32) + inbox[0, i, s].astype(F32)).astype(BF)
            pairs_joined[a].start()
    from_down = jnp.where(first, 0.0, 1.0)
    from_up = jnp.where(last, 0.0, 1.0)
    for a, (i, s) in enumerate(parts):
        pairs[a].wait_recv()
        total = own_ref[i, s] + inbox[2, i, s].astype(F32)
        total = total + inbox[1, i, s].astype(F32) * from_down + inbox[0, i, s].astype(F32) * from_up
        gp_ref[s, :, (1 + i) * width:(2 + i) * width] = total.astype(BF)
    for copy in att_mate:
        copy.wait_recv()
    for copy in att_own:
        copy.wait()
    mail.finish()


def reduce_kernel(dw_ref, dl_ref, dw_out, dl_out, *scratch):
    (dl_in, z1u, z1d, z2u, z2d, sent_u, sent_d, zsum, xin, xa_in, xa, q1u, q1d, q2u, q2d, qsent_u, qsent_d,
     whole, v1, vsum, v2, last_own, lastg, mate_in, send, recv) = scratch
    me = Place()
    c = me.core
    mail = Mail(send, recv)
    rows = dw_ref.shape[2]
    width = dw_ref.shape[3]
    hw = width // 2
    qw = width // 4
    greet((me.up, me.down, me.over, me.pair, me.mate, me.z_up, me.z_down, me.outer))
    z, xh = me.z, me.x_hi
    zu, zd, zf = (z + 1) % 4, (z + 3) % 4, (z + 2) % 4
    H1, H2 = pl.ds(0, qw), pl.ds(qw, qw)
    H3, H4 = pl.ds(hw, qw), pl.ds(hw + qw, qw)
    ZC, XC = pl.ds(0, hw), pl.ds(hw, hw)
    a1u = mail.copy(dw_ref.at[:, zf, :, H1], z1u, me.z_up)
    a1d = mail.copy(dw_ref.at[:, zf, :, H2], z1d, me.z_down)
    bx = mail.copy(dw_ref.at[1 - xh, :, :, XC], xa_in, me.outer)
    dlm = mail.copy(dl_ref.at[:, 1 - c], dl_in, me.mate)
    for copy in (a1u, a1d, bx, dlm):
        copy.start()
    sent_u[:, :, qw:] = dw_ref[:, zu, :, qw:hw]
    sent_d[:, :, :qw] = dw_ref[:, zd, :, :qw]
    a1u.wait_recv()
    sent_u[:, :, :qw] = (dw_ref[:, zu, :, :qw].astype(F32) + z1u[...].astype(F32)).astype(BF)
    a2u = mail.copy(sent_u, z2u, me.z_up)
    a2u.start()
    a1d.wait_recv()
    sent_d[:, :, qw:] = (dw_ref[:, zd, :, qw:hw].astype(F32) + z1d[...].astype(F32)).astype(BF)
    a2d = mail.copy(sent_d, z2d, me.z_down)
    a2d.start()
    a2u.wait_recv()
    a2d.wait_recv()
    zsum[...] = (dw_ref[:, z, :, :hw].astype(F32) + z2u[...].astype(F32) + z2d[...].astype(F32)).astype(BF)
    ax = mail.copy(zsum.at[1 - xh], xin, me.outer)
    ax.start()
    bx.wait_recv()
    xa[...] = (dw_ref[xh, :, :, hw:].astype(F32) + xa_in[...].astype(F32)).astype(BF)
    b1u = mail.copy(xa.at[zf, :, pl.ds(0, qw)], q1u, me.z_up)
    b1d = mail.copy(xa.at[zf, :, pl.ds(qw, qw)], q1d, me.z_down)
    b1u.start()
    b1d.start()
    qsent_u[:, qw:] = xa[zu, :, qw:]
    qsent_d[:, :qw] = xa[zd, :, :qw]
    b1u.wait_recv()
    qsent_u[:, :qw] = (xa[zu, :, :qw].astype(F32) + q1u[...].astype(F32)).astype(BF)
    b2u = mail.copy(qsent_u, q2u, me.z_up)
    b2u.start()
    b1d.wait_recv()
    qsent_d[:, qw:] = (xa[zd, :, qw:].astype(F32) + q1d[...].astype(F32)).astype(BF)
    b2d = mail.copy(qsent_d, q2d, me.z_down)
    b2d.start()
    ax.wait_recv()
    whole[:, :hw] = (zsum[xh].astype(F32) + xin[...].astype(F32)).astype(BF)
    dlm.wait_recv()
    dl_out[...] = (dl_ref[:, c].astype(F32) + dl_in[...].astype(F32)).astype(BF)
    b2u.wait_recv()
    b2d.wait_recv()
    whole[:, hw:] = (xa[z, :, :].astype(F32) + q2u[...].astype(F32) + q2d[...].astype(F32)).astype(BF)
    hr, er = rows // 2, rows // 8
    xl, y = me.x_lo, me.y
    p1 = mail.copy(whole.at[at((1 - xl) * hr, hr)], v1, me.pair)
    p1.start()
    p1.wait_recv()
    vsum[...] = (whole[at(xl * hr, hr)].astype(F32) + v1[...].astype(F32)).astype(BF)
    ring = [mail.copy(vsum.at[at(((y + 1 + d) % 4) * er, er)], v2.at[d], to) for d, to in enumerate((me.up, me.over, me.down))]
    for copy in ring:
        copy.start()
    total = vsum[at(y * er, er)].astype(F32)
    for d, copy in enumerate(ring):
        copy.wait_recv()
        total = total + v2[d].astype(F32)
    last_own[...] = total.astype(BF)
    mine = at(xl * hr + y * er, er)
    lastg[mine] = last_own[...]
    back = [mail.copy(last_own, lastg.at[mine], to) for to in (me.up, me.over, me.down)]
    for copy in back:
        copy.start()
    for copy in back:
        copy.wait_recv()
    half = at(xl * hr, hr)
    pb = mail.copy(lastg.at[half], lastg.at[half], me.pair)
    pb.start()
    ma = mail.copy(lastg.at[half], mate_in.at[half], me.mate)
    ma.start()
    pb.wait_recv()
    other = at((1 - xl) * hr, hr)
    mb = mail.copy(lastg.at[other], mate_in.at[other], me.mate)
    mb.start()
    w3 = width // 3
    for k in range(3):
        dw_out[:, pl.ds(pl.multiple_of((2 * k + c) * w3, w3), w3)] = lastg[:, k * w3:(k + 1) * w3].astype(F32)
    ma.wait_recv()
    mb.wait_recv()
    for k in range(3):
        dw_out[:, pl.ds(pl.multiple_of((2 * k + 1 - c) * w3, w3), w3)] = mate_in[:, k * w3:(k + 1) * w3].astype(F32)
    mail.finish()


def pick(values, index):
    return lax.dynamic_index_in_dim(values, index, 0, keepdims=False)


def local(latents, w_qkv, cycle_links, cross_links, d_attended):
    _, _, samples, toks, model = latents.shape
    rows, wide = w_qkv.shape
    half = model // 2
    lat = latents[0, 0]
    view = lax.axis_index("view")
    a = view - view % 2
    ANY = pl.BlockSpec(memory_space=pl.ANY)
    VM = pl.BlockSpec(memory_space=pltpu.VMEM)
    n = 48
    lat_all, w_all, g_all = pl.pallas_call(
        gather_kernel,
        in_specs=[ANY] * 3,
        out_specs=[ANY] * 3,
        out_shape=[
            jax.ShapeDtypeStruct((samples, 8, toks, model), BF),
            jax.ShapeDtypeStruct((model, wide // 2), BF),
            jax.ShapeDtypeStruct((samples, 2 * toks, half), BF),
        ],
        scratch_shapes=[pltpu.SemaphoreType.DMA((7,)), pltpu.SemaphoreType.DMA((n,)), pltpu.SemaphoreType.DMA((n,))],
        compiler_params=pltpu.CompilerParams(collective_id=0, has_side_effects=True, vmem_limit_bytes=VMEM_LIMIT),
    )(lat, w_qkv, d_attended[0, 0])

    cycle, cross = cycle_links[0], cross_links[0]
    one = jnp.ones((), jnp.int32)

    def cyc(at_view):
        return pick(cycle, (at_view + 16) % 16)

    links = jnp.stack([
        jnp.stack([pick(cross, a % 8), cyc(a - 2), one, one, one, cyc(a)]),
        jnp.stack([cyc(a - 1), one, one, one, cyc(a + 1), pick(cross, (a + 1) % 8)]),
    ])
    bias = jnp.where(links > 0, 0.0, -1e30).astype(F32)

    kv = jnp.dot(lat_all.reshape(-1, model), w_all[:, half:], preferred_element_type=F32).astype(BF)
    kv = kv.reshape(samples, 8 * toks, 2 * half)
    lat_own = lat_all[:, 3:5].reshape(-1, model)
    q = jnp.dot(lat_own, w_all[:, :half], preferred_element_type=F32).astype(BF).reshape(samples, 2 * toks, half)
    att, dq, own, terms = attention(bias, q, g_all, kv)

    big = (2, samples, 2 * toks, half)
    gp, att_full = pl.pallas_call(
        terms_kernel,
        in_specs=[VM] * 4,
        out_specs=[VM, ANY],
        out_shape=[
            jax.ShapeDtypeStruct((samples, 2 * toks, 3 * half), BF),
            jax.ShapeDtypeStruct((samples, toks, model), BF),
        ],
        scratch_shapes=[
            pltpu.VMEM((3, *big), BF),
            pltpu.VMEM(big, BF),
            pltpu.SemaphoreType.DMA((2,)),
            pltpu.SemaphoreType.DMA((n,)),
            pltpu.SemaphoreType.DMA((n,)),
        ],
        compiler_params=pltpu.CompilerParams(collective_id=1, has_side_effects=True, vmem_limit_bytes=VMEM_LIMIT),
    )(terms, own, dq, att)

    gp = gp.reshape(-1, 3 * half)
    dl = dot(gp, w_all, NT).reshape(samples, 2, toks, model)
    dw = dot(lat_own, gp, TN).astype(BF).reshape(2, 4, rows, 3 * half)
    w = 3 * half
    h, qt = w // 2, w // 4
    dw_out, dl_out = pl.pallas_call(
        reduce_kernel,
        in_specs=[VM] * 2,
        out_specs=[VM] * 2,
        out_shape=[
            jax.ShapeDtypeStruct((rows, wide), F32),
            jax.ShapeDtypeStruct((samples, toks, model), BF),
        ],
        scratch_shapes=[
            pltpu.VMEM((samples, toks, model), F32),
            *[pltpu.VMEM((2, rows, qt), BF)] * 2,
            *[pltpu.VMEM((2, rows, h), BF)] * 4,
            pltpu.VMEM((2, rows, h), BF),
            pltpu.VMEM((rows, h), BF),
            *[pltpu.VMEM((4, rows, h), BF)] * 2,
            *[pltpu.VMEM((rows, qt), BF)] * 2,
            *[pltpu.VMEM((rows, h), BF)] * 4,
            pltpu.VMEM((rows, w), BF),
            *[pltpu.VMEM((rows // 2, w), BF)] * 2,
            pltpu.VMEM((3, rows // 8, w), BF),
            pltpu.VMEM((rows // 8, w), BF),
            *[pltpu.VMEM((rows, w), BF)] * 2,
            pltpu.SemaphoreType.DMA((n,)),
            pltpu.SemaphoreType.DMA((n,)),
        ],
        compiler_params=pltpu.CompilerParams(collective_id=2, has_side_effects=True, vmem_limit_bytes=VMEM_LIMIT),
    )(dw, dl)
    return att_full[None, None], dl_out[None, None], dw_out


def solution(mesh):
    wide = P("fsdp", "view", None, None, None)
    rows = P("fsdp", None)
    return jax.shard_map(
        local,
        mesh=mesh,
        in_specs=(wide, rows, rows, rows, wide),
        out_specs=(wide, wide, rows),
        check_vma=False,
    )
```

```python
import functools

import jax
import jax.numpy as jnp
from jax import lax
from jax.experimental import pallas as pl
from jax.experimental.pallas import tpu as pltpu
from jax.sharding import PartitionSpec as P

BF, F32 = jnp.bfloat16, jnp.float32
MESH = pl.DeviceIdType.MESH
TOK = 256
LOG2E = 1.4426950408889634
SCALE = 0.125
NT = (((1,), (1,)), ((), ()))
NN = (((1,), (0,)), ((), ()))
TN = (((0,), (0,)), ((), ()))
VMEM_LIMIT = 60 * 2**20


class Place:
    def __init__(self):
        v, f = lax.axis_index("view"), lax.axis_index("fsdp")
        self.view, self.fsdp = v, f
        self.ys, self.zs = 4, 4
        self.core = v % 2
        self.y = (v // 2) % 4
        self.x_lo = v // 8
        self.z = f % 4
        self.x_hi = f // 4
        column = self.x_lo * 8 + self.core

        def at(view, fsdp):
            return {"view": view, "fsdp": fsdp}

        self.up = at(column + 2 * ((self.y + 1) % 4), f)
        self.down = at(column + 2 * ((self.y + 3) % 4), f)
        self.over = at(column + 2 * ((self.y + 2) % 4), f)
        self.pair = at((v + 8) % 16, f)
        self.mate = at(v + 1 - 2 * self.core, f)
        self.f_up = self.x_hi * 4 + (self.z + 1) % 4
        self.f_down = self.x_hi * 4 + (self.z + 3) % 4
        self.f_far = self.x_hi * 4 + (self.z + 2) % 4
        self.f_outer = (f + 4) % 8
        self.z_up = at(v, self.f_up)
        self.z_down = at(v, self.f_down)
        self.outer = at((v + 8) % 16, self.f_outer)


def greet(devices):
    barrier = pltpu.get_barrier_semaphore()
    for device in devices:
        pl.semaphore_signal(barrier, inc=1, device_id=device, device_id_type=MESH)
    pl.semaphore_wait(barrier, len(devices))


class Mail:
    def __init__(self, send, recv):
        self.send, self.recv, self.made, self.sent = send, recv, 0, []

    def copy(self, src, dst, to):
        i = self.made
        self.made += 1
        made = self.again(i, src, dst, to)
        self.sent.append(made)
        return made

    def again(self, i, src, dst, to):
        return pltpu.make_async_remote_copy(
            src_ref=src, dst_ref=dst, send_sem=self.send.at[i], recv_sem=self.recv.at[i],
            device_id=to, device_id_type=MESH)

    def finish(self):
        for copy in self.sent:
            copy.wait_send()


def at(start, size):
    return pl.ds(pl.multiple_of(start, size), size)


def dot(a, b, dims=NN):
    return lax.dot_general(a, b, dims, preferred_element_type=F32)

def gather_kernel(lat_ref, w_ref, g_ref, lat_all, w_all, g_all, local, send, recv):
    me = Place()
    c = me.core
    rows = w_ref.shape[0]
    half = w_ref.shape[1] // 6
    pairs = half // 128
    samples, toks = lat_ref.shape[0], lat_ref.shape[1]
    chunks = [(s, pl.ds(t * (toks // 4), toks // 4)) for s in range(samples) for t in range(4)]
    own_block, other_block = 3 + c, 4 - c
    strips = []
    for p in range(pairs):
        for k in range(3):
            strips.append(pltpu.make_async_copy(
                w_ref.at[:, at((2 * k + c) * half + p * 128, 128)],
                w_all.at[at(me.fsdp * rows, rows), pl.ds((3 * p + k) * 128, 128)],
                local.at[3 * p + k]))
    kept = []
    base = 3 * pairs
    for s in range(samples):
        kept.append(pltpu.make_async_copy(lat_ref.at[s], lat_all.at[s, own_block], local.at[base + s]))
        kept.append(pltpu.make_async_copy(
            g_ref.at[s, :, at(c * half, half)], g_all.at[s, at(c * toks, toks), :], local.at[base + 2 + s]))
    for copy in strips + kept:
        copy.start()
    greet((me.up, me.down, me.pair, me.mate, me.z_up, me.z_down, me.outer))
    mail = Mail(send, recv)
    remote = mail.copy

    def block(b, chunk):
        s, t = chunk
        return lat_all.at[s, b, t]

    def shard(f, part=None):
        if part is None:
            return w_all.at[at(f * rows, rows)]
        return w_all.at[at(f * rows + part * (rows // 2), rows // 2)]

    n = range(len(chunks))
    mine = [lat_ref.at[s, t] for s, t in chunks]
    up = [remote(mine[i], block(1 + c, chunks[i]), me.up) for i in n]
    down = [remote(mine[i], block(5 + c, chunks[i]), me.down) for i in n]
    up_far = [mail.again(i, block(7 * c, chunks[i]), block(1 + c, chunks[i]), me.up) for i in n]
    down_far = [mail.again(len(chunks) + i, block(7 * c, chunks[i]), block(5 + c, chunks[i]), me.down) for i in n]
    to_pair = [remote(mine[i], block(7 * c, chunks[i]), me.pair) for i in n]
    to_mate = [remote(lat_ref.at[s], lat_all.at[s, own_block], me.mate) for s in range(samples)]
    relays = {b: [remote(lat_all.at[s, bb], lat_all.at[s, bb], me.mate) for s in range(samples)]
              for b, bb in (("pair", 7 * c), ("up", 1 + c), ("down", 5 + c))}
    g_mate = [remote(
        g_ref.at[s, :, at((1 - c) * half, half)], g_all.at[s, at(c * toks, toks), :], me.mate) for s in range(samples)]
    first, last = me.y == 0, me.y == me.ys - 1
    f0, f_up, f_down, f_out, far = me.fsdp, me.f_up, me.f_down, me.f_outer, me.f_far
    w_up = remote(shard(f0), shard(f0), me.z_up)
    w_down = remote(shard(f0), shard(f0), me.z_down)
    w_out = remote(shard(f0), shard(f0), me.outer)
    w_up2 = remote(shard(f_down, 0), shard(f_down, 0), me.z_up)
    w_down2 = remote(shard(f_up, 1), shard(f_up, 1), me.z_down)
    o_up = remote(shard(f_out), shard(f_out), me.z_up)
    o_down = remote(shard(f_out), shard(f_out), me.z_down)
    o_far = [remote(shard(far, part), shard(far, part), me.outer) for part in range(2)]

    to_pair[0].start()
    to_pair[1].start()
    for copy in strips:
        copy.wait()
    w_up.start()
    w_down.start()
    w_out.start()
    for i in n:
        pl.when(jnp.logical_not(last))(up[i].start)
        pl.when(jnp.logical_not(first))(down[i].start)
    for copy in to_mate + g_mate:
        copy.start()
    for i in n:
        to_pair[i].wait_send()
        if i + 2 < len(chunks):
            to_pair[i + 2].start()
        to_pair[i].wait_recv()
        pl.when(last)(up_far[i].start)
        pl.when(first)(down_far[i].start)
        if i == len(chunks) // 2 - 1:
            relays["pair"][0].start()
        if i == 2:
            w_up.wait_recv()
            w_up2.start()
            w_down.wait_recv()
            w_down2.start()
            w_out.wait_recv()
            o_up.start()
            o_down.start()
        if i == 5:
            w_up2.wait_recv()
            o_far[0].start()
            w_down2.wait_recv()
            o_far[1].start()
    relays["pair"][1].start()
    each = len(chunks) // samples
    for s in range(samples):
        for i in range(s * each, (s + 1) * each):
            up[i].wait_recv()
        relays["up"][s].start()
        for i in range(s * each, (s + 1) * each):
            down[i].wait_recv()
        relays["down"][s].start()
    for copy in (o_up, o_down, *o_far, *to_mate, *g_mate, *relays["pair"], *relays["up"], *relays["down"]):
        copy.wait_recv()
    for i, copy in enumerate(mail.sent):
        if not 2 * len(chunks) <= i < 3 * len(chunks):
            copy.wait_send()
    for copy in kept:
        copy.wait()


def when(condition):
    if isinstance(condition, bool):
        return (lambda f: f()) if condition else (lambda f: None)
    return pl.when(condition)


def both(*conditions):
    if any(isinstance(x, bool) and not x for x in conditions):
        return False
    conditions = [x for x in conditions if not isinstance(x, bool)]
    return functools.reduce(jnp.logical_and, conditions) if conditions else True


def view_pass(bias, q, g, k_rows, v_rows, kt, vt, gt, st, pb, gs):
    lane = lax.broadcasted_iota(jnp.int32, (1, 128), 1)
    outs, dqs, qms, gms = [], [], [], []
    for h in range(2):
        mine = (lane >= 64) if h else (lane < 64)
        qm = jnp.where(mine, q, jnp.zeros_like(q))
        gm = jnp.where(mine, g, jnp.zeros_like(g))
        qms.append(qm)
        gms.append(gm)
        tops = []
        for j in range(6):
            rows = pl.ds(j * TOK, TOK)
            s = dot(k_rows(j), qm, NT)
            st[h, rows, :] = s
            tops.append(jnp.max(s, axis=0, keepdims=True) * (SCALE * LOG2E) + bias[j])
        top = functools.reduce(jnp.maximum, tops)
        total = jnp.zeros((1, TOK), F32)
        for j in range(6):
            rows = pl.ds(j * TOK, TOK)
            e = jnp.exp2(st[h, rows, :] * (SCALE * LOG2E) - (top - bias[j]))
            st[h, rows, :] = e
            total = total + jnp.sum(e, axis=0, keepdims=True)
        inv = 1.0 / total
        for j in range(6):
            rows = pl.ds(j * TOK, TOK)
            p = st[h, rows, :] * inv
            st[h, rows, :] = p
            pb[rows, h * TOK:(h + 1) * TOK] = p.astype(BF)
        ot = dot(vt, pb[:, h * TOK:(h + 1) * TOK])[h * 64:(h + 1) * 64]
        outs.append(ot)
        delta = jnp.sum(gt[h * 64:(h + 1) * 64] * ot, axis=0, keepdims=True)
        for j in range(6):
            rows = pl.ds(j * TOK, TOK)
            d = dot(v_rows(j), gm, NT)
            gs[rows, h * TOK:(h + 1) * TOK] = (st[h, rows, :] * (d - delta)).astype(BF)
        dqs.append(dot(kt, gs[:, h * TOK:(h + 1) * TOK])[h * 64:(h + 1) * 64])
    return (
        jnp.concatenate(outs, axis=0),
        jnp.concatenate(dqs, axis=0) * SCALE,
        jnp.concatenate(qms, axis=0),
        jnp.concatenate(gms, axis=0),
    )


def project(lat, w, s, p, k_s, v_s, q_s):
    span = 2 * lat.shape[1] // 8
    first = 3 * span // 2
    w_kv = w[:, at(p * 384 + 128, 128)], w[:, at(p * 384 + 256, 128)]
    w_kv = jnp.concatenate(w_kv, axis=1)
    for r in range(lat.shape[1] // span):
        rows = pl.ds(r * span, span)
        kv = dot(lat[s, rows, :], w_kv).astype(BF)
        k_s[rows, :] = kv[:, :128]
        v_s[rows, :] = kv[:, 128:]
    q_s[...] = dot(lat[s, pl.ds(first, span), :], w[:, at(p * 384, 128)]).astype(BF)


def attend(bias, s, p, g_ref, k_s, v_s, q_s, st, pb, gs, att, dq, own, term):
    kt = k_s[...].T
    vt = v_s[...].T
    held = []
    for view in range(2):
        rows = pl.ds(view * TOK, TOK)
        q = q_s[rows, :]
        g = g_ref[s, rows, at(p * 128, 128)]
        gt = g.astype(F32).T
        span = slice(2 * view * TOK, (2 * view + 6) * TOK)

        def rows_of(ref, view=view):
            return lambda j: ref[pl.ds((2 * view + j) * TOK, TOK), :]

        ot, dqt, qm, gm = view_pass(
            bias[view], q, g, rows_of(k_s), rows_of(v_s), kt[:, span], vt[:, span], gt,
            st.at[view], pb.at[view], gs.at[view])
        att[rows, :] = ot.T.astype(BF)
        dq[rows, :] = dqt.T.astype(BF)
        held.append((qm, gm))
    for b in range(8):
        parts = []
        for view in range(2):
            j = b - 2 * view
            if 0 <= j < 6:
                qm, gm = held[view]
                rows = pl.ds(j * TOK, TOK)
                dk = dot(gs[view, rows, :], qm) * SCALE
                dv = dot(pb[view, rows, :], gm)
                parts.append((dk, dv))
        dk, dv = parts[0]
        if b in (3, 4):
            w = b - 3
            mine, other = parts[w], parts[1 - w]
            rows = pl.ds(w * TOK, TOK)
            own[0, rows, :] = mine[0] + other[0].astype(BF).astype(F32)
            own[1, rows, :] = mine[1] + other[1].astype(BF).astype(F32)
        else:
            if len(parts) == 2:
                dk = dk.astype(BF).astype(F32) + parts[1][0].astype(BF).astype(F32)
                dv = dv.astype(BF).astype(F32) + parts[1][1].astype(BF).astype(F32)
            n, w = {0: (2, 0), 1: (0, 0), 2: (0, 1), 5: (1, 0), 6: (1, 1), 7: (2, 1)}[b]
            rows = pl.ds(w * TOK, TOK)
            term[n, 0, rows, :] = dk.astype(BF)
            term[n, 1, rows, :] = dv.astype(BF)


STEPS = 8
KINDS = ("a1u", "a1d", "bx", "a2u", "a2d", "b1u", "b1d", "ax", "b2u", "b2d", "p1", "r0", "r1", "r2", "g0", "g1", "g2", "pb", "ma", "mb")


def main_kernel(cycle_ref, cross_ref, lat_hbm, w_hbm, g_hbm, att_full, dw_out, dl_out,
                lat, w, g, k_s, v_s, q_s, st, pb, gs, att, own, out, inbox, gp, dwb, dl_out_s, dl_in,
                z1u, z1d, z2u, z2d, su, sd, zs, xin, xain, xa, q1u, q1d, q2u, q2d, qsu, qsd,
                whole, v1, vsum, v2, fin, fing, mate_in,
                local, tsend, trecv, rsend, rrecv, dsend, drecv):
    me = Place()
    c, y, z, xh, xl = me.core, me.y, me.z, me.x_hi, me.x_lo
    zu, zd, zf = (z + 1) % 4, (z + 3) % 4, (z + 2) % 4
    width = 512
    loads = [pltpu.make_async_copy(w_hbm, w, local.at[0]), pltpu.make_async_copy(lat_hbm.at[0], lat.at[0], local.at[1]),
             pltpu.make_async_copy(g_hbm, g, local.at[2]), pltpu.make_async_copy(lat_hbm.at[1], lat.at[1], local.at[3])]
    for copy in loads:
        copy.start()
    greet((me.up, me.down, me.over, me.pair, me.mate, me.z_up, me.z_down, me.outer))

    def weight(link):
        return jnp.where(link > 0, 0.0, -1e30).astype(F32)

    a = me.view - c

    def cyc(v):
        return weight(cycle_ref[(v + 16) % 16])

    bias = [
        [weight(cross_ref[a % 8]), cyc(a - 2), 0.0, 0.0, 0.0, cyc(a)],
        [cyc(a - 1), 0.0, 0.0, 0.0, cyc(a + 1), weight(cross_ref[(a + 1) % 8])],
    ]
    first, last = y == 0, y == 3
    edge = jnp.logical_or(first, last)
    keep_down = jnp.where(first, 0.0, 1.0)
    keep_up = jnp.where(last, 0.0, 1.0)

    def mail(src, dst, send, recv, to):
        return pltpu.make_async_remote_copy(
            src_ref=src, dst_ref=dst, send_sem=send, recv_sem=recv, device_id=to, device_id_type=MESH)

    def up(t):
        return mail(out.at[t % 3, 1], inbox.at[t, 1], tsend.at[0, t % 3], trecv.at[0, t], me.up)

    def down(t):
        return mail(out.at[t % 3, 0], inbox.at[t, 0], tsend.at[1, t % 3], trecv.at[1, t], me.down)

    def across(t):
        return mail(out.at[t % 3, 2], inbox.at[t, 2], tsend.at[2, t % 3], trecv.at[2, t], me.pair)

    def columns(t):
        return at(c * width + (t // 2) * 128, 128)

    def att_mate(t):
        return mail(att.at[t % 3, at((1 - c) * TOK, TOK)], att_full.at[t % 2, :, columns(t)],
                    tsend.at[3, t % 3], trecv.at[3, t], me.mate)

    def att_own(t):
        return pltpu.make_async_copy(
            att.at[t % 3, at(c * TOK, TOK)], att_full.at[t % 2, :, columns(t)], tsend.at[4, t % 3])

    def red(kind, p, src, dst, to):
        i = KINDS.index(kind)
        return mail(src, dst, rsend.at[i, p], rrecv.at[i, p], to)

    lo, hi, top, low = pl.ds(0, 32), pl.ds(32, 32), pl.ds(0, 64), pl.ds(64, 64)
    hr, er = 64, 16
    mine = at(xl * hr + y * er, er)
    half = at(xl * hr, hr)
    other = at((1 - xl) * hr, hr)

    def a1u(p):
        return red("a1u", p, dwb.at[p, :, zf, lo], z1u.at[p], me.z_up)

    def a1d(p):
        return red("a1d", p, dwb.at[p, :, zf, hi], z1d.at[p], me.z_down)

    def bx(p):
        return red("bx", p, dwb.at[p, 1 - xh, :, low], xain.at[p], me.outer)

    def a2u(p):
        return red("a2u", p, su.at[p], z2u.at[p], me.z_up)

    def a2d(p):
        return red("a2d", p, sd.at[p], z2d.at[p], me.z_down)

    def b1u(p):
        return red("b1u", p, xa.at[p, zf, lo], q1u.at[p], me.z_up)

    def b1d(p):
        return red("b1d", p, xa.at[p, zf, hi], q1d.at[p], me.z_down)

    def ax(p):
        return red("ax", p, zs.at[p, 1 - xh], xin.at[p], me.outer)

    def b2u(p):
        return red("b2u", p, qsu.at[p], q2u.at[p], me.z_up)

    def b2d(p):
        return red("b2d", p, qsd.at[p], q2d.at[p], me.z_down)

    def p1(p):
        return red("p1", p, whole.at[p, other], v1.at[p], me.pair)

    def ring(p):
        return [red(f"r{d}", p, vsum.at[p, at(((y + 1 + d) % 4) * er, er)], v2.at[p, d], to)
                for d, to in enumerate((me.up, me.over, me.down))]

    def back(p):
        return [red(f"g{d}", p, fin.at[p], fing.at[p, mine], to) for d, to in enumerate((me.up, me.over, me.down))]

    def pair_back(p):
        return red("pb", p, fing.at[p, half], fing.at[p, half], me.pair)

    def mate_half(p):
        return red("ma", p, fing.at[p, half], mate_in.at[p, half], me.mate)

    def mate_other(p):
        return red("mb", p, fing.at[p, other], mate_in.at[p, other], me.mate)

    def f32(x):
        return x.astype(F32)

    def weight_grad(p):
        for f in range(8):
            total = None
            for s in range(2):
                part = dot(lat[s, pl.ds(3 * TOK, 2 * TOK), f * 128:(f + 1) * 128], gp[p, pl.ds(s * 512, 512), :], TN)
                total = part if total is None else total + part
            dwb[p, f // 4, f % 4] = total.astype(BF)

    def phase1(p):
        weight_grad(p)
        for make in (a1u, a1d, bx):
            make(p).start()

    def phase2(p):
        a1u(p).wait_recv()
        a1d(p).wait_recv()
        su[p, :, lo] = (f32(dwb[p, :, zu, lo]) + f32(z1u[p])).astype(BF)
        su[p, :, hi] = dwb[p, :, zu, hi]
        sd[p, :, lo] = dwb[p, :, zd, lo]
        sd[p, :, hi] = (f32(dwb[p, :, zd, hi]) + f32(z1d[p])).astype(BF)
        a2u(p).start()
        a2d(p).start()
        bx(p).wait_recv()
        xa[p] = (f32(dwb[p, xh, :, low]) + f32(xain[p])).astype(BF)
        b1u(p).start()
        b1d(p).start()

    def phase3(p):
        b1u(p).wait_recv()
        b1d(p).wait_recv()
        qsu[p, lo] = (f32(xa[p, zu, lo]) + f32(q1u[p])).astype(BF)
        qsu[p, hi] = xa[p, zu, hi]
        qsd[p, lo] = xa[p, zd, lo]
        qsd[p, hi] = (f32(xa[p, zd, hi]) + f32(q1d[p])).astype(BF)
        b2u(p).start()
        b2d(p).start()
        a2u(p).wait_recv()
        a2d(p).wait_recv()
        zs[p] = (f32(dwb[p, :, z, top]) + f32(z2u[p]) + f32(z2d[p])).astype(BF)
        ax(p).start()

    def phase4(p):
        b2u(p).wait_recv()
        b2d(p).wait_recv()
        whole[p, low] = (f32(xa[p, z]) + f32(q2u[p]) + f32(q2d[p])).astype(BF)
        ax(p).wait_recv()
        whole[p, top] = (f32(zs[p, xh]) + f32(xin[p])).astype(BF)
        p1(p).start()

    def phase5(p):
        p1(p).wait_recv()
        vsum[p] = (f32(whole[p, half]) + f32(v1[p])).astype(BF)
        for copy in ring(p):
            copy.start()

    def phase6(p):
        total = f32(vsum[p, at(y * er, er)])
        for d, copy in enumerate(ring(p)):
            copy.wait_recv()
            total = total + f32(v2[p, d])
        fin[p] = total.astype(BF)
        fing[p, mine] = total.astype(BF)
        for copy in back(p):
            copy.start()

    def phase7(p):
        for copy in back(p):
            copy.wait_recv()
        pair_back(p).start()
        mate_half(p).start()

    def phase8(p):
        pair_back(p).wait_recv()
        mate_other(p).start()

    phases = (phase1, phase2, phase3, phase4, phase5, phase6, phase7, phase8)

    def gather_grads(t):
        across(t).wait_recv()
        s, p = t % 2, t // 2
        for i in range(2):
            total = own[t % 3, i] + f32(inbox[t, 2, i]) + f32(inbox[t, 1, i]) * keep_down + f32(inbox[t, 0, i]) * keep_up
            gp[p, at(s * 512, 512), (1 + i) * 128:(2 + i) * 128] = total.astype(BF)

    def service(t):
        @when(both(t >= 1, t <= STEPS))
        def _():
            u = t - 1
            up(u).wait_recv()
            down(u).wait_recv()

            @pl.when(first)
            def _():
                out[u % 3, 2] = (f32(out[u % 3, 2]) + f32(inbox[u, 1])).astype(BF)

            @pl.when(last)
            def _():
                out[u % 3, 2] = (f32(out[u % 3, 2]) + f32(inbox[u, 0])).astype(BF)

            @pl.when(edge)
            def _():
                across(u).start()

        when(both(t >= 2, t <= STEPS + 1))(lambda: gather_grads(t - 2))
        for k, phase in enumerate(phases):
            if isinstance(t, int) or k < 5:
                due = t - 3 - k
                when(both(due >= 0, due <= 6, due % 2 == 0))(lambda: phase(due // 2))

    loads[0].wait()
    loads[1].wait()
    loads[2].wait()

    def step(t, carry):
        s, p = t % 2, t // 2

        @pl.when(t == 1)
        def _():
            loads[3].wait()

        @pl.when(t >= 3)
        def _():
            u = t - 3
            up(u).wait_send()
            down(u).wait_send()
            across(u).wait_send()
            att_mate(u).wait_send()
            att_own(u).wait()

        project(lat, w, s, p, k_s, v_s, q_s)
        attend(bias, s, p, g, k_s, v_s, q_s, st, pb, gs, att.at[t % 3], gp.at[p, at(s * 512, 512), pl.ds(0, 128)],
               own.at[t % 3], out.at[t % 3])
        up(t).start()
        down(t).start()

        @pl.when(jnp.logical_not(edge))
        def _():
            across(t).start()

        att_mate(t).start()
        att_own(t).start()
        service(t)
        return carry

    lax.fori_loop(0, STEPS, step, 0)

    def latent_grad():
        for n in range(4):
            w_n = w[pl.ds(n * 256, 256), :]
            for r in range(4):
                rows = pl.ds(r * 256, 256)
                total = None
                for p in range(4):
                    part = dot(gp[p, rows, :], w_n[:, p * 384:(p + 1) * 384], NT)
                    total = part if total is None else total + part
                st[n // 2, n % 2, rows, :] = total

    def dl_mate():
        return mail(dl_out_s, dl_in, dsend.at[0], drecv.at[0], me.mate)

    service(STEPS)
    service(STEPS + 1)
    latent_grad()
    for s in range(2):
        for n in range(4):
            dl_out_s[s, :, n * 256:(n + 1) * 256] = st[n // 2, n % 2, at(s * 512 + (1 - c) * TOK, TOK), :].astype(BF)
    dl_mate().start()
    service(STEPS + 2)
    service(STEPS + 3)
    dl_mate().wait_recv()
    for s in range(2):
        for n in range(4):
            cols = slice(n * 256, (n + 1) * 256)
            dl_out[s, :, cols] = (st[n // 2, n % 2, at(s * 512 + c * TOK, TOK), :] + f32(dl_in[s, :, cols])).astype(BF)
    for t in range(STEPS + 4, STEPS + 9):
        service(t)
    for p in range(4):
        for k in range(3):
            dw_out[:, at((2 * k + c) * width + p * 128, 128)] = f32(fing[p, :, k * 128:(k + 1) * 128])
        mate_half(p).wait_recv()
        mate_other(p).wait_recv()
        for k in range(3):
            dw_out[:, at((2 * k + 1 - c) * width + p * 128, 128)] = f32(mate_in[p, :, k * 128:(k + 1) * 128])
    for t in range(STEPS - 3, STEPS):
        for make in (up, down, across, att_mate):
            make(t).wait_send()
        att_own(t).wait()
    for t in range(STEPS):
        att_mate(t).wait_recv()
    dl_mate().wait_send()
    for p in range(4):
        for make in (a1u, a1d, bx, a2u, a2d, b1u, b1d, ax, b2u, b2d, p1, pair_back, mate_half, mate_other):
            make(p).wait_send()
        for copy in ring(p) + back(p):
            copy.wait_send()


def local(latents, w_qkv, cycle_links, cross_links, d_attended):
    _, _, samples, toks, model = latents.shape
    rows, wide = w_qkv.shape
    half = model // 2
    ANY = pl.BlockSpec(memory_space=pl.ANY)
    VM = pl.BlockSpec(memory_space=pltpu.VMEM)
    SM = pl.BlockSpec(memory_space=pltpu.SMEM)
    n = 48
    lat_all, w_all, g_all = pl.pallas_call(
        gather_kernel,
        in_specs=[ANY] * 3,
        out_specs=[ANY] * 3,
        out_shape=[
            jax.ShapeDtypeStruct((samples, 8, toks, model), BF),
            jax.ShapeDtypeStruct((model, wide // 2), BF),
            jax.ShapeDtypeStruct((samples, 2 * toks, half), BF),
        ],
        scratch_shapes=[pltpu.SemaphoreType.DMA((16,)), pltpu.SemaphoreType.DMA((n,)), pltpu.SemaphoreType.DMA((n,))],
        compiler_params=pltpu.CompilerParams(collective_id=0, has_side_effects=True, vmem_limit_bytes=VMEM_LIMIT),
    )(latents[0, 0], w_qkv, d_attended[0, 0])

    def vm(*shape, dtype=BF):
        return pltpu.VMEM(shape, dtype)

    W = 384
    att_full, dw_out, dl_out = pl.pallas_call(
        main_kernel,
        in_specs=[SM, SM, ANY, ANY, ANY],
        out_specs=[ANY, VM, VM],
        out_shape=[
            jax.ShapeDtypeStruct((samples, toks, model), BF),
            jax.ShapeDtypeStruct((rows, wide), F32),
            jax.ShapeDtypeStruct((samples, toks, model), BF),
        ],
        scratch_shapes=[
            vm(samples, 8 * toks, model), vm(model, wide // 2), vm(samples, 2 * toks, half),
            vm(8 * toks, 128), vm(8 * toks, 128), vm(2 * toks, 128),
            vm(2, 2, 6 * toks, toks, dtype=F32), vm(2, 6 * toks, 2 * toks), vm(2, 6 * toks, 2 * toks),
            vm(3, 2 * toks, 128), vm(3, 2, 2 * toks, 128, dtype=F32),
            vm(3, 3, 2, 2 * toks, 128), vm(STEPS, 3, 2, 2 * toks, 128),
            vm(4, samples * 2 * toks, W), vm(4, 2, 4, rows, W),
            vm(samples, toks, model), vm(samples, toks, model),
            vm(4, 2, 32, W), vm(4, 2, 32, W),
            vm(4, 2, 64, W), vm(4, 2, 64, W), vm(4, 2, 64, W), vm(4, 2, 64, W), vm(4, 2, 64, W),
            vm(4, 64, W), vm(4, 4, 64, W), vm(4, 4, 64, W),
            vm(4, 32, W), vm(4, 32, W),
            vm(4, 64, W), vm(4, 64, W), vm(4, 64, W), vm(4, 64, W),
            vm(4, rows, W), vm(4, 64, W), vm(4, 64, W), vm(4, 3, 16, W), vm(4, 16, W), vm(4, rows, W), vm(4, rows, W),
            pltpu.SemaphoreType.DMA((4,)),
            pltpu.SemaphoreType.DMA((5, 3)), pltpu.SemaphoreType.DMA((4, STEPS)),
            pltpu.SemaphoreType.DMA((len(KINDS), 4)), pltpu.SemaphoreType.DMA((len(KINDS), 4)),
            pltpu.SemaphoreType.DMA((1,)), pltpu.SemaphoreType.DMA((1,)),
        ],
        compiler_params=pltpu.CompilerParams(collective_id=1, has_side_effects=True, vmem_limit_bytes=63 * 2**20),
    )(cycle_links[0], cross_links[0], lat_all.reshape(samples, 8 * toks, model), w_all, g_all)
    return att_full[None, None], dl_out[None, None], dw_out


def solution(mesh):
    wide = P("fsdp", "view", None, None, None)
    rows = P("fsdp", None)
    return jax.shard_map(
        local,
        mesh=mesh,
        in_specs=(wide, rows, rows, rows, wide),
        out_specs=(wide, wide, rows),
        check_vma=False,
    )
```

```python
import functools

import jax
import jax.numpy as jnp
from jax import lax
from jax.experimental import pallas as pl
from jax.experimental.pallas import tpu as pltpu
from jax.sharding import PartitionSpec as P

BF, F32 = jnp.bfloat16, jnp.float32
MESH = pl.DeviceIdType.MESH
TOK = 256
LOG2E = 1.4426950408889634
SCALE = 0.125
NT = (((1,), (1,)), ((), ()))
NN = (((1,), (0,)), ((), ()))
TN = (((0,), (0,)), ((), ()))
VMEM_LIMIT = 60 * 2**20


class Place:
    def __init__(self):
        v, f = lax.axis_index("view"), lax.axis_index("fsdp")
        self.view, self.fsdp = v, f
        self.ys, self.zs = 4, 4
        self.core = v % 2
        self.y = (v // 2) % 4
        self.x_lo = v // 8
        self.z = f % 4
        self.x_hi = f // 4
        column = self.x_lo * 8 + self.core

        def at(view, fsdp):
            return {"view": view, "fsdp": fsdp}

        self.up = at(column + 2 * ((self.y + 1) % 4), f)
        self.down = at(column + 2 * ((self.y + 3) % 4), f)
        self.over = at(column + 2 * ((self.y + 2) % 4), f)
        self.pair = at((v + 8) % 16, f)
        self.mate = at(v + 1 - 2 * self.core, f)
        self.f_up = self.x_hi * 4 + (self.z + 1) % 4
        self.f_down = self.x_hi * 4 + (self.z + 3) % 4
        self.f_far = self.x_hi * 4 + (self.z + 2) % 4
        self.f_outer = (f + 4) % 8
        self.z_up = at(v, self.f_up)
        self.z_down = at(v, self.f_down)
        self.outer = at((v + 8) % 16, self.f_outer)


def greet(devices):
    barrier = pltpu.get_barrier_semaphore()
    for device in devices:
        pl.semaphore_signal(barrier, inc=1, device_id=device, device_id_type=MESH)
    pl.semaphore_wait(barrier, len(devices))


class Mail:
    def __init__(self, send, recv):
        self.send, self.recv, self.made, self.sent = send, recv, 0, []

    def copy(self, src, dst, to):
        i = self.made
        self.made += 1
        made = self.again(i, src, dst, to)
        self.sent.append(made)
        return made

    def again(self, i, src, dst, to):
        return pltpu.make_async_remote_copy(
            src_ref=src, dst_ref=dst, send_sem=self.send.at[i], recv_sem=self.recv.at[i],
            device_id=to, device_id_type=MESH)

    def finish(self):
        for copy in self.sent:
            copy.wait_send()


def at(start, size):
    return pl.ds(pl.multiple_of(start, size), size)


def dot(a, b, dims=NN):
    return lax.dot_general(a, b, dims, preferred_element_type=F32)


def when(condition):
    if isinstance(condition, bool):
        return (lambda f: f()) if condition else (lambda f: None)
    return pl.when(condition)


def both(*conditions):
    if any(isinstance(x, bool) and not x for x in conditions):
        return False
    conditions = [x for x in conditions if not isinstance(x, bool)]
    return functools.reduce(jnp.logical_and, conditions) if conditions else True


def view_pass(bias, q, g, k_rows, v_rows, kt, vt, gt, st, pb, gs):
    lane = lax.broadcasted_iota(jnp.int32, (1, 128), 1)
    outs, dqs, qms, gms = [], [], [], []
    for h in range(2):
        mine = (lane >= 64) if h else (lane < 64)
        qm = jnp.where(mine, q, jnp.zeros_like(q))
        gm = jnp.where(mine, g, jnp.zeros_like(g))
        qms.append(qm)
        gms.append(gm)
        tops = []
        for j in range(6):
            rows = pl.ds(j * TOK, TOK)
            s = dot(k_rows(j), qm, NT)
            st[h, rows, :] = s
            tops.append(jnp.max(s, axis=0, keepdims=True) * (SCALE * LOG2E) + bias[j])
        top = functools.reduce(jnp.maximum, tops)
        total = jnp.zeros((1, TOK), F32)
        for j in range(6):
            rows = pl.ds(j * TOK, TOK)
            e = jnp.exp2(st[h, rows, :] * (SCALE * LOG2E) - (top - bias[j]))
            st[h, rows, :] = e
            total = total + jnp.sum(e, axis=0, keepdims=True)
        inv = 1.0 / total
        for j in range(6):
            rows = pl.ds(j * TOK, TOK)
            p = st[h, rows, :] * inv
            st[h, rows, :] = p
            pb[rows, h * TOK:(h + 1) * TOK] = p.astype(BF)
        ot = dot(vt, pb[:, h * TOK:(h + 1) * TOK])[h * 64:(h + 1) * 64]
        outs.append(ot)
        delta = jnp.sum(gt[h * 64:(h + 1) * 64] * ot, axis=0, keepdims=True)
        for j in range(6):
            rows = pl.ds(j * TOK, TOK)
            d = dot(v_rows(j), gm, NT)
            gs[rows, h * TOK:(h + 1) * TOK] = (st[h, rows, :] * (d - delta)).astype(BF)
        dqs.append(dot(kt, gs[:, h * TOK:(h + 1) * TOK])[h * 64:(h + 1) * 64])
    return (
        jnp.concatenate(outs, axis=0),
        jnp.concatenate(dqs, axis=0) * SCALE,
        jnp.concatenate(qms, axis=0),
        jnp.concatenate(gms, axis=0),
    )


def project(lat, w, s, p, k_s, v_s, q_s):
    span = 2 * lat.shape[1] // 8
    first = 3 * span // 2
    w_kv = w[:, at(p * 384 + 128, 128)], w[:, at(p * 384 + 256, 128)]
    w_kv = jnp.concatenate(w_kv, axis=1)
    for r in range(lat.shape[1] // span):
        rows = pl.ds(r * span, span)
        kv = dot(lat[s, rows, :], w_kv).astype(BF)
        k_s[rows, :] = kv[:, :128]
        v_s[rows, :] = kv[:, 128:]
    q_s[...] = dot(lat[s, pl.ds(first, span), :], w[:, at(p * 384, 128)]).astype(BF)


def attend(bias, s, p, g_ref, k_s, v_s, q_s, st, pb, gs, att, dq, own, term):
    kt = k_s[...].T
    vt = v_s[...].T
    held = []
    for view in range(2):
        rows = pl.ds(view * TOK, TOK)
        q = q_s[rows, :]
        g = g_ref[s, rows, at(p * 128, 128)]
        gt = g.astype(F32).T
        span = slice(2 * view * TOK, (2 * view + 6) * TOK)

        def rows_of(ref, view=view):
            return lambda j: ref[pl.ds((2 * view + j) * TOK, TOK), :]

        ot, dqt, qm, gm = view_pass(
            bias[view], q, g, rows_of(k_s), rows_of(v_s), kt[:, span], vt[:, span], gt,
            st.at[view], pb.at[view], gs.at[view])
        att[rows, :] = ot.T.astype(BF)
        dq[rows, :] = dqt.T.astype(BF)
        held.append((qm, gm))
    for b in range(8):
        parts = []
        for view in range(2):
            j = b - 2 * view
            if 0 <= j < 6:
                qm, gm = held[view]
                rows = pl.ds(j * TOK, TOK)
                dk = dot(gs[view, rows, :], qm) * SCALE
                dv = dot(pb[view, rows, :], gm)
                parts.append((dk, dv))
        dk, dv = parts[0]
        if b in (3, 4):
            w = b - 3
            mine, other = parts[w], parts[1 - w]
            rows = pl.ds(w * TOK, TOK)
            own[0, rows, :] = mine[0] + other[0].astype(BF).astype(F32)
            own[1, rows, :] = mine[1] + other[1].astype(BF).astype(F32)
        else:
            if len(parts) == 2:
                dk = dk.astype(BF).astype(F32) + parts[1][0].astype(BF).astype(F32)
                dv = dv.astype(BF).astype(F32) + parts[1][1].astype(BF).astype(F32)
            n, w = {0: (2, 0), 1: (0, 0), 2: (0, 1), 5: (1, 0), 6: (1, 1), 7: (2, 1)}[b]
            rows = pl.ds(w * TOK, TOK)
            term[n, 0, rows, :] = dk.astype(BF)
            term[n, 1, rows, :] = dv.astype(BF)


STEPS = 8
KINDS = ("a1u", "a1d", "bx", "a2u", "a2d", "b1u", "b1d", "ax", "b2u", "b2d", "p1", "r0", "r1", "r2", "g0", "g1", "g2", "pb", "ma", "mb")


def sample_and_pair(t):
    if isinstance(t, int):
        return (t // 2, t % 2) if t < 4 else (t % 2, t // 2)
    early = t < 4
    return jnp.where(early, t // 2, t % 2), jnp.where(early, t % 2, t // 2)


def main_kernel(cycle_ref, cross_ref, lat_hbm, w_hbm, g_hbm, att_full, dw_out, dl_out,
                lat, w, g, k_s, v_s, q_s, st, pb, gs, att, own, out, inbox, gp, dwb, dl_out_s, dl_in,
                z1u, z1d, z2u, z2d, su, sd, zs, xin, xain, xa, q1u, q1d, q2u, q2d, qsu, qsd,
                whole, v1, vsum, v2, fin, fing, mate_in,
                local, tsend, trecv, rsend, rrecv, dsend, drecv, gsend, grecv):
    me = Place()
    c, y, z, xh, xl = me.core, me.y, me.z, me.x_hi, me.x_lo
    zu, zd, zf = (z + 1) % 4, (z + 3) % 4, (z + 2) % 4
    width = 512
    strips, kept = [], []
    for p in range(4):
        for k in range(3):
            strips.append(pltpu.make_async_copy(
                w_hbm.at[:, at((2 * k + c) * width + p * 128, 128)],
                w.at[at(me.fsdp * 128, 128), pl.ds((3 * p + k) * 128, 128)], local.at[3 * p + k]))
    for s in range(2):
        kept.append(pltpu.make_async_copy(lat_hbm.at[s], lat.at[s, at((3 + c) * TOK, TOK)], local.at[12 + s]))
        kept.append(pltpu.make_async_copy(g_hbm.at[s, :, at(c * width, width)], g.at[s, at(c * TOK, TOK)], local.at[14 + s]))
    for copy in strips + kept:
        copy.start()
    greet((me.up, me.down, me.over, me.pair, me.mate, me.z_up, me.z_down, me.outer))

    def weight(link):
        return jnp.where(link > 0, 0.0, -1e30).astype(F32)

    a = me.view - c

    def cyc(v):
        return weight(cycle_ref[(v + 16) % 16])

    bias = [
        [weight(cross_ref[a % 8]), cyc(a - 2), 0.0, 0.0, 0.0, cyc(a)],
        [cyc(a - 1), 0.0, 0.0, 0.0, cyc(a + 1), weight(cross_ref[(a + 1) % 8])],
    ]
    first, last = y == 0, y == 3
    edge = jnp.logical_or(first, last)
    keep_down = jnp.where(first, 0.0, 1.0)
    keep_up = jnp.where(last, 0.0, 1.0)

    def mail(src, dst, send, recv, to):
        return pltpu.make_async_remote_copy(
            src_ref=src, dst_ref=dst, send_sem=send, recv_sem=recv, device_id=to, device_id_type=MESH)

    def up(t):
        return mail(out.at[t % 3, 1], inbox.at[t, 1], tsend.at[0, t % 3], trecv.at[0, t], me.up)

    def down(t):
        return mail(out.at[t % 3, 0], inbox.at[t, 0], tsend.at[1, t % 3], trecv.at[1, t], me.down)

    def across(t):
        return mail(out.at[t % 3, 2], inbox.at[t, 2], tsend.at[2, t % 3], trecv.at[2, t], me.pair)

    def columns(t):
        return at(c * width + sample_and_pair(t)[1] * 128, 128)

    def att_mate(t):
        return mail(att.at[t % 3, at((1 - c) * TOK, TOK)], att_full.at[sample_and_pair(t)[0], :, columns(t)],
                    tsend.at[3, t % 3], trecv.at[3, t], me.mate)

    def att_own(t):
        return pltpu.make_async_copy(
            att.at[t % 3, at(c * TOK, TOK)], att_full.at[sample_and_pair(t)[0], :, columns(t)], tsend.at[4, t % 3])

    def red(kind, p, src, dst, to):
        i = KINDS.index(kind)
        return mail(src, dst, rsend.at[i, p], rrecv.at[i, p], to)

    lo, hi, top, low = pl.ds(0, 32), pl.ds(32, 32), pl.ds(0, 64), pl.ds(64, 64)
    hr, er = 64, 16
    mine = at(xl * hr + y * er, er)
    half = at(xl * hr, hr)
    other = at((1 - xl) * hr, hr)

    def a1u(p):
        return red("a1u", p, dwb.at[p, :, zf, lo], z1u.at[p], me.z_up)

    def a1d(p):
        return red("a1d", p, dwb.at[p, :, zf, hi], z1d.at[p], me.z_down)

    def bx(p):
        return red("bx", p, dwb.at[p, 1 - xh, :, low], xain.at[p], me.outer)

    def a2u(p):
        return red("a2u", p, su.at[p], z2u.at[p], me.z_up)

    def a2d(p):
        return red("a2d", p, sd.at[p], z2d.at[p], me.z_down)

    def b1u(p):
        return red("b1u", p, xa.at[p, zf, lo], q1u.at[p], me.z_up)

    def b1d(p):
        return red("b1d", p, xa.at[p, zf, hi], q1d.at[p], me.z_down)

    def ax(p):
        return red("ax", p, zs.at[p, 1 - xh], xin.at[p], me.outer)

    def b2u(p):
        return red("b2u", p, qsu.at[p], q2u.at[p], me.z_up)

    def b2d(p):
        return red("b2d", p, qsd.at[p], q2d.at[p], me.z_down)

    def p1(p):
        return red("p1", p, whole.at[p, other], v1.at[p], me.pair)

    def ring(p):
        return [red(f"r{d}", p, vsum.at[p, at(((y + 1 + d) % 4) * er, er)], v2.at[p, d], to)
                for d, to in enumerate((me.up, me.over, me.down))]

    def back(p):
        return [red(f"g{d}", p, fin.at[p], fing.at[p, mine], to) for d, to in enumerate((me.up, me.over, me.down))]

    def pair_back(p):
        return red("pb", p, fing.at[p, half], fing.at[p, half], me.pair)

    def mate_half(p):
        return red("ma", p, fing.at[p, half], mate_in.at[p, half], me.mate)

    def mate_other(p):
        return red("mb", p, fing.at[p, other], mate_in.at[p, other], me.mate)

    def f32(x):
        return x.astype(F32)

    def weight_grad(p):
        for f in range(8):
            total = None
            for s in range(2):
                part = dot(lat[s, pl.ds(3 * TOK, 2 * TOK), f * 128:(f + 1) * 128], gp[p, pl.ds(s * 512, 512), :], TN)
                total = part if total is None else total + part
            dwb[p, f // 4, f % 4] = total.astype(BF)

    def phase1(p):
        weight_grad(p)
        for make in (a1u, a1d, bx):
            make(p).start()

    def phase2(p):
        a1u(p).wait_recv()
        a1d(p).wait_recv()
        su[p, :, lo] = (f32(dwb[p, :, zu, lo]) + f32(z1u[p])).astype(BF)
        su[p, :, hi] = dwb[p, :, zu, hi]
        sd[p, :, lo] = dwb[p, :, zd, lo]
        sd[p, :, hi] = (f32(dwb[p, :, zd, hi]) + f32(z1d[p])).astype(BF)
        a2u(p).start()
        a2d(p).start()
        bx(p).wait_recv()
        xa[p] = (f32(dwb[p, xh, :, low]) + f32(xain[p])).astype(BF)
        b1u(p).start()
        b1d(p).start()

    def phase3(p):
        b1u(p).wait_recv()
        b1d(p).wait_recv()
        qsu[p, lo] = (f32(xa[p, zu, lo]) + f32(q1u[p])).astype(BF)
        qsu[p, hi] = xa[p, zu, hi]
        qsd[p, lo] = xa[p, zd, lo]
        qsd[p, hi] = (f32(xa[p, zd, hi]) + f32(q1d[p])).astype(BF)
        b2u(p).start()
        b2d(p).start()
        a2u(p).wait_recv()
        a2d(p).wait_recv()
        zs[p] = (f32(dwb[p, :, z, top]) + f32(z2u[p]) + f32(z2d[p])).astype(BF)
        ax(p).start()

    def phase4(p):
        b2u(p).wait_recv()
        b2d(p).wait_recv()
        whole[p, low] = (f32(xa[p, z]) + f32(q2u[p]) + f32(q2d[p])).astype(BF)
        ax(p).wait_recv()
        whole[p, top] = (f32(zs[p, xh]) + f32(xin[p])).astype(BF)
        p1(p).start()

    def phase5(p):
        p1(p).wait_recv()
        vsum[p] = (f32(whole[p, half]) + f32(v1[p])).astype(BF)
        for copy in ring(p):
            copy.start()

    def phase6(p):
        total = f32(vsum[p, at(y * er, er)])
        for d, copy in enumerate(ring(p)):
            copy.wait_recv()
            total = total + f32(v2[p, d])
        fin[p] = total.astype(BF)
        fing[p, mine] = total.astype(BF)
        for copy in back(p):
            copy.start()

    def phase7(p):
        for copy in back(p):
            copy.wait_recv()
        pair_back(p).start()
        mate_half(p).start()

    def phase8(p):
        pair_back(p).wait_recv()
        mate_other(p).start()

    phases = (phase1, phase2, phase3, phase4, phase5, phase6, phase7, phase8)
    begins = (4, 5, 7, 9)

    def gather_grads(t):
        across(t).wait_recv()
        s, p = sample_and_pair(t)
        for i in range(2):
            total = own[t % 3, i] + f32(inbox[t, 2, i]) + f32(inbox[t, 1, i]) * keep_down + f32(inbox[t, 0, i]) * keep_up
            gp[p, at(s * 512, 512), (1 + i) * 128:(2 + i) * 128] = total.astype(BF)

    def service(t):
        @when(both(t >= 1, t <= STEPS))
        def _():
            u = t - 1
            up(u).wait_recv()
            down(u).wait_recv()

            @pl.when(first)
            def _():
                out[u % 3, 2] = (f32(out[u % 3, 2]) + f32(inbox[u, 1])).astype(BF)

            @pl.when(last)
            def _():
                out[u % 3, 2] = (f32(out[u % 3, 2]) + f32(inbox[u, 0])).astype(BF)

            @pl.when(edge)
            def _():
                across(u).start()

        when(both(t >= 2, t <= STEPS + 1))(lambda: gather_grads(t - 2))
        for p, begin in reversed(list(enumerate(begins))):
            for k, phase in enumerate(phases):
                if isinstance(t, int) or begin + k < STEPS:
                    when(t == begin + k)(functools.partial(phase, p))

    sent = []
    slots = iter(range(64))

    def post(src, dst, to, own=None):
        i = next(slots)
        made = mail(src, dst, gsend.at[i], grecv.at[i], to)
        sent.append(made)
        return made if own is None else (made, mail(own, dst, gsend.at[i], grecv.at[i], to))

    def rows_at(s, b, start=0, size=TOK):
        return lat.at[s, at(b * TOK + start, size)]

    def w_at(f, group, start=0, size=128):
        return w.at[at(f * 128 + start, size), pl.ds(group * 768, 768)]

    cuts = {0: [(i * 64, 64) for i in range(4)], 1: [(0, TOK)]}
    to_pair, to_up, to_down, to_mate, relays, g_mate = {}, {}, {}, {}, {}, []
    for s in range(2):
        to_pair[s] = [post(lat_hbm.at[s, pl.ds(*cut)], rows_at(s, 7 * c, *cut), me.pair) for cut in cuts[s]]
        to_up[s] = [post(rows_at(s, 7 * c, *cut), rows_at(s, 1 + c, *cut), me.up, lat_hbm.at[s, pl.ds(*cut)]) for cut in cuts[s]]
        to_down[s] = [post(rows_at(s, 7 * c, *cut), rows_at(s, 5 + c, *cut), me.down, lat_hbm.at[s, pl.ds(*cut)]) for cut in cuts[s]]
        to_mate[s] = post(lat_hbm.at[s], rows_at(s, 3 + c), me.mate)
        relays[s] = [post(rows_at(s, b), rows_at(s, b), me.mate) for b in (7 * c, 1 + c, 5 + c)]
        g_mate.append(post(g_hbm.at[s, :, at((1 - c) * width, width)], g.at[s, at(c * TOK, TOK)], me.mate))
    f0, f_up, f_down, f_out, far = me.fsdp, me.f_up, me.f_down, me.f_outer, me.f_far
    w_mail = [dict(
        up=post(w_at(f0, grp), w_at(f0, grp), me.z_up),
        down=post(w_at(f0, grp), w_at(f0, grp), me.z_down),
        out=post(w_at(f0, grp), w_at(f0, grp), me.outer),
        up2=post(w_at(f_down, grp, 0, 64), w_at(f_down, grp, 0, 64), me.z_up),
        down2=post(w_at(f_up, grp, 64, 64), w_at(f_up, grp, 64, 64), me.z_down),
        out_up=post(w_at(f_out, grp), w_at(f_out, grp), me.z_up),
        out_down=post(w_at(f_out, grp), w_at(f_out, grp), me.z_down),
        far0=post(w_at(far, grp, 0, 64), w_at(far, grp, 0, 64), me.outer),
        far1=post(w_at(far, grp, 64, 64), w_at(far, grp, 64, 64), me.outer),
    ) for grp in range(2)]

    def w_first(grp):
        for copy in strips[6 * grp:6 * grp + 6]:
            copy.wait()
        for name in ("up", "down", "out"):
            w_mail[grp][name].start()

    def w_second(grp):
        m = w_mail[grp]
        m["up"].wait_recv()
        m["up2"].start()
        m["down"].wait_recv()
        m["down2"].start()
        m["out"].wait_recv()
        m["out_up"].start()
        m["out_down"].start()

    def w_third(grp):
        m = w_mail[grp]
        m["up2"].wait_recv()
        m["far0"].start()
        m["down2"].wait_recv()
        m["far1"].start()

    def w_last(grp):
        for name in ("out_up", "out_down", "far0", "far1"):
            w_mail[grp][name].wait_recv()

    def lat_first(s):
        for i in range(len(cuts[s])):
            pl.when(jnp.logical_not(last))(to_up[s][i][1].start)
            pl.when(jnp.logical_not(first))(to_down[s][i][1].start)
        to_mate[s].start()
        g_mate[s].start()

    def lat_wrap(s, i):
        to_pair[s][i].wait_recv()
        pl.when(last)(to_up[s][i][0].start)
        pl.when(first)(to_down[s][i][0].start)

    def lat_relay(s):
        for i in range(len(cuts[s])):
            to_up[s][i][0].wait_recv()
        relays[s][1].start()
        for i in range(len(cuts[s])):
            to_down[s][i][0].wait_recv()
        relays[s][2].start()

    def lat_last(s):
        for copy in (to_mate[s], g_mate[s], *relays[s]):
            copy.wait_recv()

    chunks = len(cuts[0])
    to_pair[0][0].start()
    to_pair[0][1].start()
    w_first(0)
    lat_first(0)
    for i in range(chunks):
        to_pair[0][i].wait_send()
        if i + 2 < chunks:
            to_pair[0][i + 2].start()
        lat_wrap(0, i)
        if i == 1:
            w_second(0)
        if i == 2:
            w_third(0)
    relays[0][0].start()
    to_pair[1][0].start()
    lat_relay(0)
    w_first(1)
    lat_first(1)
    w_last(0)
    for copy in kept:
        copy.wait()
    lat_last(0)

    def step(t, carry):
        s, p = sample_and_pair(t)

        @pl.when(t == 2)
        def _():
            lat_last(1)

        @pl.when(t == 4)
        def _():
            w_last(1)

        @pl.when(t >= 3)
        def _():
            u = t - 3
            up(u).wait_send()
            down(u).wait_send()
            across(u).wait_send()
            att_mate(u).wait_send()
            att_own(u).wait()

        project(lat, w, s, p, k_s, v_s, q_s)
        attend(bias, s, p, g, k_s, v_s, q_s, st, pb, gs, att.at[t % 3], gp.at[p, at(s * 512, 512), pl.ds(0, 128)],
               own.at[t % 3], out.at[t % 3])
        up(t).start()
        down(t).start()

        @pl.when(jnp.logical_not(edge))
        def _():
            across(t).start()

        att_mate(t).start()
        att_own(t).start()

        @pl.when(t == 0)
        def _():
            lat_wrap(1, 0)
            relays[1][0].start()
            w_second(1)

        @pl.when(t == 1)
        def _():
            lat_relay(1)
            w_third(1)

        service(t)
        return carry

    lax.fori_loop(0, STEPS, step, 0)

    def latent_grad():
        for n in range(4):
            w_n = w[pl.ds(n * 256, 256), :]
            for r in range(4):
                rows = pl.ds(r * 256, 256)
                total = None
                for p in range(4):
                    part = dot(gp[p, rows, :], w_n[:, p * 384:(p + 1) * 384], NT)
                    total = part if total is None else total + part
                st[n // 2, n % 2, rows, :] = total

    def dl_mate():
        return mail(dl_out_s, dl_in, dsend.at[0], drecv.at[0], me.mate)

    service(STEPS)
    service(STEPS + 1)
    latent_grad()
    for s in range(2):
        for n in range(4):
            dl_out_s[s, :, n * 256:(n + 1) * 256] = st[n // 2, n % 2, at(s * 512 + (1 - c) * TOK, TOK), :].astype(BF)
    dl_mate().start()
    service(STEPS + 2)
    service(STEPS + 3)
    dl_mate().wait_recv()
    for s in range(2):
        for n in range(4):
            cols = slice(n * 256, (n + 1) * 256)
            dl_out[s, :, cols] = (st[n // 2, n % 2, at(s * 512 + c * TOK, TOK), :] + f32(dl_in[s, :, cols])).astype(BF)
    for t in range(STEPS + 4, STEPS + 9):
        service(t)
    for p in range(4):
        for k in range(3):
            dw_out[:, at((2 * k + c) * width + p * 128, 128)] = f32(fing[p, :, k * 128:(k + 1) * 128])
        mate_half(p).wait_recv()
        mate_other(p).wait_recv()
        for k in range(3):
            dw_out[:, at((2 * k + 1 - c) * width + p * 128, 128)] = f32(mate_in[p, :, k * 128:(k + 1) * 128])
    for t in range(STEPS - 3, STEPS):
        for make in (up, down, across, att_mate):
            make(t).wait_send()
        att_own(t).wait()
    for t in range(STEPS):
        att_mate(t).wait_recv()
    dl_mate().wait_send()
    for p in range(4):
        for make in (a1u, a1d, bx, a2u, a2d, b1u, b1d, ax, b2u, b2d, p1, pair_back, mate_half, mate_other):
            make(p).wait_send()
        for copy in ring(p) + back(p):
            copy.wait_send()
    for i, copy in enumerate(sent):
        if i >= chunks:
            copy.wait_send()


def local(latents, w_qkv, cycle_links, cross_links, d_attended):
    _, _, samples, toks, model = latents.shape
    rows, wide = w_qkv.shape
    half = model // 2
    ANY = pl.BlockSpec(memory_space=pl.ANY)
    VM = pl.BlockSpec(memory_space=pltpu.VMEM)
    SM = pl.BlockSpec(memory_space=pltpu.SMEM)
    def vm(*shape, dtype=BF):
        return pltpu.VMEM(shape, dtype)

    W = 384
    att_full, dw_out, dl_out = pl.pallas_call(
        main_kernel,
        in_specs=[SM, SM, ANY, ANY, ANY],
        out_specs=[ANY, VM, VM],
        out_shape=[
            jax.ShapeDtypeStruct((samples, toks, model), BF),
            jax.ShapeDtypeStruct((rows, wide), F32),
            jax.ShapeDtypeStruct((samples, toks, model), BF),
        ],
        scratch_shapes=[
            vm(samples, 8 * toks, model), vm(model, wide // 2), vm(samples, 2 * toks, half),
            vm(8 * toks, 128), vm(8 * toks, 128), vm(2 * toks, 128),
            vm(2, 2, 6 * toks, toks, dtype=F32), vm(2, 6 * toks, 2 * toks), vm(2, 6 * toks, 2 * toks),
            vm(3, 2 * toks, 128), vm(3, 2, 2 * toks, 128, dtype=F32),
            vm(3, 3, 2, 2 * toks, 128), vm(STEPS, 3, 2, 2 * toks, 128),
            vm(4, samples * 2 * toks, W), vm(4, 2, 4, rows, W),
            vm(samples, toks, model), vm(samples, toks, model),
            vm(4, 2, 32, W), vm(4, 2, 32, W),
            vm(4, 2, 64, W), vm(4, 2, 64, W), vm(4, 2, 64, W), vm(4, 2, 64, W), vm(4, 2, 64, W),
            vm(4, 64, W), vm(4, 4, 64, W), vm(4, 4, 64, W),
            vm(4, 32, W), vm(4, 32, W),
            vm(4, 64, W), vm(4, 64, W), vm(4, 64, W), vm(4, 64, W),
            vm(4, rows, W), vm(4, 64, W), vm(4, 64, W), vm(4, 3, 16, W), vm(4, 16, W), vm(4, rows, W), vm(4, rows, W),
            pltpu.SemaphoreType.DMA((16,)),
            pltpu.SemaphoreType.DMA((5, 3)), pltpu.SemaphoreType.DMA((4, STEPS)),
            pltpu.SemaphoreType.DMA((len(KINDS), 4)), pltpu.SemaphoreType.DMA((len(KINDS), 4)),
            pltpu.SemaphoreType.DMA((1,)), pltpu.SemaphoreType.DMA((1,)),
            pltpu.SemaphoreType.DMA((64,)), pltpu.SemaphoreType.DMA((64,)),
        ],
        compiler_params=pltpu.CompilerParams(collective_id=0, has_side_effects=True, vmem_limit_bytes=63 * 2**20),
    )(cycle_links[0], cross_links[0], latents[0, 0], w_qkv, d_attended[0, 0])
    return att_full[None, None], dl_out[None, None], dw_out


def solution(mesh):
    wide = P("fsdp", "view", None, None, None)
    rows = P("fsdp", None)
    return jax.shard_map(
        local,
        mesh=mesh,
        in_specs=(wide, rows, rows, rows, wide),
        out_specs=(wide, wide, rows),
        check_vma=False,
    )
```

```python
import functools

import jax
import jax.numpy as jnp
from jax import lax
from jax.experimental import pallas as pl
from jax.experimental.pallas import tpu as pltpu
from jax.sharding import PartitionSpec as P

BF, F32 = jnp.bfloat16, jnp.float32
MESH = pl.DeviceIdType.MESH
TOK = 256
LOG2E = 1.4426950408889634
SCALE = 0.125
NT = (((1,), (1,)), ((), ()))
NN = (((1,), (0,)), ((), ()))
TN = (((0,), (0,)), ((), ()))
VMEM_LIMIT = 60 * 2**20


class Place:
    def __init__(self):
        v, f = lax.axis_index("view"), lax.axis_index("fsdp")
        self.view, self.fsdp = v, f
        self.ys, self.zs = 4, 4
        self.core = v % 2
        self.y = (v // 2) % 4
        self.x_lo = v // 8
        self.z = f % 4
        self.x_hi = f // 4
        column = self.x_lo * 8 + self.core

        def at(view, fsdp):
            return {"view": view, "fsdp": fsdp}

        self.up = at(column + 2 * ((self.y + 1) % 4), f)
        self.down = at(column + 2 * ((self.y + 3) % 4), f)
        self.over = at(column + 2 * ((self.y + 2) % 4), f)
        self.pair = at((v + 8) % 16, f)
        self.mate = at(v + 1 - 2 * self.core, f)
        self.f_up = self.x_hi * 4 + (self.z + 1) % 4
        self.f_down = self.x_hi * 4 + (self.z + 3) % 4
        self.f_far = self.x_hi * 4 + (self.z + 2) % 4
        self.f_outer = (f + 4) % 8
        self.z_up = at(v, self.f_up)
        self.z_down = at(v, self.f_down)
        self.outer = at((v + 8) % 16, self.f_outer)


def greet(devices):
    barrier = pltpu.get_barrier_semaphore()
    for device in devices:
        pl.semaphore_signal(barrier, inc=1, device_id=device, device_id_type=MESH)
    pl.semaphore_wait(barrier, len(devices))


class Mail:
    def __init__(self, send, recv):
        self.send, self.recv, self.made, self.sent = send, recv, 0, []

    def copy(self, src, dst, to):
        i = self.made
        self.made += 1
        made = self.again(i, src, dst, to)
        self.sent.append(made)
        return made

    def again(self, i, src, dst, to):
        return pltpu.make_async_remote_copy(
            src_ref=src, dst_ref=dst, send_sem=self.send.at[i], recv_sem=self.recv.at[i],
            device_id=to, device_id_type=MESH)

    def finish(self):
        for copy in self.sent:
            copy.wait_send()


def at(start, size):
    return pl.ds(pl.multiple_of(start, size), size)


def dot(a, b, dims=NN):
    return lax.dot_general(a, b, dims, preferred_element_type=F32)


def when(condition):
    if isinstance(condition, bool):
        return (lambda f: f()) if condition else (lambda f: None)
    return pl.when(condition)


def both(*conditions):
    if any(isinstance(x, bool) and not x for x in conditions):
        return False
    conditions = [x for x in conditions if not isinstance(x, bool)]
    return functools.reduce(jnp.logical_and, conditions) if conditions else True


def head_pass(view, h, bias, qt, gt, k_rows, v_rows, kt, vt, st, pb, gs, att_t, dq_t, own, term):
    head = slice(h * 64, (h + 1) * 64)
    row = lax.broadcasted_iota(jnp.int32, (128, 1), 0)
    mine = (row >= 64) if h else (row < 64)
    qm = jnp.where(mine, qt, jnp.zeros_like(qt)).astype(BF)
    gm = jnp.where(mine, gt, jnp.zeros_like(gt)).astype(BF)
    cols = slice(h * TOK, (h + 1) * TOK)
    blocks = [pl.ds(j * TOK, TOK) for j in range(6)]
    tops = []
    for j in range(0, 6, SPAN):
        s = dot(k_rows(j, SPAN), qm)
        for i in range(SPAN):
            part = s[i * TOK:(i + 1) * TOK]
            st[h, blocks[j + i], :] = part
            tops.append(jnp.max(part, axis=0, keepdims=True) * (SCALE * LOG2E) + bias[j + i])
            yield
    top = functools.reduce(jnp.maximum, tops)
    total = jnp.zeros((1, TOK), F32)
    for j, rows in enumerate(blocks):
        e = jnp.exp2(st[h, rows, :] * (SCALE * LOG2E) - (top - bias[j]))
        st[h, rows, :] = e
        total = total + jnp.sum(e, axis=0, keepdims=True)
        yield
    inv = 1.0 / total
    for rows in blocks:
        pb[rows, cols] = (st[h, rows, :] * inv).astype(BF)
        yield
    ot = dot(vt()[head], pb[:, cols])
    att_t[h] = ot
    delta = jnp.sum(gt[head] * ot, axis=0, keepdims=True)
    yield
    for j in range(0, 6, SPAN):
        d = dot(v_rows(j, SPAN), gm)
        for i in range(SPAN):
            part = d[i * TOK:(i + 1) * TOK]
            gs[blocks[j + i], cols] = (st[h, blocks[j + i], :] * inv * (part - delta)).astype(BF)
            yield
    dq_t[h] = dot(kt()[head], gs[:, cols]) * SCALE
    yield
    q_head, g_head = qt[head].astype(BF), gt[head].astype(BF)
    for j, rows in enumerate(blocks):
        b = j + 2 * view
        grads = dot(q_head, gs[rows, cols], NT) * SCALE, dot(g_head, pb[rows, cols], NT)
        for i, grad in enumerate(grads):
            if b in (3, 4):
                w = pl.ds((b - 3) * TOK, TOK)
                grad = grad if b - 3 == view else grad.astype(BF).astype(F32)
                own[i, head, w] = grad if view == 0 else own[i, head, w] + grad
            else:
                n, w = {0: (2, 0), 1: (0, 0), 2: (0, 1), 5: (1, 0), 6: (1, 1), 7: (2, 1)}[b]
                w = pl.ds(w * TOK, TOK)
                grad = grad.astype(BF)
                if b in (2, 5) and view == 1:
                    grad = (term[n, i, head, w].astype(F32) + grad.astype(F32)).astype(BF)
                term[n, i, head, w] = grad
        yield


def project(lat, w, s, p, k_s, v_s, q_s):
    span = PROJECT_ROWS
    first, count = 3 * lat.shape[1] // 8, lat.shape[1] // 4
    w_kv = w[:, pl.ds(pl.multiple_of(p * 384 + 128, 128), 256)]
    for r in range(lat.shape[1] // span):
        rows = pl.ds(r * span, span)
        kv = dot(lat[s, rows, :], w_kv).astype(BF)
        k_s[rows, :] = kv[:, :128]
        v_s[rows, :] = kv[:, 128:]
        yield
    q_s[...] = dot(lat[s, pl.ds(first, count), :], w[:, at(p * 384, 128)]).astype(BF)
    yield


def weave(threads):
    threads = list(threads)
    tick = 0
    while threads:
        for thread in list(threads):
            start, every, work = thread
            if tick >= start and (tick - start) % every == 0:
                try:
                    next(work)
                except StopIteration:
                    threads.remove(thread)
        tick += 1


def attend(bias, s, p, g_ref, k_s, v_s, q_s, st, pb, gs, att, dq, own, term, beside=()):
    kt = k_s[...].T
    vt = v_s[...].T
    threads = list(beside)
    results = []
    for view in range(2):
        rows = pl.ds(view * TOK, TOK)
        q = q_s[rows, :]
        g = g_ref[s, rows, at(p * 128, 128)]
        gt = g.astype(F32).T
        span = slice(2 * view * TOK, (2 * view + 6) * TOK)

        qt = q.astype(F32).T

        def rows_of(ref, view=view):
            return lambda j, n: ref[pl.ds((2 * view + j) * TOK, n * TOK), :]

        att_t, dq_t = {}, {}
        results.append((rows, att_t, dq_t))
        for h in range(2):
            threads.append((OFFSET * (2 * view + h), 1, head_pass(
                view, h, bias[view], qt, gt, rows_of(k_s), rows_of(v_s), lambda span=span: kt[:, span],
                lambda span=span: vt[:, span], st.at[view], pb.at[view], gs.at[view], att_t, dq_t, own, term)))
    weave(threads)
    for rows, att_t, dq_t in results:
        att[rows, :] = jnp.concatenate([att_t[0], att_t[1]], axis=0).T.astype(BF)
        dq[rows, :] = jnp.concatenate([dq_t[0], dq_t[1]], axis=0).T.astype(BF)


OFFSET, SPAN, PROJECT_ROWS = 9, 1, 512
STEPS = 8
KINDS = ("a1u", "a1d", "bx", "a2u", "a2d", "b1u", "b1d", "ax", "b2u", "b2d", "p1", "r0", "r1", "r2", "g0", "g1", "g2", "pb", "ma", "mb")


def sample_and_pair(t):
    if isinstance(t, int):
        return (t // 2, t % 2) if t < 4 else (t % 2, t // 2)
    early = t < 4
    return jnp.where(early, t // 2, t % 2), jnp.where(early, t % 2, t // 2)


def main_kernel(cycle_ref, cross_ref, lat_hbm, w_hbm, g_hbm, att_full, dw_out, dl_out,
                lat, w, g, k_s, v_s, q_s, st, pb, gs, att, own, out, inbox, gp, dwb, dl_out_s, dl_in,
                z1u, z1d, z2u, z2d, su, sd, zs, xin, xain, xa, q1u, q1d, q2u, q2d, qsu, qsd,
                whole, v1, vsum, v2, fin, fing, mate_in,
                local, tsend, trecv, rsend, rrecv, dsend, drecv, gsend, grecv):
    me = Place()
    c, y, z, xh, xl = me.core, me.y, me.z, me.x_hi, me.x_lo
    zu, zd, zf = (z + 1) % 4, (z + 3) % 4, (z + 2) % 4
    width = 512
    strips, kept = [], []
    for p in range(4):
        for k in range(3):
            strips.append(pltpu.make_async_copy(
                w_hbm.at[:, at((2 * k + c) * width + p * 128, 128)],
                w.at[at(me.fsdp * 128, 128), pl.ds((3 * p + k) * 128, 128)], local.at[3 * p + k]))
    for s in range(2):
        kept.append(pltpu.make_async_copy(lat_hbm.at[s], lat.at[s, at((3 + c) * TOK, TOK)], local.at[12 + s]))
        kept.append(pltpu.make_async_copy(g_hbm.at[s, :, at(c * width, width)], g.at[s, at(c * TOK, TOK)], local.at[14 + s]))
    for copy in strips + kept:
        copy.start()
    greet((me.up, me.down, me.over, me.pair, me.mate, me.z_up, me.z_down, me.outer))

    def weight(link):
        return jnp.where(link > 0, 0.0, -1e30).astype(F32)

    a = me.view - c

    def cyc(v):
        return weight(cycle_ref[(v + 16) % 16])

    bias = [
        [weight(cross_ref[a % 8]), cyc(a - 2), 0.0, 0.0, 0.0, cyc(a)],
        [cyc(a - 1), 0.0, 0.0, 0.0, cyc(a + 1), weight(cross_ref[(a + 1) % 8])],
    ]
    first, last = y == 0, y == 3
    edge = jnp.logical_or(first, last)
    keep_down = jnp.where(first, 0.0, 1.0)
    keep_up = jnp.where(last, 0.0, 1.0)

    def mail(src, dst, send, recv, to):
        return pltpu.make_async_remote_copy(
            src_ref=src, dst_ref=dst, send_sem=send, recv_sem=recv, device_id=to, device_id_type=MESH)

    def up(t):
        return mail(out.at[t % 3, 1], inbox.at[t, 1], tsend.at[0, t % 3], trecv.at[0, t], me.up)

    def down(t):
        return mail(out.at[t % 3, 0], inbox.at[t, 0], tsend.at[1, t % 3], trecv.at[1, t], me.down)

    def across(t):
        return mail(out.at[t % 3, 2], inbox.at[t, 2], tsend.at[2, t % 3], trecv.at[2, t], me.pair)

    def columns(t):
        return at(c * width + sample_and_pair(t)[1] * 128, 128)

    def att_mate(t):
        return mail(att.at[t % 3, at((1 - c) * TOK, TOK)], att_full.at[sample_and_pair(t)[0], :, columns(t)],
                    tsend.at[3, t % 3], trecv.at[3, t], me.mate)

    def att_own(t):
        return pltpu.make_async_copy(
            att.at[t % 3, at(c * TOK, TOK)], att_full.at[sample_and_pair(t)[0], :, columns(t)], tsend.at[4, t % 3])

    def red(kind, p, src, dst, to):
        i = KINDS.index(kind)
        return mail(src, dst, rsend.at[i, p], rrecv.at[i, p], to)

    lo, hi, top, low = pl.ds(0, 32), pl.ds(32, 32), pl.ds(0, 64), pl.ds(64, 64)
    hr, er = 64, 16
    mine = at(xl * hr + y * er, er)
    half = at(xl * hr, hr)
    other = at((1 - xl) * hr, hr)

    def a1u(p):
        return red("a1u", p, dwb.at[p, :, zf, lo], z1u.at[p], me.z_up)

    def a1d(p):
        return red("a1d", p, dwb.at[p, :, zf, hi], z1d.at[p], me.z_down)

    def bx(p):
        return red("bx", p, dwb.at[p, 1 - xh, :, low], xain.at[p], me.outer)

    def a2u(p):
        return red("a2u", p, su.at[p], z2u.at[p], me.z_up)

    def a2d(p):
        return red("a2d", p, sd.at[p], z2d.at[p], me.z_down)

    def b1u(p):
        return red("b1u", p, xa.at[p, zf, lo], q1u.at[p], me.z_up)

    def b1d(p):
        return red("b1d", p, xa.at[p, zf, hi], q1d.at[p], me.z_down)

    def ax(p):
        return red("ax", p, zs.at[p, 1 - xh], xin.at[p], me.outer)

    def b2u(p):
        return red("b2u", p, qsu.at[p], q2u.at[p], me.z_up)

    def b2d(p):
        return red("b2d", p, qsd.at[p], q2d.at[p], me.z_down)

    def p1(p):
        return red("p1", p, whole.at[p, other], v1.at[p], me.pair)

    def ring(p):
        return [red(f"r{d}", p, vsum.at[p, at(((y + 1 + d) % 4) * er, er)], v2.at[p, d], to)
                for d, to in enumerate((me.up, me.over, me.down))]

    def back(p):
        return [red(f"g{d}", p, fin.at[p], fing.at[p, mine], to) for d, to in enumerate((me.up, me.over, me.down))]

    def pair_back(p):
        return red("pb", p, fing.at[p, half], fing.at[p, half], me.pair)

    def mate_half(p):
        return red("ma", p, fing.at[p, half], mate_in.at[p, half], me.mate)

    def mate_other(p):
        return red("mb", p, fing.at[p, other], mate_in.at[p, other], me.mate)

    def f32(x):
        return x.astype(F32)

    def weight_grad(p):
        for f in range(8):
            total = None
            for s in range(2):
                part = dot(lat[s, pl.ds(3 * TOK, 2 * TOK), f * 128:(f + 1) * 128], gp[p, pl.ds(s * 512, 512), :], TN)
                total = part if total is None else total + part
            dwb[p, f // 4, f % 4] = total.astype(BF)

    def phase1(p):
        weight_grad(p)
        for make in (a1u, a1d, bx):
            make(p).start()

    def phase2(p):
        a1u(p).wait_recv()
        a1d(p).wait_recv()
        su[p, :, lo] = (f32(dwb[p, :, zu, lo]) + f32(z1u[p])).astype(BF)
        su[p, :, hi] = dwb[p, :, zu, hi]
        sd[p, :, lo] = dwb[p, :, zd, lo]
        sd[p, :, hi] = (f32(dwb[p, :, zd, hi]) + f32(z1d[p])).astype(BF)
        a2u(p).start()
        a2d(p).start()
        bx(p).wait_recv()
        xa[p] = (f32(dwb[p, xh, :, low]) + f32(xain[p])).astype(BF)
        b1u(p).start()
        b1d(p).start()

    def phase3(p):
        b1u(p).wait_recv()
        b1d(p).wait_recv()
        qsu[p, lo] = (f32(xa[p, zu, lo]) + f32(q1u[p])).astype(BF)
        qsu[p, hi] = xa[p, zu, hi]
        qsd[p, lo] = xa[p, zd, lo]
        qsd[p, hi] = (f32(xa[p, zd, hi]) + f32(q1d[p])).astype(BF)
        b2u(p).start()
        b2d(p).start()
        a2u(p).wait_recv()
        a2d(p).wait_recv()
        zs[p] = (f32(dwb[p, :, z, top]) + f32(z2u[p]) + f32(z2d[p])).astype(BF)
        ax(p).start()

    def phase4(p):
        b2u(p).wait_recv()
        b2d(p).wait_recv()
        whole[p, low] = (f32(xa[p, z]) + f32(q2u[p]) + f32(q2d[p])).astype(BF)
        ax(p).wait_recv()
        whole[p, top] = (f32(zs[p, xh]) + f32(xin[p])).astype(BF)
        p1(p).start()

    def phase5(p):
        p1(p).wait_recv()
        vsum[p] = (f32(whole[p, half]) + f32(v1[p])).astype(BF)
        for copy in ring(p):
            copy.start()

    def phase6(p):
        total = f32(vsum[p, at(y * er, er)])
        for d, copy in enumerate(ring(p)):
            copy.wait_recv()
            total = total + f32(v2[p, d])
        fin[p] = total.astype(BF)
        fing[p, mine] = total.astype(BF)
        for copy in back(p):
            copy.start()

    def phase7(p):
        for copy in back(p):
            copy.wait_recv()
        pair_back(p).start()
        mate_half(p).start()

    def phase8(p):
        pair_back(p).wait_recv()
        mate_other(p).start()

    phases = (phase1, phase2, phase3, phase4, phase5, phase6, phase7, phase8)
    begins = (4, 5, 7, 9)

    def gather_grads(t):
        across(t).wait_recv()
        s, p = sample_and_pair(t)
        for i in range(2):
            total = own[t % 3, i] + f32(inbox[t, 2, i]) + f32(inbox[t, 1, i]) * keep_down + f32(inbox[t, 0, i]) * keep_up
            gp[p, at(s * 512, 512), (1 + i) * 128:(2 + i) * 128] = total.T.astype(BF)

    def service(t):
        @when(both(t >= 1, t <= STEPS))
        def _():
            u = t - 1
            up(u).wait_recv()
            down(u).wait_recv()

            @pl.when(first)
            def _():
                out[u % 3, 2] = (f32(out[u % 3, 2]) + f32(inbox[u, 1])).astype(BF)

            @pl.when(last)
            def _():
                out[u % 3, 2] = (f32(out[u % 3, 2]) + f32(inbox[u, 0])).astype(BF)

            @pl.when(edge)
            def _():
                across(u).start()

        when(both(t >= 2, t <= STEPS + 1))(lambda: gather_grads(t - 2))
        for p, begin in reversed(list(enumerate(begins))):
            for k, phase in enumerate(phases):
                if isinstance(t, int) or begin + k < STEPS:
                    when(t == begin + k)(functools.partial(phase, p))

    sent = []
    slots = iter(range(64))

    def post(src, dst, to, own=None):
        i = next(slots)
        made = mail(src, dst, gsend.at[i], grecv.at[i], to)
        sent.append(made)
        return made if own is None else (made, mail(own, dst, gsend.at[i], grecv.at[i], to))

    def rows_at(s, b, start=0, size=TOK):
        return lat.at[s, at(b * TOK + start, size)]

    def w_at(f, group, start=0, size=128):
        return w.at[at(f * 128 + start, size), pl.ds(group * 768, 768)]

    cuts = {0: [(i * 64, 64) for i in range(4)], 1: [(0, TOK)]}
    to_pair, to_up, to_down, to_mate, relays, g_mate = {}, {}, {}, {}, {}, []
    for s in range(2):
        to_pair[s] = [post(lat_hbm.at[s, pl.ds(*cut)], rows_at(s, 7 * c, *cut), me.pair) for cut in cuts[s]]
        to_up[s] = [post(rows_at(s, 7 * c, *cut), rows_at(s, 1 + c, *cut), me.up, lat_hbm.at[s, pl.ds(*cut)]) for cut in cuts[s]]
        to_down[s] = [post(rows_at(s, 7 * c, *cut), rows_at(s, 5 + c, *cut), me.down, lat_hbm.at[s, pl.ds(*cut)]) for cut in cuts[s]]
        to_mate[s] = post(lat_hbm.at[s], rows_at(s, 3 + c), me.mate)
        relays[s] = [post(rows_at(s, b), rows_at(s, b), me.mate) for b in (7 * c, 1 + c, 5 + c)]
        g_mate.append(post(g_hbm.at[s, :, at((1 - c) * width, width)], g.at[s, at(c * TOK, TOK)], me.mate))
    f0, f_up, f_down, f_out, far = me.fsdp, me.f_up, me.f_down, me.f_outer, me.f_far
    w_mail = [dict(
        up=post(w_at(f0, grp), w_at(f0, grp), me.z_up),
        down=post(w_at(f0, grp), w_at(f0, grp), me.z_down),
        out=post(w_at(f0, grp), w_at(f0, grp), me.outer),
        up2=post(w_at(f_down, grp, 0, 64), w_at(f_down, grp, 0, 64), me.z_up),
        down2=post(w_at(f_up, grp, 64, 64), w_at(f_up, grp, 64, 64), me.z_down),
        out_up=post(w_at(f_out, grp), w_at(f_out, grp), me.z_up),
        out_down=post(w_at(f_out, grp), w_at(f_out, grp), me.z_down),
        far0=post(w_at(far, grp, 0, 64), w_at(far, grp, 0, 64), me.outer),
        far1=post(w_at(far, grp, 64, 64), w_at(far, grp, 64, 64), me.outer),
    ) for grp in range(2)]

    def w_first(grp):
        for copy in strips[6 * grp:6 * grp + 6]:
            copy.wait()
        for name in ("up", "down", "out"):
            w_mail[grp][name].start()

    def w_second(grp):
        m = w_mail[grp]
        m["up"].wait_recv()
        m["up2"].start()
        m["down"].wait_recv()
        m["down2"].start()
        m["out"].wait_recv()
        m["out_up"].start()
        m["out_down"].start()

    def w_third(grp):
        m = w_mail[grp]
        m["up2"].wait_recv()
        m["far0"].start()
        m["down2"].wait_recv()
        m["far1"].start()

    def w_last(grp):
        for name in ("out_up", "out_down", "far0", "far1"):
            w_mail[grp][name].wait_recv()

    def lat_first(s):
        for i in range(len(cuts[s])):
            pl.when(jnp.logical_not(last))(to_up[s][i][1].start)
            pl.when(jnp.logical_not(first))(to_down[s][i][1].start)
        to_mate[s].start()
        g_mate[s].start()

    def lat_wrap(s, i):
        to_pair[s][i].wait_recv()
        pl.when(last)(to_up[s][i][0].start)
        pl.when(first)(to_down[s][i][0].start)

    def lat_relay(s):
        for i in range(len(cuts[s])):
            to_up[s][i][0].wait_recv()
        relays[s][1].start()
        for i in range(len(cuts[s])):
            to_down[s][i][0].wait_recv()
        relays[s][2].start()

    def lat_last(s):
        for copy in (to_mate[s], g_mate[s], *relays[s]):
            copy.wait_recv()

    chunks = len(cuts[0])
    to_pair[0][0].start()
    to_pair[0][1].start()
    w_first(0)
    lat_first(0)
    for i in range(chunks):
        to_pair[0][i].wait_send()
        if i + 2 < chunks:
            to_pair[0][i + 2].start()
        lat_wrap(0, i)
        if i == 1:
            w_second(0)
        if i == 2:
            w_third(0)
    relays[0][0].start()
    to_pair[1][0].start()
    lat_relay(0)
    w_first(1)
    lat_first(1)
    w_last(0)
    for copy in kept:
        copy.wait()
    lat_last(0)

    def projected(t, slot):
        for _ in project(lat, w, *sample_and_pair(t), k_s.at[slot], v_s.at[slot], q_s.at[slot]):
            pass

    projected(0, 0)

    def step(t, carry):
        s, p = sample_and_pair(t)

        @pl.when(t == 2)
        def _():
            lat_last(1)
            projected(2, 0)

        @pl.when(t == 3)
        def _():
            w_last(1)

        @pl.when(t >= 3)
        def _():
            u = t - 3
            up(u).wait_send()
            down(u).wait_send()
            across(u).wait_send()
            att_mate(u).wait_send()
            att_own(u).wait()

        now, later = t % 2, (t + 1) % 2
        s_next, p_next = sample_and_pair(jnp.where(t == 1, 1, jnp.minimum(t + 1, STEPS - 1)))
        beside = project(lat, w, s_next, p_next, k_s.at[later], v_s.at[later], q_s.at[later])
        attend(bias, s, p, g, k_s.at[now], v_s.at[now], q_s.at[now], st, pb, gs, att.at[t % 3],
               gp.at[p, at(s * 512, 512), pl.ds(0, 128)], own.at[t % 3], out.at[t % 3], [(4, 2, beside)])
        up(t).start()
        down(t).start()

        @pl.when(jnp.logical_not(edge))
        def _():
            across(t).start()

        att_mate(t).start()
        att_own(t).start()

        @pl.when(t == 0)
        def _():
            lat_wrap(1, 0)
            relays[1][0].start()
            w_second(1)

        @pl.when(t == 1)
        def _():
            lat_relay(1)
            w_third(1)

        service(t)
        return carry

    lax.fori_loop(0, STEPS, step, 0)

    def latent_grad():
        for n in range(4):
            w_n = w[pl.ds(n * 256, 256), :]
            for r in range(4):
                rows = pl.ds(r * 256, 256)
                total = None
                for p in range(4):
                    part = dot(gp[p, rows, :], w_n[:, p * 384:(p + 1) * 384], NT)
                    total = part if total is None else total + part
                st[n // 2, n % 2, rows, :] = total

    def dl_mate():
        return mail(dl_out_s, dl_in, dsend.at[0], drecv.at[0], me.mate)

    service(STEPS)
    service(STEPS + 1)
    latent_grad()
    for s in range(2):
        for n in range(4):
            dl_out_s[s, :, n * 256:(n + 1) * 256] = st[n // 2, n % 2, at(s * 512 + (1 - c) * TOK, TOK), :].astype(BF)
    dl_mate().start()
    service(STEPS + 2)
    service(STEPS + 3)
    dl_mate().wait_recv()
    for s in range(2):
        for n in range(4):
            cols = slice(n * 256, (n + 1) * 256)
            dl_out[s, :, cols] = (st[n // 2, n % 2, at(s * 512 + c * TOK, TOK), :] + f32(dl_in[s, :, cols])).astype(BF)
    for t in range(STEPS + 4, STEPS + 9):
        service(t)
    for p in range(4):
        for k in range(3):
            dw_out[:, at((2 * k + c) * width + p * 128, 128)] = f32(fing[p, :, k * 128:(k + 1) * 128])
        mate_half(p).wait_recv()
        mate_other(p).wait_recv()
        for k in range(3):
            dw_out[:, at((2 * k + 1 - c) * width + p * 128, 128)] = f32(mate_in[p, :, k * 128:(k + 1) * 128])
    for t in range(STEPS - 3, STEPS):
        for make in (up, down, across, att_mate):
            make(t).wait_send()
        att_own(t).wait()
    for t in range(STEPS):
        att_mate(t).wait_recv()
    dl_mate().wait_send()
    for p in range(4):
        for make in (a1u, a1d, bx, a2u, a2d, b1u, b1d, ax, b2u, b2d, p1, pair_back, mate_half, mate_other):
            make(p).wait_send()
        for copy in ring(p) + back(p):
            copy.wait_send()
    for i, copy in enumerate(sent):
        if i >= chunks:
            copy.wait_send()


def local(latents, w_qkv, cycle_links, cross_links, d_attended):
    _, _, samples, toks, model = latents.shape
    rows, wide = w_qkv.shape
    half = model // 2
    ANY = pl.BlockSpec(memory_space=pl.ANY)
    VM = pl.BlockSpec(memory_space=pltpu.VMEM)
    SM = pl.BlockSpec(memory_space=pltpu.SMEM)
    def vm(*shape, dtype=BF):
        return pltpu.VMEM(shape, dtype)

    W = 384
    att_full, dw_out, dl_out = pl.pallas_call(
        main_kernel,
        in_specs=[SM, SM, ANY, ANY, ANY],
        out_specs=[ANY, VM, VM],
        out_shape=[
            jax.ShapeDtypeStruct((samples, toks, model), BF),
            jax.ShapeDtypeStruct((rows, wide), F32),
            jax.ShapeDtypeStruct((samples, toks, model), BF),
        ],
        scratch_shapes=[
            vm(samples, 8 * toks, model), vm(model, wide // 2), vm(samples, 2 * toks, half),
            vm(2, 8 * toks, 128), vm(2, 8 * toks, 128), vm(2, 2 * toks, 128),
            vm(2, 2, 6 * toks, toks, dtype=F32), vm(2, 6 * toks, 2 * toks), vm(2, 6 * toks, 2 * toks),
            vm(3, 2 * toks, 128), vm(3, 2, 128, 2 * toks, dtype=F32),
            vm(3, 3, 2, 128, 2 * toks), vm(STEPS, 3, 2, 128, 2 * toks),
            vm(4, samples * 2 * toks, W), vm(4, 2, 4, rows, W),
            vm(samples, toks, model), vm(samples, toks, model),
            vm(4, 2, 32, W), vm(4, 2, 32, W),
            vm(4, 2, 64, W), vm(4, 2, 64, W), vm(4, 2, 64, W), vm(4, 2, 64, W), vm(4, 2, 64, W),
            vm(4, 64, W), vm(4, 4, 64, W), vm(4, 4, 64, W),
            vm(4, 32, W), vm(4, 32, W),
            vm(4, 64, W), vm(4, 64, W), vm(4, 64, W), vm(4, 64, W),
            vm(4, rows, W), vm(4, 64, W), vm(4, 64, W), vm(4, 3, 16, W), vm(4, 16, W), vm(4, rows, W), vm(4, rows, W),
            pltpu.SemaphoreType.DMA((16,)),
            pltpu.SemaphoreType.DMA((5, 3)), pltpu.SemaphoreType.DMA((4, STEPS)),
            pltpu.SemaphoreType.DMA((len(KINDS), 4)), pltpu.SemaphoreType.DMA((len(KINDS), 4)),
            pltpu.SemaphoreType.DMA((1,)), pltpu.SemaphoreType.DMA((1,)),
            pltpu.SemaphoreType.DMA((64,)), pltpu.SemaphoreType.DMA((64,)),
        ],
        compiler_params=pltpu.CompilerParams(collective_id=0, has_side_effects=True, vmem_limit_bytes=63 * 2**20),
    )(cycle_links[0], cross_links[0], latents[0, 0], w_qkv, d_attended[0, 0])
    return att_full[None, None], dl_out[None, None], dw_out


def solution(mesh):
    wide = P("fsdp", "view", None, None, None)
    rows = P("fsdp", None)
    return jax.shard_map(
        local,
        mesh=mesh,
        in_specs=(wide, rows, rows, rows, wide),
        out_specs=(wide, wide, rows),
        check_vma=False,
    )
```

```python
import functools

import jax
import jax.numpy as jnp
from jax import lax
from jax.experimental import pallas as pl
from jax.experimental.pallas import tpu as pltpu
from jax.sharding import PartitionSpec as P

BF, F32 = jnp.bfloat16, jnp.float32
MESH = pl.DeviceIdType.MESH
TOK = 256
LOG2E = 1.4426950408889634
SCALE = 0.125
NT = (((1,), (1,)), ((), ()))
NN = (((1,), (0,)), ((), ()))
TN = (((0,), (0,)), ((), ()))
VMEM_LIMIT = 60 * 2**20


class Place:
    def __init__(self):
        v, f = lax.axis_index("view"), lax.axis_index("fsdp")
        self.view, self.fsdp = v, f
        self.ys, self.zs = 4, 4
        self.core = v % 2
        self.y = (v // 2) % 4
        self.x_lo = v // 8
        self.z = f % 4
        self.x_hi = f // 4
        column = self.x_lo * 8 + self.core

        def at(view, fsdp):
            return {"view": view, "fsdp": fsdp}

        self.up = at(column + 2 * ((self.y + 1) % 4), f)
        self.down = at(column + 2 * ((self.y + 3) % 4), f)
        self.over = at(column + 2 * ((self.y + 2) % 4), f)
        self.pair = at((v + 8) % 16, f)
        self.mate = at(v + 1 - 2 * self.core, f)
        self.f_up = self.x_hi * 4 + (self.z + 1) % 4
        self.f_down = self.x_hi * 4 + (self.z + 3) % 4
        self.f_far = self.x_hi * 4 + (self.z + 2) % 4
        self.f_outer = (f + 4) % 8
        self.z_up = at(v, self.f_up)
        self.z_down = at(v, self.f_down)
        self.outer = at((v + 8) % 16, self.f_outer)


def greet(devices):
    barrier = pltpu.get_barrier_semaphore()
    for device in devices:
        pl.semaphore_signal(barrier, inc=1, device_id=device, device_id_type=MESH)
    pl.semaphore_wait(barrier, len(devices))


class Mail:
    def __init__(self, send, recv):
        self.send, self.recv, self.made, self.sent = send, recv, 0, []

    def copy(self, src, dst, to):
        i = self.made
        self.made += 1
        made = self.again(i, src, dst, to)
        self.sent.append(made)
        return made

    def again(self, i, src, dst, to):
        return pltpu.make_async_remote_copy(
            src_ref=src, dst_ref=dst, send_sem=self.send.at[i], recv_sem=self.recv.at[i],
            device_id=to, device_id_type=MESH)

    def finish(self):
        for copy in self.sent:
            copy.wait_send()


def at(start, size):
    return pl.ds(pl.multiple_of(start, size), size)


def dot(a, b, dims=NN):
    return lax.dot_general(a, b, dims, preferred_element_type=F32)


def when(condition):
    if isinstance(condition, bool):
        return (lambda f: f()) if condition else (lambda f: None)
    return pl.when(condition)


def both(*conditions):
    if any(isinstance(x, bool) and not x for x in conditions):
        return False
    conditions = [x for x in conditions if not isinstance(x, bool)]
    return functools.reduce(jnp.logical_and, conditions) if conditions else True


def head_pass(view, h, bias, qt, gt, k_rows, v_rows, kt, vt, st, pb, gs, att_t, dq_t, own, term):
    head = slice(h * 64, (h + 1) * 64)
    row = lax.broadcasted_iota(jnp.int32, (128, 1), 0)
    mine = (row >= 64) if h else (row < 64)
    qm = jnp.where(mine, qt, jnp.zeros_like(qt)).astype(BF)
    gm = jnp.where(mine, gt, jnp.zeros_like(gt)).astype(BF)
    cols = slice(h * TOK, (h + 1) * TOK)
    blocks = [pl.ds(j * TOK, TOK) for j in range(6)]
    tops = []
    for j in range(0, 6, SPAN):
        s = dot(k_rows(j, SPAN), qm)
        for i in range(SPAN):
            part = s[i * TOK:(i + 1) * TOK]
            st[h, blocks[j + i], :] = part
            tops.append(jnp.max(part, axis=0, keepdims=True) * (SCALE * LOG2E) + bias[j + i])
            yield
    top = functools.reduce(jnp.maximum, tops)
    total = jnp.zeros((1, TOK), F32)
    for j, rows in enumerate(blocks):
        e = jnp.exp2(st[h, rows, :] * (SCALE * LOG2E) - (top - bias[j]))
        st[h, rows, :] = e
        total = total + jnp.sum(e, axis=0, keepdims=True)
        yield
    inv = 1.0 / total
    for rows in blocks:
        pb[rows, cols] = (st[h, rows, :] * inv).astype(BF)
        yield
    ot = dot(vt()[head], pb[:, cols])
    att_t[h] = ot
    delta = jnp.sum(gt[head] * ot, axis=0, keepdims=True)
    yield
    for j in range(0, 6, SPAN):
        d = dot(v_rows(j, SPAN), gm)
        for i in range(SPAN):
            part = d[i * TOK:(i + 1) * TOK]
            gs[blocks[j + i], cols] = (st[h, blocks[j + i], :] * inv * (part - delta)).astype(BF)
            yield
    dq_t[h] = dot(kt()[head], gs[:, cols]) * SCALE
    yield
    q_head, g_head = qt[head].astype(BF), gt[head].astype(BF)
    for j, rows in enumerate(blocks):
        b = j + 2 * view
        grads = dot(q_head, gs[rows, cols], NT) * SCALE, dot(g_head, pb[rows, cols], NT)
        for i, grad in enumerate(grads):
            if b in (3, 4):
                w = pl.ds((b - 3) * TOK, TOK)
                grad = grad if b - 3 == view else grad.astype(BF).astype(F32)
                own[i, head, w] = grad if view == 0 else own[i, head, w] + grad
            else:
                n, w = {0: (2, 0), 1: (0, 0), 2: (0, 1), 5: (1, 0), 6: (1, 1), 7: (2, 1)}[b]
                w = pl.ds(w * TOK, TOK)
                grad = grad.astype(BF)
                if b in (2, 5) and view == 1:
                    grad = (term[n, i, head, w].astype(F32) + grad.astype(F32)).astype(BF)
                term[n, i, head, w] = grad
        yield


def project(lat, w, s, p, k_s, v_s, q_s):
    span = PROJECT_ROWS
    first, count = 3 * lat.shape[1] // 8, lat.shape[1] // 4
    w_kv = w[:, pl.ds(pl.multiple_of(p * 384 + 128, 128), 256)]
    for r in range(lat.shape[1] // span):
        rows = pl.ds(r * span, span)
        kv = dot(lat[s, rows, :], w_kv).astype(BF)
        k_s[rows, :] = kv[:, :128]
        v_s[rows, :] = kv[:, 128:]
        yield
    q_s[...] = dot(lat[s, pl.ds(first, count), :], w[:, at(p * 384, 128)]).astype(BF)
    yield


def weave(threads):
    threads = list(threads)
    tick = 0
    while threads:
        for thread in list(threads):
            start, every, work = thread
            if tick >= start and (tick - start) % every == 0:
                try:
                    next(work)
                except StopIteration:
                    threads.remove(thread)
        tick += 1


def attend(bias, s, p, g_ref, k_s, v_s, q_s, st, pb, gs, att, dq, own, term, beside=()):
    kt = k_s[...].T
    vt = v_s[...].T
    threads = list(beside)
    results = []
    for view in range(2):
        rows = pl.ds(view * TOK, TOK)
        q = q_s[rows, :]
        g = g_ref[s, rows, at(p * 128, 128)]
        gt = g.astype(F32).T
        span = slice(2 * view * TOK, (2 * view + 6) * TOK)

        qt = q.astype(F32).T

        def rows_of(ref, view=view):
            return lambda j, n: ref[pl.ds((2 * view + j) * TOK, n * TOK), :]

        att_t, dq_t = {}, {}
        results.append((rows, att_t, dq_t))
        for h in range(2):
            threads.append((OFFSET * (2 * view + h), 1, head_pass(
                view, h, bias[view], qt, gt, rows_of(k_s), rows_of(v_s), lambda span=span: kt[:, span],
                lambda span=span: vt[:, span], st.at[view], pb.at[view], gs.at[view], att_t, dq_t, own, term)))
    weave(threads)
    for rows, att_t, dq_t in results:
        att[rows, :] = jnp.concatenate([att_t[0], att_t[1]], axis=0).T.astype(BF)
        dq[rows, :] = jnp.concatenate([dq_t[0], dq_t[1]], axis=0).T.astype(BF)


OFFSET, SPAN, PROJECT_ROWS = 9, 1, 512
STEPS = 8
KINDS = ("a1u", "a1d", "bx", "a2u", "a2d", "b1u", "b1d", "ax", "b2u", "b2d")


def sample_and_pair(t):
    return t // 4, t % 4


def main_kernel(cycle_ref, cross_ref, lat_hbm, w_hbm, g_hbm, att_full, dw_out, dl_out,
                lat, w, g, k_s, v_s, q_s, st, pb, gs, att, own, out, inbox, gp, dwb, dl_out_s, dl_in,
                z1u, z1d, z2u, z2d, su, sd, zs, xin, xain, xa, q1u, q1d, q2u, q2d, qsu, qsd,
                whole, parts, fin, fing,
                local, tsend, trecv, rsend, rrecv, vsend, vrecv, dsend, drecv, gsend, grecv):
    me = Place()
    c, y, z, xh, xl = me.core, me.y, me.z, me.x_hi, me.x_lo
    zu, zd, zf = (z + 1) % 4, (z + 3) % 4, (z + 2) % 4
    width = 512
    strips, kept = [], []
    for p in range(4):
        for k in range(3):
            strips.append(pltpu.make_async_copy(
                w_hbm.at[:, at((2 * k + c) * width + p * 128, 128)],
                w.at[at(me.fsdp * 128, 128), pl.ds((3 * p + k) * 128, 128)], local.at[3 * p + k]))
    for s in range(2):
        kept.append(pltpu.make_async_copy(lat_hbm.at[s], lat.at[s, at((3 + c) * TOK, TOK)], local.at[12 + s]))
        kept.append(pltpu.make_async_copy(g_hbm.at[s, :, at(c * width, width)], g.at[s, at(c * TOK, TOK)], local.at[14 + s]))
    for copy in strips + kept:
        copy.start()
    chip = me.view // 2
    chips = [{"view": 2 * ((chip + d) % 8) + c, "fsdp": me.fsdp} for d in range(8)]
    others = [{"view": 2 * ((chip + d) % 8) + 1 - c, "fsdp": me.fsdp} for d in range(8)]
    greet((*chips[1:], *others, me.z_up, me.z_down, me.outer))

    def weight(link):
        return jnp.where(link > 0, 0.0, -1e30).astype(F32)

    a = me.view - c

    def cyc(v):
        return weight(cycle_ref[(v + 16) % 16])

    bias = [
        [weight(cross_ref[a % 8]), cyc(a - 2), 0.0, 0.0, 0.0, cyc(a)],
        [cyc(a - 1), 0.0, 0.0, 0.0, cyc(a + 1), weight(cross_ref[(a + 1) % 8])],
    ]
    first, last = y == 0, y == 3
    edge = jnp.logical_or(first, last)
    keep_down = jnp.where(first, 0.0, 1.0)
    keep_up = jnp.where(last, 0.0, 1.0)

    def mail(src, dst, send, recv, to):
        return pltpu.make_async_remote_copy(
            src_ref=src, dst_ref=dst, send_sem=send, recv_sem=recv, device_id=to, device_id_type=MESH)

    def up(t, i):
        return mail(out.at[t % 3, 1, i], inbox.at[t, 1, i], tsend.at[i, t % 3], trecv.at[i, t], me.up)

    def down(t, i):
        return mail(out.at[t % 3, 0, i], inbox.at[t, 0, i], tsend.at[2 + i, t % 3], trecv.at[2 + i, t], me.down)

    def across(t, i):
        return mail(out.at[t % 3, 2, i], inbox.at[t, 2, i], tsend.at[4 + i, t % 3], trecv.at[4 + i, t], me.pair)

    def columns(t):
        return at(c * width + sample_and_pair(t)[1] * 128, 128)

    def att_mate(t):
        return mail(att.at[t % 3, at((1 - c) * TOK, TOK)], att_full.at[sample_and_pair(t)[0], :, columns(t)],
                    tsend.at[6, t % 3], trecv.at[6, t], me.mate)

    def att_own(t):
        return pltpu.make_async_copy(
            att.at[t % 3, at(c * TOK, TOK)], att_full.at[sample_and_pair(t)[0], :, columns(t)], tsend.at[7, t % 3])

    def red(kind, p, src, dst, to):
        i = KINDS.index(kind)
        return mail(src, dst, rsend.at[i, p], rrecv.at[i, p], to)

    lo, hi, top, low = pl.ds(0, 32), pl.ds(32, 32), pl.ds(0, 64), pl.ds(64, 64)
    def a1u(p):
        return red("a1u", p, dwb.at[p, :, zf, lo], z1u.at[p], me.z_up)

    def a1d(p):
        return red("a1d", p, dwb.at[p, :, zf, hi], z1d.at[p], me.z_down)

    def bx(p):
        return red("bx", p, dwb.at[p, 1 - xh, :, low], xain.at[p], me.outer)

    def a2u(p):
        return red("a2u", p, su.at[p], z2u.at[p], me.z_up)

    def a2d(p):
        return red("a2d", p, sd.at[p], z2d.at[p], me.z_down)

    def b1u(p):
        return red("b1u", p, xa.at[p, zf, lo], q1u.at[p], me.z_up)

    def b1d(p):
        return red("b1d", p, xa.at[p, zf, hi], q1d.at[p], me.z_down)

    def ax(p):
        return red("ax", p, zs.at[p, 1 - xh], xin.at[p], me.outer)

    def b2u(p):
        return red("b2u", p, qsu.at[p], q2u.at[p], me.z_up)

    def b2d(p):
        return red("b2d", p, qsd.at[p], q2d.at[p], me.z_down)

    def scatter(group):
        return [mail(whole.at[pl.ds(2 * group, 2), at(((chip + d) % 8) * 16, 16)], parts.at[group, d - 1],
                     vsend.at[group, d - 1], vrecv.at[group, d - 1], chips[d]) for d in range(1, 8)]

    def spread(group):
        rows = at(chip * 16, 16)
        return [mail(fin.at[group], fing.at[c, pl.ds(2 * group, 2), rows], vsend.at[group, 7 + i], vrecv.at[group, 7 + i], to)
                for i, to in enumerate((*chips[1:], *others))]

    def f32(x):
        return x.astype(F32)

    def weight_grad(t):
        slot = t % 3
        p = sample_and_pair(t)[1]

        def share(b):
            if b in (3, 4):
                part = own[slot, :, :, (b - 3) * TOK:(b - 2) * TOK].astype(BF)
            else:
                n, w = {0: (2, 0), 1: (0, 0), 2: (0, 1), 5: (1, 0), 6: (1, 1), 7: (2, 1)}[b]
                part = out[slot, n, :, :, w * TOK:(w + 1) * TOK]
            return part.reshape(256, TOK)

        mine = pl.ds(3 * TOK, 2 * TOK)
        queries = gp[p, pl.ds(512, 512), :128].astype(F32).T.astype(BF)
        sums = gp[p, pl.ds(0, 512), :].astype(F32).T.astype(BF)
        for f in range(4):
            cols = slice(f * 256, (f + 1) * 256)
            earlier = dot(sums, lat[0, mine, cols])
            total = earlier[128:]
            for b in range(8):
                total = total + dot(share(b), lat[1, pl.ds(b * TOK, TOK), cols])
            for k in range(2):
                half = slice(k * 128, (k + 1) * 128)
                block = dwb.at[p, f // 2, 2 * (f % 2) + k]
                block[:, :128] = (earlier[:128, half] + dot(queries, lat[1, mine, f * 256 + k * 128:f * 256 + (k + 1) * 128])).T.astype(BF)
                block[:, 128:] = total[:, half].T.astype(BF)

    def phase1(p):
        for make in (a1u, a1d, bx):
            make(p).start()

    def phase2(p):
        a1u(p).wait_recv()
        a1d(p).wait_recv()
        su[p, :, lo] = (f32(dwb[p, :, zu, lo]) + f32(z1u[p])).astype(BF)
        su[p, :, hi] = dwb[p, :, zu, hi]
        sd[p, :, lo] = dwb[p, :, zd, lo]
        sd[p, :, hi] = (f32(dwb[p, :, zd, hi]) + f32(z1d[p])).astype(BF)
        a2u(p).start()
        a2d(p).start()
        bx(p).wait_recv()
        xa[p] = (f32(dwb[p, xh, :, low]) + f32(xain[p])).astype(BF)
        b1u(p).start()
        b1d(p).start()

    def phase3(p):
        b1u(p).wait_recv()
        b1d(p).wait_recv()
        qsu[p, lo] = (f32(xa[p, zu, lo]) + f32(q1u[p])).astype(BF)
        qsu[p, hi] = xa[p, zu, hi]
        qsd[p, lo] = xa[p, zd, lo]
        qsd[p, hi] = (f32(xa[p, zd, hi]) + f32(q1d[p])).astype(BF)
        b2u(p).start()
        b2d(p).start()
        a2u(p).wait_recv()
        a2d(p).wait_recv()
        zs[p] = (f32(dwb[p, :, z, top]) + f32(z2u[p]) + f32(z2d[p])).astype(BF)
        ax(p).start()

    def phase4(p):
        b2u(p).wait_recv()
        b2d(p).wait_recv()
        whole[p, low] = (f32(xa[p, z]) + f32(q2u[p]) + f32(q2d[p])).astype(BF)
        ax(p).wait_recv()
        whole[p, top] = (f32(zs[p, xh]) + f32(xin[p])).astype(BF)
        if p % 2:
            for copy in scatter(p // 2):
                copy.start()

    def phase5(p):
        if p % 2:
            group = p // 2
            total = f32(whole[2 * group:2 * group + 2, at(chip * 16, 16)])
            for d, copy in enumerate(scatter(group)):
                copy.wait_recv()
                total = total + f32(parts[group, d])
            fin[group] = total.astype(BF)
            fing[c, 2 * group:2 * group + 2, at(chip * 16, 16)] = total.astype(BF)
            for copy in spread(group):
                copy.start()

    phases = (phase1, phase2, phase3, phase4, phase5)
    begins = (4, 5, 6, 7)

    def gather_grads(t):
        across(t, 0).wait_recv()
        across(t, 1).wait_recv()
        s, p = sample_and_pair(t)
        for i in range(2):
            total = own[t % 3, i] + f32(inbox[t, 2, i]) + f32(inbox[t, 1, i]) * keep_down + f32(inbox[t, 0, i]) * keep_up
            gp[p, at(s * 512, 512), (1 + i) * 128:(2 + i) * 128] = total.T.astype(BF)

    def join(u, i):
        up(u, i).wait_recv()
        down(u, i).wait_recv()

        @pl.when(first)
        def _():
            out[u % 3, 2, i] = (f32(out[u % 3, 2, i]) + f32(inbox[u, 1, i])).astype(BF)

        @pl.when(last)
        def _():
            out[u % 3, 2, i] = (f32(out[u % 3, 2, i]) + f32(inbox[u, 0, i])).astype(BF)

        pl.when(edge)(across(u, i).start)

    def service(t):
        @pl.when(t >= 1)
        def _():
            join(t - 1, 0)
            join(t - 1, 1)

        for p, begin in reversed(list(enumerate(begins))):
            for k, phase in enumerate(phases):
                if 0 < k and begin + k < STEPS:
                    pl.when(t == begin + k)(functools.partial(phase, p))

        pl.when(t >= 2)(lambda: gather_grads(t - 2))

    sent = []
    slots = iter(range(64))

    def post(src, dst, to, own=None):
        i = next(slots)
        made = mail(src, dst, gsend.at[i], grecv.at[i], to)
        sent.append(made)
        return made if own is None else (made, mail(own, dst, gsend.at[i], grecv.at[i], to))

    def rows_at(s, b, start=0, size=TOK):
        return lat.at[s, at(b * TOK + start, size)]

    def w_at(f, group, start=0, size=128):
        return w.at[at(f * 128 + start, size), pl.ds(1152, 384) if group else pl.ds(0, 1152)]

    cuts = {0: [(i * 64, 64) for i in range(4)], 1: [(0, TOK // 2), (TOK // 2, TOK // 2)]}
    to_pair, to_up, to_down, to_mate, relays, g_mate = {}, {}, {}, {}, {}, []
    for s in range(2):
        to_pair[s] = [post(lat_hbm.at[s, pl.ds(*cut)], rows_at(s, 7 * c, *cut), me.pair) for cut in cuts[s]]
        to_up[s] = [post(rows_at(s, 7 * c, *cut), rows_at(s, 1 + c, *cut), me.up, lat_hbm.at[s, pl.ds(*cut)]) for cut in cuts[s]]
        to_down[s] = [post(rows_at(s, 7 * c, *cut), rows_at(s, 5 + c, *cut), me.down, lat_hbm.at[s, pl.ds(*cut)]) for cut in cuts[s]]
        to_mate[s] = post(lat_hbm.at[s], rows_at(s, 3 + c), me.mate)
        relays[s] = [post(rows_at(s, b), rows_at(s, b), me.mate) for b in (7 * c, 1 + c, 5 + c)]
        g_mate.append(post(g_hbm.at[s, :, at((1 - c) * width, width)], g.at[s, at(c * TOK, TOK)], me.mate))
    f0, f_up, f_down, f_out, far = me.fsdp, me.f_up, me.f_down, me.f_outer, me.f_far
    w_mail = [dict(
        up=post(w_at(f0, grp), w_at(f0, grp), me.z_up),
        down=post(w_at(f0, grp), w_at(f0, grp), me.z_down),
        out=post(w_at(f0, grp), w_at(f0, grp), me.outer),
        up2=post(w_at(f_down, grp, 0, 64), w_at(f_down, grp, 0, 64), me.z_up),
        down2=post(w_at(f_up, grp, 64, 64), w_at(f_up, grp, 64, 64), me.z_down),
        out_up=post(w_at(f_out, grp), w_at(f_out, grp), me.z_up),
        out_down=post(w_at(f_out, grp), w_at(f_out, grp), me.z_down),
        far0=post(w_at(far, grp, 0, 64), w_at(far, grp, 0, 64), me.outer),
        far1=post(w_at(far, grp, 64, 64), w_at(far, grp, 64, 64), me.outer),
    ) for grp in range(2)]

    def w_first(grp):
        for copy in strips[9:] if grp else strips[:9]:
            copy.wait()
        for name in ("up", "down", "out"):
            w_mail[grp][name].start()

    def w_second(grp):
        m = w_mail[grp]
        m["up"].wait_recv()
        m["up2"].start()
        m["down"].wait_recv()
        m["down2"].start()
        m["out"].wait_recv()
        m["out_up"].start()
        m["out_down"].start()

    def w_third(grp):
        m = w_mail[grp]
        m["up2"].wait_recv()
        m["far0"].start()
        m["down2"].wait_recv()
        m["far1"].start()

    def w_last(grp):
        for name in ("out_up", "out_down", "far0", "far1"):
            w_mail[grp][name].wait_recv()

    def lat_first(s):
        for i in range(len(cuts[s])):
            pl.when(jnp.logical_not(last))(to_up[s][i][1].start)
            pl.when(jnp.logical_not(first))(to_down[s][i][1].start)
        to_mate[s].start()
        g_mate[s].start()

    def lat_wrap(s, i):
        to_pair[s][i].wait_recv()
        pl.when(last)(to_up[s][i][0].start)
        pl.when(first)(to_down[s][i][0].start)

    def lat_relay(s):
        for i in range(len(cuts[s])):
            to_up[s][i][0].wait_recv()
        relays[s][1].start()
        for i in range(len(cuts[s])):
            to_down[s][i][0].wait_recv()
        relays[s][2].start()

    def lat_last(s):
        for copy in (to_mate[s], g_mate[s], *relays[s]):
            copy.wait_recv()

    chunks = len(cuts[0])
    to_pair[0][0].start()
    to_pair[0][1].start()
    w_first(0)
    lat_first(0)
    for i in range(chunks):
        to_pair[0][i].wait_send()
        if i + 2 < chunks:
            to_pair[0][i + 2].start()
        lat_wrap(0, i)
        if i == 1:
            w_second(0)
            to_pair[1][0].start()
        if i == 2:
            w_third(0)
    relays[0][0].start()
    to_pair[1][1].start()
    w_first(1)
    lat_relay(0)
    lat_first(1)
    w_second(1)
    w_last(0)
    for copy in kept:
        copy.wait()
    lat_last(0)
    lat_wrap(1, 0)

    def projected(t, slot):
        for _ in project(lat, w, *sample_and_pair(t), k_s.at[slot], v_s.at[slot], q_s.at[slot]):
            pass

    projected(0, 0)

    def step(t, carry):
        s, p = sample_and_pair(t)

        @pl.when(t == 2)
        def _():
            w_last(1)

        @pl.when(t == 4)
        def _():
            lat_last(1)
            projected(4, 0)

        @pl.when(t >= 3)
        def _():
            u = t - 3
            for i in range(2):
                up(u, i).wait_send()
                down(u, i).wait_send()
                across(u, i).wait_send()
            att_mate(u).wait_send()
            att_own(u).wait()

        now, later = t % 2, (t + 1) % 2
        s_next, p_next = sample_and_pair(jnp.where(t == 3, 3, jnp.minimum(t + 1, STEPS - 1)))
        beside = project(lat, w, s_next, p_next, k_s.at[later], v_s.at[later], q_s.at[later])
        attend(bias, s, p, g, k_s.at[now], v_s.at[now], q_s.at[now], st, pb, gs, att.at[t % 3],
               gp.at[p, at(s * 512, 512), pl.ds(0, 128)], own.at[t % 3], out.at[t % 3], [(4, 2, beside)])
        def send(i):
            up(t, i).start()
            down(t, i).start()
            pl.when(jnp.logical_not(edge))(across(t, i).start)

        send(0)
        att_mate(t).start()
        att_own(t).start()

        @pl.when(t >= 4)
        def _():
            weight_grad(t)
            phase1(t - 4)

        send(1)

        @pl.when(t == 0)
        def _():
            lat_wrap(1, 1)
            relays[1][0].start()
            w_third(1)

        @pl.when(t == 2)
        def _():
            lat_relay(1)

        service(t)
        return carry

    lax.fori_loop(0, STEPS, step, 0)

    def latent_grad(pairs):
        for n in range(4):
            for r in range(4):
                rows = pl.ds(r * 256, 256)
                total = None if pairs[0] == 0 else st[n // 2, n % 2, rows, :]
                for p in pairs:
                    part = dot(gp[p, rows, :], w[pl.ds(n * 256, 256), p * 384:(p + 1) * 384], NT)
                    total = part if total is None else total + part
                st[n // 2, n % 2, rows, :] = total

    def dl_mate():
        return mail(dl_out_s, dl_in, dsend.at[0], drecv.at[0], me.mate)

    def finish(group):
        for copy in spread(group):
            copy.wait_recv()
        for p in (2 * group, 2 * group + 1):
            for core in range(2):
                for k in range(3):
                    first_column = (2 * k + core) * width + p * 128
                    dw_out[:, first_column:first_column + 128] = f32(fing[core, p, :, k * 128:(k + 1) * 128])

    end = STEPS - 1
    join(end, 0)
    latent_grad((0,))
    join(end, 1)
    phase2(3)
    phase3(2)
    phase4(1)
    gather_grads(end - 1)
    latent_grad((1,))
    phase3(3)
    phase4(2)
    phase5(1)
    gather_grads(end)
    latent_grad((2,))
    phase4(3)
    latent_grad((3,))
    for s in range(2):
        for n in range(4):
            dl_out_s[s, :, n * 256:(n + 1) * 256] = st[n // 2, n % 2, at(s * 512 + (1 - c) * TOK, TOK), :].astype(BF)
    dl_mate().start()
    phase5(3)
    finish(0)
    dl_mate().wait_recv()
    for s in range(2):
        for n in range(4):
            cols = slice(n * 256, (n + 1) * 256)
            dl_out[s, :, cols] = (st[n // 2, n % 2, at(s * 512 + c * TOK, TOK), :] + f32(dl_in[s, :, cols])).astype(BF)
    finish(1)
    for t in range(STEPS - 3, STEPS):
        for make in (up, down, across):
            make(t, 0).wait_send()
            make(t, 1).wait_send()
        att_mate(t).wait_send()
        att_own(t).wait()
    for t in range(STEPS):
        att_mate(t).wait_recv()
    dl_mate().wait_send()
    for p in range(4):
        for make in (a1u, a1d, bx, a2u, a2d, b1u, b1d, ax, b2u, b2d):
            make(p).wait_send()
    for group in range(2):
        for copy in scatter(group) + spread(group):
            copy.wait_send()
    for i, copy in enumerate(sent):
        if i >= chunks:
            copy.wait_send()


def local(latents, w_qkv, cycle_links, cross_links, d_attended):
    _, _, samples, toks, model = latents.shape
    rows, wide = w_qkv.shape
    half = model // 2
    ANY = pl.BlockSpec(memory_space=pl.ANY)
    VM = pl.BlockSpec(memory_space=pltpu.VMEM)
    SM = pl.BlockSpec(memory_space=pltpu.SMEM)
    def vm(*shape, dtype=BF):
        return pltpu.VMEM(shape, dtype)

    W = 384
    att_full, dw_out, dl_out = pl.pallas_call(
        main_kernel,
        in_specs=[SM, SM, ANY, ANY, ANY],
        out_specs=[VM, VM, VM],
        out_shape=[
            jax.ShapeDtypeStruct((samples, toks, model), BF),
            jax.ShapeDtypeStruct((rows, wide), F32),
            jax.ShapeDtypeStruct((samples, toks, model), BF),
        ],
        scratch_shapes=[
            vm(samples, 8 * toks, model), vm(model, wide // 2), vm(samples, 2 * toks, half),
            vm(2, 8 * toks, 128), vm(2, 8 * toks, 128), vm(2, 2 * toks, 128),
            vm(2, 2, 6 * toks, toks, dtype=F32), vm(2, 6 * toks, 2 * toks), vm(2, 6 * toks, 2 * toks),
            vm(3, 2 * toks, 128), vm(3, 2, 128, 2 * toks, dtype=F32),
            vm(3, 3, 2, 128, 2 * toks), vm(STEPS, 3, 2, 128, 2 * toks),
            vm(4, samples * 2 * toks, W), vm(4, 2, 4, rows, W),
            vm(samples, toks, model), vm(samples, toks, model),
            vm(4, 2, 32, W), vm(4, 2, 32, W),
            vm(4, 2, 64, W), vm(4, 2, 64, W), vm(4, 2, 64, W), vm(4, 2, 64, W), vm(4, 2, 64, W),
            vm(4, 64, W), vm(4, 4, 64, W), vm(4, 4, 64, W),
            vm(4, 32, W), vm(4, 32, W),
            vm(4, 64, W), vm(4, 64, W), vm(4, 64, W), vm(4, 64, W),
            vm(4, rows, W), vm(2, 7, 2, 16, W), vm(2, 2, 16, W), vm(2, 4, rows, W),
            pltpu.SemaphoreType.DMA((16,)),
            pltpu.SemaphoreType.DMA((8, 3)), pltpu.SemaphoreType.DMA((7, STEPS)),
            pltpu.SemaphoreType.DMA((len(KINDS), 4)), pltpu.SemaphoreType.DMA((len(KINDS), 4)),
            pltpu.SemaphoreType.DMA((2, 22)), pltpu.SemaphoreType.DMA((2, 22)),
            pltpu.SemaphoreType.DMA((1,)), pltpu.SemaphoreType.DMA((1,)),
            pltpu.SemaphoreType.DMA((64,)), pltpu.SemaphoreType.DMA((64,)),
        ],
        compiler_params=pltpu.CompilerParams(collective_id=0, has_side_effects=True, vmem_limit_bytes=63 * 2**20),
    )(cycle_links[0], cross_links[0], latents[0, 0], w_qkv, d_attended[0, 0])
    return att_full[None, None], dl_out[None, None], dw_out


def solution(mesh):
    wide = P("fsdp", "view", None, None, None)
    rows = P("fsdp", None)
    return jax.shard_map(
        local,
        mesh=mesh,
        in_specs=(wide, rows, rows, rows, wide),
        out_specs=(wide, wide, rows),
        check_vma=False,
    )
```

```python
import functools

import jax
import jax.numpy as jnp
from jax import lax
from jax.experimental import pallas as pl
from jax.experimental.pallas import tpu as pltpu
from jax.sharding import PartitionSpec as P

BF, F32 = jnp.bfloat16, jnp.float32
MESH = pl.DeviceIdType.MESH
TOK = 256
LOG2E = 1.4426950408889634
SCALE = 0.125
NT = (((1,), (1,)), ((), ()))
NN = (((1,), (0,)), ((), ()))
TN = (((0,), (0,)), ((), ()))
VMEM_LIMIT = 60 * 2**20


class Place:
    def __init__(self):
        v, f = lax.axis_index("view"), lax.axis_index("fsdp")
        self.view, self.fsdp = v, f
        self.ys, self.zs = 4, 4
        self.core = v % 2
        self.y = (v // 2) % 4
        self.x_lo = v // 8
        self.z = f % 4
        self.x_hi = f // 4
        column = self.x_lo * 8 + self.core

        def at(view, fsdp):
            return {"view": view, "fsdp": fsdp}

        self.up = at(column + 2 * ((self.y + 1) % 4), f)
        self.down = at(column + 2 * ((self.y + 3) % 4), f)
        self.over = at(column + 2 * ((self.y + 2) % 4), f)
        self.pair = at((v + 8) % 16, f)
        self.mate = at(v + 1 - 2 * self.core, f)
        self.f_up = self.x_hi * 4 + (self.z + 1) % 4
        self.f_down = self.x_hi * 4 + (self.z + 3) % 4
        self.f_far = self.x_hi * 4 + (self.z + 2) % 4
        self.f_outer = (f + 4) % 8
        self.z_up = at(v, self.f_up)
        self.z_down = at(v, self.f_down)
        self.outer = at((v + 8) % 16, self.f_outer)


def greet(devices):
    barrier = pltpu.get_barrier_semaphore()
    for device in devices:
        pl.semaphore_signal(barrier, inc=1, device_id=device, device_id_type=MESH)
    pl.semaphore_wait(barrier, len(devices))


class Mail:
    def __init__(self, send, recv):
        self.send, self.recv, self.made, self.sent = send, recv, 0, []

    def copy(self, src, dst, to):
        i = self.made
        self.made += 1
        made = self.again(i, src, dst, to)
        self.sent.append(made)
        return made

    def again(self, i, src, dst, to):
        return pltpu.make_async_remote_copy(
            src_ref=src, dst_ref=dst, send_sem=self.send.at[i], recv_sem=self.recv.at[i],
            device_id=to, device_id_type=MESH)

    def finish(self):
        for copy in self.sent:
            copy.wait_send()


def at(start, size):
    return pl.ds(pl.multiple_of(start, size), size)


def dot(a, b, dims=NN):
    return lax.dot_general(a, b, dims, preferred_element_type=F32)


def when(condition):
    if isinstance(condition, bool):
        return (lambda f: f()) if condition else (lambda f: None)
    return pl.when(condition)


def both(*conditions):
    if any(isinstance(x, bool) and not x for x in conditions):
        return False
    conditions = [x for x in conditions if not isinstance(x, bool)]
    return functools.reduce(jnp.logical_and, conditions) if conditions else True


def head_pass(view, h, bias, qt, gt, k_rows, v_rows, kt, vt, st, pb, gs, att_t, dq_t, own, term):
    head = slice(h * 64, (h + 1) * 64)
    row = lax.broadcasted_iota(jnp.int32, (128, 1), 0)
    mine = (row >= 64) if h else (row < 64)
    qm = jnp.where(mine, qt, jnp.zeros_like(qt)).astype(BF)
    gm = jnp.where(mine, gt, jnp.zeros_like(gt)).astype(BF)
    cols = slice(h * TOK, (h + 1) * TOK)
    blocks = [pl.ds(j * TOK, TOK) for j in range(6)]
    tops = []
    for j in range(0, 6, SPAN):
        s = dot(k_rows(j, SPAN), qm)
        for i in range(SPAN):
            part = s[i * TOK:(i + 1) * TOK]
            st[h, blocks[j + i], :] = part
            tops.append(jnp.max(part, axis=0, keepdims=True) * (SCALE * LOG2E) + bias[j + i])
            yield
    top = functools.reduce(jnp.maximum, tops)
    total = jnp.zeros((1, TOK), F32)
    for j, rows in enumerate(blocks):
        e = jnp.exp2(st[h, rows, :] * (SCALE * LOG2E) - (top - bias[j]))
        st[h, rows, :] = e
        total = total + jnp.sum(e, axis=0, keepdims=True)
        yield
    inv = 1.0 / total
    for rows in blocks:
        pb[rows, cols] = (st[h, rows, :] * inv).astype(BF)
        yield
    ot = dot(vt()[head], pb[:, cols])
    att_t[h] = ot
    delta = jnp.sum(gt[head] * ot, axis=0, keepdims=True)
    yield
    for j in range(0, 6, SPAN):
        d = dot(v_rows(j, SPAN), gm)
        for i in range(SPAN):
            part = d[i * TOK:(i + 1) * TOK]
            gs[blocks[j + i], cols] = (st[h, blocks[j + i], :] * inv * (part - delta)).astype(BF)
            yield
    dq_t[h] = dot(kt()[head], gs[:, cols]) * SCALE
    yield
    q_head, g_head = qt[head].astype(BF), gt[head].astype(BF)
    for j, rows in enumerate(blocks):
        b = j + 2 * view
        grads = dot(q_head, gs[rows, cols], NT) * SCALE, dot(g_head, pb[rows, cols], NT)
        for i, grad in enumerate(grads):
            if b in (3, 4):
                w = pl.ds((b - 3) * TOK, TOK)
                grad = grad if b - 3 == view else grad.astype(BF).astype(F32)
                own[i, head, w] = grad if view == 0 else own[i, head, w] + grad
            else:
                n, w = {0: (2, 0), 1: (0, 0), 2: (0, 1), 5: (1, 0), 6: (1, 1), 7: (2, 1)}[b]
                w = pl.ds(w * TOK, TOK)
                grad = grad.astype(BF)
                if b in (2, 5) and view == 1:
                    grad = (term[n, i, head, w].astype(F32) + grad.astype(F32)).astype(BF)
                term[n, i, head, w] = grad
        yield


def project(lat, w, s, p, k_s, v_s, q_s):
    span = PROJECT_ROWS
    first, count = 3 * lat.shape[1] // 8, lat.shape[1] // 4
    w_kv = w[:, pl.ds(pl.multiple_of(p * 384 + 128, 128), 256)]
    for r in range(lat.shape[1] // span):
        rows = pl.ds(r * span, span)
        kv = dot(lat[s, rows, :], w_kv).astype(BF)
        k_s[rows, :] = kv[:, :128]
        v_s[rows, :] = kv[:, 128:]
        yield
    q_s[...] = dot(lat[s, pl.ds(first, count), :], w[:, at(p * 384, 128)]).astype(BF)
    yield


def weave(threads):
    threads = list(threads)
    tick = 0
    while threads:
        for thread in list(threads):
            start, every, work = thread
            if tick >= start and (tick - start) % every == 0:
                try:
                    next(work)
                except StopIteration:
                    threads.remove(thread)
        tick += 1


def attend(bias, s, p, g_ref, k_s, v_s, q_s, st, pb, gs, att, dq, own, term, beside=()):
    kt = k_s[...].T
    vt = v_s[...].T
    threads = list(beside)
    results = []
    for view in range(2):
        rows = pl.ds(view * TOK, TOK)
        q = q_s[rows, :]
        g = g_ref[s, rows, at(p * 128, 128)]
        gt = g.astype(F32).T
        span = slice(2 * view * TOK, (2 * view + 6) * TOK)

        qt = q.astype(F32).T

        def rows_of(ref, view=view):
            return lambda j, n: ref[pl.ds((2 * view + j) * TOK, n * TOK), :]

        att_t, dq_t = {}, {}
        results.append((rows, att_t, dq_t))
        for h in range(2):
            threads.append((OFFSET * (2 * view + h), 1, head_pass(
                view, h, bias[view], qt, gt, rows_of(k_s), rows_of(v_s), lambda span=span: kt[:, span],
                lambda span=span: vt[:, span], st.at[view], pb.at[view], gs.at[view], att_t, dq_t, own, term)))
    weave(threads)
    for rows, att_t, dq_t in results:
        att[rows, :] = jnp.concatenate([att_t[0], att_t[1]], axis=0).T.astype(BF)
        dq[rows, :] = jnp.concatenate([dq_t[0], dq_t[1]], axis=0).T.astype(BF)


OFFSET, SPAN, PROJECT_ROWS = 10, 1, 512
STEPS, SLOTS = 8, 4
KINDS = ("a1u", "a1d", "bx", "a2u", "a2d", "b1u", "b1d", "ax", "b2u", "b2d")


def sample_and_pair(t):
    return t // 4, t % 4


def main_kernel(cycle_ref, cross_ref, lat_hbm, w_hbm, g_hbm, att_full, dw_out, dl_out,
                lat, w, g, k_s, v_s, q_s, st, pb, gs, att, own, out, inbox, gp, dwb, dl_out_s, dl_in,
                z1u, z1d, z2u, z2d, su, sd, zs, xin, xain, xa, q1u, q1d, q2u, q2d, qsu, qsd,
                whole, parts, fin, fing,
                local, tsend, trecv, rsend, rrecv, vsend, vrecv, dsend, drecv, gsend, grecv):
    me = Place()
    c, y, z, xh, xl = me.core, me.y, me.z, me.x_hi, me.x_lo
    zu, zd, zf = (z + 1) % 4, (z + 3) % 4, (z + 2) % 4
    width = 512
    strips, kept = [], []
    for p in range(4):
        for k in range(3):
            strips.append(pltpu.make_async_copy(
                w_hbm.at[:, at((2 * k + c) * width + p * 128, 128)],
                w.at[at(me.fsdp * 128, 128), pl.ds((3 * p + k) * 128, 128)], local.at[3 * p + k]))
    for s in range(2):
        kept.append(pltpu.make_async_copy(lat_hbm.at[s], lat.at[s, at((3 + c) * TOK, TOK)], local.at[12 + s]))
        kept.append(pltpu.make_async_copy(g_hbm.at[s, :, at(c * width, width)], g.at[s, at(c * TOK, TOK)], local.at[14 + s]))
    for copy in strips + kept:
        copy.start()
    chip = me.view // 2
    chips = [{"view": 2 * ((chip + d) % 8) + c, "fsdp": me.fsdp} for d in range(8)]
    others = [{"view": 2 * ((chip + d) % 8) + 1 - c, "fsdp": me.fsdp} for d in range(8)]
    greet((*chips[1:], *others, me.z_up, me.z_down, me.outer))

    def weight(link):
        return jnp.where(link > 0, 0.0, -1e30).astype(F32)

    a = me.view - c

    def cyc(v):
        return weight(cycle_ref[(v + 16) % 16])

    bias = [
        [weight(cross_ref[a % 8]), cyc(a - 2), 0.0, 0.0, 0.0, cyc(a)],
        [cyc(a - 1), 0.0, 0.0, 0.0, cyc(a + 1), weight(cross_ref[(a + 1) % 8])],
    ]
    first, last = y == 0, y == 3
    edge = jnp.logical_or(first, last)
    keep_down = jnp.where(first, 0.0, 1.0)
    keep_up = jnp.where(last, 0.0, 1.0)

    def mail(src, dst, send, recv, to):
        return pltpu.make_async_remote_copy(
            src_ref=src, dst_ref=dst, send_sem=send, recv_sem=recv, device_id=to, device_id_type=MESH)

    def up(t, i):
        return mail(out.at[t % SLOTS, 1, i], inbox.at[t, 1, i], tsend.at[i, t % SLOTS], trecv.at[i, t], me.up)

    def down(t, i):
        return mail(out.at[t % SLOTS, 0, i], inbox.at[t, 0, i], tsend.at[2 + i, t % SLOTS], trecv.at[2 + i, t], me.down)

    def across(t, i):
        return mail(out.at[t % SLOTS, 2, i], inbox.at[t, 2, i], tsend.at[4 + i, t % SLOTS], trecv.at[4 + i, t], me.pair)

    def columns(t):
        return at(c * width + sample_and_pair(t)[1] * 128, 128)

    def att_mate(t):
        return mail(att.at[t % SLOTS, at((1 - c) * TOK, TOK)], att_full.at[sample_and_pair(t)[0], :, columns(t)],
                    tsend.at[6, t % SLOTS], trecv.at[6, t], me.mate)

    def att_own(t):
        return pltpu.make_async_copy(
            att.at[t % SLOTS, at(c * TOK, TOK)], att_full.at[sample_and_pair(t)[0], :, columns(t)], tsend.at[7, t % SLOTS])

    def red(kind, p, src, dst, to):
        i = KINDS.index(kind)
        return mail(src, dst, rsend.at[i, p], rrecv.at[i, p], to)

    lo, hi, top, low = pl.ds(0, 32), pl.ds(32, 32), pl.ds(0, 64), pl.ds(64, 64)
    def a1u(p):
        return red("a1u", p, dwb.at[p, :, zf, lo], z1u.at[p], me.z_up)

    def a1d(p):
        return red("a1d", p, dwb.at[p, :, zf, hi], z1d.at[p], me.z_down)

    def bx(p):
        return red("bx", p, dwb.at[p, 1 - xh, :, low], xain.at[p], me.outer)

    def a2u(p):
        return red("a2u", p, su.at[p], z2u.at[p], me.z_up)

    def a2d(p):
        return red("a2d", p, sd.at[p], z2d.at[p], me.z_down)

    def b1u(p):
        return red("b1u", p, xa.at[p, zf, lo], q1u.at[p], me.z_up)

    def b1d(p):
        return red("b1d", p, xa.at[p, zf, hi], q1d.at[p], me.z_down)

    def ax(p):
        return red("ax", p, zs.at[p, 1 - xh], xin.at[p], me.outer)

    def b2u(p):
        return red("b2u", p, qsu.at[p], q2u.at[p], me.z_up)

    def b2d(p):
        return red("b2d", p, qsd.at[p], q2d.at[p], me.z_down)

    def scatter(group):
        return [mail(whole.at[pl.ds(2 * group, 2), at(((chip + d) % 8) * 16, 16)], parts.at[group, d - 1],
                     vsend.at[group, d - 1], vrecv.at[group, d - 1], chips[d]) for d in range(1, 8)]

    def spread(group):
        rows = at(chip * 16, 16)
        return [mail(fin.at[group], fing.at[c, pl.ds(2 * group, 2), rows], vsend.at[group, 7 + i], vrecv.at[group, 7 + i], to)
                for i, to in enumerate((*chips[1:], *others))]

    def f32(x):
        return x.astype(F32)

    def weight_grad(t):
        slot = t % SLOTS
        p = sample_and_pair(t)[1]

        def share(b):
            if b in (3, 4):
                part = own[slot, :, :, (b - 3) * TOK:(b - 2) * TOK].astype(BF)
            else:
                n, w = {0: (2, 0), 1: (0, 0), 2: (0, 1), 5: (1, 0), 6: (1, 1), 7: (2, 1)}[b]
                part = out[slot, n, :, :, w * TOK:(w + 1) * TOK]
            return part.reshape(256, TOK)

        mine = pl.ds(3 * TOK, 2 * TOK)
        queries = gp[p, pl.ds(512, 512), :128].astype(F32).T.astype(BF)
        sums = gp[p, pl.ds(0, 512), :].astype(F32).T.astype(BF)
        for f in range(4):
            cols = slice(f * 256, (f + 1) * 256)
            earlier = dot(sums, lat[0, mine, cols])
            total = earlier[128:]
            for b in range(8):
                total = total + dot(share(b), lat[1, pl.ds(b * TOK, TOK), cols])
            for k in range(2):
                half = slice(k * 128, (k + 1) * 128)
                block = dwb.at[p, f // 2, 2 * (f % 2) + k]
                block[:, :128] = (earlier[:128, half] + dot(queries, lat[1, mine, f * 256 + k * 128:f * 256 + (k + 1) * 128])).T.astype(BF)
                block[:, 128:] = total[:, half].T.astype(BF)

    def phase1(p):
        for make in (a1u, a1d, bx):
            make(p).start()

    def phase2(p):
        a1u(p).wait_recv()
        a1d(p).wait_recv()
        su[p, :, lo] = (f32(dwb[p, :, zu, lo]) + f32(z1u[p])).astype(BF)
        su[p, :, hi] = dwb[p, :, zu, hi]
        sd[p, :, lo] = dwb[p, :, zd, lo]
        sd[p, :, hi] = (f32(dwb[p, :, zd, hi]) + f32(z1d[p])).astype(BF)
        a2u(p).start()
        a2d(p).start()
        bx(p).wait_recv()
        xa[p] = (f32(dwb[p, xh, :, low]) + f32(xain[p])).astype(BF)
        b1u(p).start()
        b1d(p).start()

    def phase3(p):
        b1u(p).wait_recv()
        b1d(p).wait_recv()
        qsu[p, lo] = (f32(xa[p, zu, lo]) + f32(q1u[p])).astype(BF)
        qsu[p, hi] = xa[p, zu, hi]
        qsd[p, lo] = xa[p, zd, lo]
        qsd[p, hi] = (f32(xa[p, zd, hi]) + f32(q1d[p])).astype(BF)
        b2u(p).start()
        b2d(p).start()
        a2u(p).wait_recv()
        a2d(p).wait_recv()
        zs[p] = (f32(dwb[p, :, z, top]) + f32(z2u[p]) + f32(z2d[p])).astype(BF)
        ax(p).start()

    def phase4(p):
        b2u(p).wait_recv()
        b2d(p).wait_recv()
        whole[p, low] = (f32(xa[p, z]) + f32(q2u[p]) + f32(q2d[p])).astype(BF)
        ax(p).wait_recv()
        whole[p, top] = (f32(zs[p, xh]) + f32(xin[p])).astype(BF)
        if p % 2:
            for copy in scatter(p // 2):
                copy.start()

    def phase5(p):
        if p % 2:
            group = p // 2
            total = f32(whole[2 * group:2 * group + 2, at(chip * 16, 16)])
            for d, copy in enumerate(scatter(group)):
                copy.wait_recv()
                total = total + f32(parts[group, d])
            fin[group] = total.astype(BF)
            fing[c, 2 * group:2 * group + 2, at(chip * 16, 16)] = total.astype(BF)
            for copy in spread(group):
                copy.start()


    def gather_grads(t):
        across(t, 0).wait_recv()
        across(t, 1).wait_recv()
        s, p = sample_and_pair(t)
        for i in range(2):
            total = own[t % SLOTS, i] + f32(inbox[t, 2, i]) + f32(inbox[t, 1, i]) * keep_down + f32(inbox[t, 0, i]) * keep_up
            gp[p, at(s * 512, 512), (1 + i) * 128:(2 + i) * 128] = total.T.astype(BF)

    def join(u, i):
        up(u, i).wait_recv()
        down(u, i).wait_recv()

        @pl.when(first)
        def _():
            out[u % SLOTS, 2, i] = (f32(out[u % SLOTS, 2, i]) + f32(inbox[u, 1, i])).astype(BF)

        @pl.when(last)
        def _():
            out[u % SLOTS, 2, i] = (f32(out[u % SLOTS, 2, i]) + f32(inbox[u, 0, i])).astype(BF)

        pl.when(edge)(across(u, i).start)

    def service(t):
        def joins(first_step, count=1):
            for u in range(count):
                join(first_step + u, 0)
                join(first_step + u, 1)

        pl.when(both(t >= 2, t <= 4))(lambda: joins(t - 2))
        pl.when(t == 4)(lambda: joins(3))
        pl.when(t >= 5)(lambda: joins(t - 1))

        pl.when(t == 6)(lambda: phase2(0))
        pl.when(t == 7)(lambda: phase2(1))
        pl.when(t == 7)(lambda: phase3(0))

        pl.when(both(t >= 3, t <= 5))(lambda: gather_grads(t - 3))
        pl.when(t == 5)(lambda: gather_grads(3))
        pl.when(t >= 6)(lambda: gather_grads(t - 2))

    sent = []
    slots = iter(range(64))

    def post(src, dst, to, own=None):
        i = next(slots)
        made = mail(src, dst, gsend.at[i], grecv.at[i], to)
        sent.append(made)
        return made if own is None else (made, mail(own, dst, gsend.at[i], grecv.at[i], to))

    def rows_at(s, b, start=0, size=TOK):
        return lat.at[s, at(b * TOK + start, size)]

    def w_at(f, group, start=0, size=128):
        return w.at[at(f * 128 + start, size), pl.ds(1152, 384) if group else pl.ds(0, 1152)]

    cuts = {0: [(i * 64, 64) for i in range(4)], 1: [(0, TOK // 2), (TOK // 2, TOK // 2)]}
    to_pair, to_up, to_down, to_mate, relays, g_mate = {}, {}, {}, {}, {}, []
    for s in range(2):
        to_pair[s] = [post(lat_hbm.at[s, pl.ds(*cut)], rows_at(s, 7 * c, *cut), me.pair) for cut in cuts[s]]
        to_up[s] = [post(rows_at(s, 7 * c, *cut), rows_at(s, 1 + c, *cut), me.up, lat_hbm.at[s, pl.ds(*cut)]) for cut in cuts[s]]
        to_down[s] = [post(rows_at(s, 7 * c, *cut), rows_at(s, 5 + c, *cut), me.down, lat_hbm.at[s, pl.ds(*cut)]) for cut in cuts[s]]
        to_mate[s] = post(lat_hbm.at[s], rows_at(s, 3 + c), me.mate)
        relays[s] = [post(rows_at(s, b), rows_at(s, b), me.mate) for b in (7 * c, 1 + c, 5 + c)]
        g_mate.append(post(g_hbm.at[s, :, at((1 - c) * width, width)], g.at[s, at(c * TOK, TOK)], me.mate))
    f0, f_up, f_down, f_out, far = me.fsdp, me.f_up, me.f_down, me.f_outer, me.f_far
    w_mail = [dict(
        up=post(w_at(f0, grp), w_at(f0, grp), me.z_up),
        down=post(w_at(f0, grp), w_at(f0, grp), me.z_down),
        out=post(w_at(f0, grp), w_at(f0, grp), me.outer),
        up2=post(w_at(f_down, grp, 0, 64), w_at(f_down, grp, 0, 64), me.z_up),
        down2=post(w_at(f_up, grp, 64, 64), w_at(f_up, grp, 64, 64), me.z_down),
        out_up=post(w_at(f_out, grp), w_at(f_out, grp), me.z_up),
        out_down=post(w_at(f_out, grp), w_at(f_out, grp), me.z_down),
        far0=post(w_at(far, grp, 0, 64), w_at(far, grp, 0, 64), me.outer),
        far1=post(w_at(far, grp, 64, 64), w_at(far, grp, 64, 64), me.outer),
    ) for grp in range(2)]

    def w_first(grp):
        for copy in strips[9:] if grp else strips[:9]:
            copy.wait()
        for name in ("up", "down", "out"):
            w_mail[grp][name].start()

    def w_second(grp):
        m = w_mail[grp]
        m["up"].wait_recv()
        m["up2"].start()
        m["down"].wait_recv()
        m["down2"].start()
        m["out"].wait_recv()
        m["out_up"].start()
        m["out_down"].start()

    def w_third(grp):
        m = w_mail[grp]
        m["up2"].wait_recv()
        m["far0"].start()
        m["down2"].wait_recv()
        m["far1"].start()

    def w_last(grp):
        for name in ("out_up", "out_down", "far0", "far1"):
            w_mail[grp][name].wait_recv()

    def lat_first(s):
        for i in range(len(cuts[s])):
            pl.when(jnp.logical_not(last))(to_up[s][i][1].start)
            pl.when(jnp.logical_not(first))(to_down[s][i][1].start)
        to_mate[s].start()
        g_mate[s].start()

    def lat_wrap(s, i):
        to_pair[s][i].wait_recv()
        pl.when(last)(to_up[s][i][0].start)
        pl.when(first)(to_down[s][i][0].start)

    def lat_relay(s):
        for i in range(len(cuts[s])):
            to_up[s][i][0].wait_recv()
        relays[s][1].start()
        for i in range(len(cuts[s])):
            to_down[s][i][0].wait_recv()
        relays[s][2].start()

    def lat_last(s):
        for copy in (to_mate[s], g_mate[s], *relays[s]):
            copy.wait_recv()

    chunks = len(cuts[0])
    to_pair[0][0].start()
    to_pair[0][1].start()
    w_first(0)
    lat_first(0)
    for i in range(chunks):
        to_pair[0][i].wait_send()
        if i + 2 < chunks:
            to_pair[0][i + 2].start()
        lat_wrap(0, i)
        if i == 1:
            w_second(0)
            to_pair[1][0].start()
        if i == 2:
            w_third(0)
    relays[0][0].start()
    to_pair[1][1].start()
    w_first(1)
    lat_relay(0)
    lat_first(1)
    w_second(1)
    w_last(0)
    for copy in kept:
        copy.wait()
    lat_last(0)
    lat_wrap(1, 0)

    def projected(t, slot):
        for _ in project(lat, w, *sample_and_pair(t), k_s.at[slot], v_s.at[slot], q_s.at[slot]):
            pass

    projected(0, 0)

    def step(t, carry):
        s, p = sample_and_pair(t)

        @pl.when(t == 2)
        def _():
            w_last(1)

        @pl.when(t == 4)
        def _():
            lat_last(1)
            projected(4, 0)

        @pl.when(t >= SLOTS)
        def _():
            u = t - SLOTS
            for i in range(2):
                up(u, i).wait_send()
                down(u, i).wait_send()
                across(u, i).wait_send()
            att_mate(u).wait_send()
            att_own(u).wait()

        now, later = t % 2, (t + 1) % 2
        s_next, p_next = sample_and_pair(jnp.where(t == 3, 3, jnp.minimum(t + 1, STEPS - 1)))
        beside = project(lat, w, s_next, p_next, k_s.at[later], v_s.at[later], q_s.at[later])
        attend(bias, s, p, g, k_s.at[now], v_s.at[now], q_s.at[now], st, pb, gs, att.at[t % SLOTS],
               gp.at[p, at(s * 512, 512), pl.ds(0, 128)], own.at[t % SLOTS], out.at[t % SLOTS], [(4, 2, beside)])
        def send(i):
            up(t, i).start()
            down(t, i).start()
            pl.when(jnp.logical_not(edge))(across(t, i).start)

        send(0)
        att_mate(t).start()
        att_own(t).start()

        @pl.when(t >= 4)
        def _():
            weight_grad(t)
            phase1(t - 4)

        send(1)

        @pl.when(t == 0)
        def _():
            lat_wrap(1, 1)
            relays[1][0].start()
            w_third(1)

        @pl.when(t == 2)
        def _():
            lat_relay(1)

        service(t)
        return carry

    lax.fori_loop(0, STEPS, step, 0)

    def latent_grad(pairs):
        for n in range(4):
            for r in range(4):
                rows = pl.ds(r * 256, 256)
                total = None if pairs[0] == 0 else st[n // 2, n % 2, rows, :]
                for p in pairs:
                    part = dot(gp[p, rows, :], w[pl.ds(n * 256, 256), p * 384:(p + 1) * 384], NT)
                    total = part if total is None else total + part
                st[n // 2, n % 2, rows, :] = total

    def dl_mate():
        return mail(dl_out_s, dl_in, dsend.at[0], drecv.at[0], me.mate)

    def finish(group):
        for copy in spread(group):
            copy.wait_recv()
        for p in (2 * group, 2 * group + 1):
            for core in range(2):
                for k in range(3):
                    first_column = (2 * k + core) * width + p * 128
                    dw_out[:, first_column:first_column + 128] = f32(fing[core, p, :, k * 128:(k + 1) * 128])

    end = STEPS - 1
    join(end, 0)
    phase2(2)
    phase3(1)
    phase4(0)
    latent_grad((0,))
    join(end, 1)
    phase2(3)
    phase3(2)
    phase4(1)
    gather_grads(end - 1)
    latent_grad((1,))
    phase3(3)
    phase4(2)
    phase5(1)
    latent_grad((2,))
    phase4(3)
    gather_grads(end)
    latent_grad((3,))
    for s in range(2):
        for n in range(4):
            dl_out_s[s, :, n * 256:(n + 1) * 256] = st[n // 2, n % 2, at(s * 512 + (1 - c) * TOK, TOK), :].astype(BF)
    dl_mate().start()
    phase5(3)
    finish(0)
    dl_mate().wait_recv()
    for s in range(2):
        for n in range(4):
            cols = slice(n * 256, (n + 1) * 256)
            dl_out[s, :, cols] = (st[n // 2, n % 2, at(s * 512 + c * TOK, TOK), :] + f32(dl_in[s, :, cols])).astype(BF)
    finish(1)
    for t in range(STEPS - SLOTS, STEPS):
        for make in (up, down, across):
            make(t, 0).wait_send()
            make(t, 1).wait_send()
        att_mate(t).wait_send()
        att_own(t).wait()
    for t in range(STEPS):
        att_mate(t).wait_recv()
    dl_mate().wait_send()
    for p in range(4):
        for make in (a1u, a1d, bx, a2u, a2d, b1u, b1d, ax, b2u, b2d):
            make(p).wait_send()
    for group in range(2):
        for copy in scatter(group) + spread(group):
            copy.wait_send()
    for i, copy in enumerate(sent):
        if i >= chunks:
            copy.wait_send()


def hand_over_kernel(*refs):
    ins, outs, held, sems = refs[:3], refs[3:6], refs[6:9], refs[9]
    loads = [pltpu.make_async_copy(ins[i], held[i], sems.at[0, i]) for i in range(3)]
    stores = [pltpu.make_async_copy(held[i], outs[i], sems.at[1, i]) for i in range(3)]
    for load in loads:
        load.start()
    for load, store in zip(loads, stores):
        load.wait()
        store.start()
    for store in stores:
        store.wait()


def hand_over(arrays):
    ANY = pl.BlockSpec(memory_space=pl.ANY)
    return pl.pallas_call(
        hand_over_kernel,
        in_specs=[ANY] * 3,
        out_specs=[ANY] * 3,
        out_shape=[jax.ShapeDtypeStruct(a.shape, a.dtype) for a in arrays],
        scratch_shapes=[*[pltpu.VMEM(a.shape, a.dtype) for a in arrays], pltpu.SemaphoreType.DMA((2, 3))],
        compiler_params=pltpu.CompilerParams(vmem_limit_bytes=VMEM_LIMIT),
    )(*arrays)


def local(latents, w_qkv, cycle_links, cross_links, d_attended):
    _, _, samples, toks, model = latents.shape
    rows, wide = w_qkv.shape
    half = model // 2
    ANY = pl.BlockSpec(memory_space=pl.ANY)
    VM = pl.BlockSpec(memory_space=pltpu.VMEM)
    SM = pl.BlockSpec(memory_space=pltpu.SMEM)
    def vm(*shape, dtype=BF):
        return pltpu.VMEM(shape, dtype)

    W = 384
    att_full, dw_out, dl_out = pl.pallas_call(
        main_kernel,
        in_specs=[SM, SM, ANY, ANY, ANY],
        out_specs=[VM, VM, VM],
        out_shape=[
            jax.ShapeDtypeStruct((samples, toks, model), BF),
            jax.ShapeDtypeStruct((rows, wide), F32),
            jax.ShapeDtypeStruct((samples, toks, model), BF),
        ],
        scratch_shapes=[
            vm(samples, 8 * toks, model), vm(model, wide // 2), vm(samples, 2 * toks, half),
            vm(2, 8 * toks, 128), vm(2, 8 * toks, 128), vm(2, 2 * toks, 128),
            vm(2, 2, 6 * toks, toks, dtype=F32), vm(2, 6 * toks, 2 * toks), vm(2, 6 * toks, 2 * toks),
            vm(SLOTS, 2 * toks, 128), vm(SLOTS, 2, 128, 2 * toks, dtype=F32),
            vm(SLOTS, 3, 2, 128, 2 * toks), vm(STEPS, 3, 2, 128, 2 * toks),
            vm(4, samples * 2 * toks, W), vm(4, 2, 4, rows, W),
            vm(samples, toks, model), vm(samples, toks, model),
            vm(4, 2, 32, W), vm(4, 2, 32, W),
            vm(4, 2, 64, W), vm(4, 2, 64, W), vm(4, 2, 64, W), vm(4, 2, 64, W), vm(4, 2, 64, W),
            vm(4, 64, W), vm(4, 4, 64, W), vm(4, 4, 64, W),
            vm(4, 32, W), vm(4, 32, W),
            vm(4, 64, W), vm(4, 64, W), vm(4, 64, W), vm(4, 64, W),
            vm(4, rows, W), vm(2, 7, 2, 16, W), vm(2, 2, 16, W), vm(2, 4, rows, W),
            pltpu.SemaphoreType.DMA((16,)),
            pltpu.SemaphoreType.DMA((8, SLOTS)), pltpu.SemaphoreType.DMA((7, STEPS)),
            pltpu.SemaphoreType.DMA((len(KINDS), 4)), pltpu.SemaphoreType.DMA((len(KINDS), 4)),
            pltpu.SemaphoreType.DMA((2, 22)), pltpu.SemaphoreType.DMA((2, 22)),
            pltpu.SemaphoreType.DMA((1,)), pltpu.SemaphoreType.DMA((1,)),
            pltpu.SemaphoreType.DMA((64,)), pltpu.SemaphoreType.DMA((64,)),
        ],
        compiler_params=pltpu.CompilerParams(collective_id=0, has_side_effects=True, vmem_limit_bytes=63 * 2**20),
    )(cycle_links[0], cross_links[0], latents[0, 0], w_qkv, d_attended[0, 0])
    att_full, dl_out, dw_out = hand_over((att_full, dl_out, dw_out))
    return att_full[None, None], dl_out[None, None], dw_out


def solution(mesh):
    wide = P("fsdp", "view", None, None, None)
    rows = P("fsdp", None)
    return jax.shard_map(
        local,
        mesh=mesh,
        in_specs=(wide, rows, rows, rows, wide),
        out_specs=(wide, wide, rows),
        check_vma=False,
    )
```

```python
import functools

import jax
import jax.numpy as jnp
from jax import lax
from jax.experimental import pallas as pl
from jax.experimental.pallas import tpu as pltpu
from jax.sharding import PartitionSpec as P

BF, F32 = jnp.bfloat16, jnp.float32
MESH = pl.DeviceIdType.MESH
TOK = 256
LOG2E = 1.4426950408889634
SCALE = 0.125
NT = (((1,), (1,)), ((), ()))
NN = (((1,), (0,)), ((), ()))
TN = (((0,), (0,)), ((), ()))
VMEM_LIMIT = 60 * 2**20


class Place:
    def __init__(self):
        v, f = lax.axis_index("view"), lax.axis_index("fsdp")
        self.view, self.fsdp = v, f
        self.ys, self.zs = 4, 4
        self.core = v % 2
        self.y = (v // 2) % 4
        self.x_lo = v // 8
        self.z = f % 4
        self.x_hi = f // 4
        column = self.x_lo * 8 + self.core

        def at(view, fsdp):
            return {"view": view, "fsdp": fsdp}

        self.up = at(column + 2 * ((self.y + 1) % 4), f)
        self.down = at(column + 2 * ((self.y + 3) % 4), f)
        self.over = at(column + 2 * ((self.y + 2) % 4), f)
        self.pair = at((v + 8) % 16, f)
        self.mate = at(v + 1 - 2 * self.core, f)
        self.f_up = self.x_hi * 4 + (self.z + 1) % 4
        self.f_down = self.x_hi * 4 + (self.z + 3) % 4
        self.f_far = self.x_hi * 4 + (self.z + 2) % 4
        self.f_outer = (f + 4) % 8
        self.z_up = at(v, self.f_up)
        self.z_down = at(v, self.f_down)
        self.outer = at((v + 8) % 16, self.f_outer)


def greet(devices):
    barrier = pltpu.get_barrier_semaphore()
    for device in devices:
        pl.semaphore_signal(barrier, inc=1, device_id=device, device_id_type=MESH)
    pl.semaphore_wait(barrier, len(devices))


class Mail:
    def __init__(self, send, recv):
        self.send, self.recv, self.made, self.sent = send, recv, 0, []

    def copy(self, src, dst, to):
        i = self.made
        self.made += 1
        made = self.again(i, src, dst, to)
        self.sent.append(made)
        return made

    def again(self, i, src, dst, to):
        return pltpu.make_async_remote_copy(
            src_ref=src, dst_ref=dst, send_sem=self.send.at[i], recv_sem=self.recv.at[i],
            device_id=to, device_id_type=MESH)

    def finish(self):
        for copy in self.sent:
            copy.wait_send()


def at(start, size):
    return pl.ds(pl.multiple_of(start, size), size)


def dot(a, b, dims=NN):
    return lax.dot_general(a, b, dims, preferred_element_type=F32)


def when(condition):
    if isinstance(condition, bool):
        return (lambda f: f()) if condition else (lambda f: None)
    return pl.when(condition)


def both(*conditions):
    if any(isinstance(x, bool) and not x for x in conditions):
        return False
    conditions = [x for x in conditions if not isinstance(x, bool)]
    return functools.reduce(jnp.logical_and, conditions) if conditions else True


def head_pass(view, h, bias, qt, gt, k_rows, v_rows, kt, vt, st, pb, gs, att_t, dq_t, own, term):
    head = slice(h * 64, (h + 1) * 64)
    row = lax.broadcasted_iota(jnp.int32, (128, 1), 0)
    mine = (row >= 64) if h else (row < 64)
    qm = jnp.where(mine, qt, jnp.zeros_like(qt)).astype(BF)
    gm = jnp.where(mine, gt, jnp.zeros_like(gt)).astype(BF)
    cols = slice(h * TOK, (h + 1) * TOK)
    blocks = [pl.ds(j * TOK, TOK) for j in range(6)]
    tops = []
    for j in range(0, 6, SPAN):
        s = dot(k_rows(j, SPAN), qm)
        for i in range(SPAN):
            part = s[i * TOK:(i + 1) * TOK]
            st[h, blocks[j + i], :] = part
            tops.append(jnp.max(part, axis=0, keepdims=True) * (SCALE * LOG2E) + bias[j + i])
            yield
    top = functools.reduce(jnp.maximum, tops)
    total = jnp.zeros((1, TOK), F32)
    for j, rows in enumerate(blocks):
        e = jnp.exp2(st[h, rows, :] * (SCALE * LOG2E) - (top - bias[j]))
        st[h, rows, :] = e
        total = total + jnp.sum(e, axis=0, keepdims=True)
        yield
    inv = 1.0 / total
    for rows in blocks:
        pb[rows, cols] = (st[h, rows, :] * inv).astype(BF)
        yield
    ot = dot(vt()[head], pb[:, cols])
    att_t[h] = ot
    delta = jnp.sum(gt[head] * ot, axis=0, keepdims=True)
    yield
    for j in range(0, 6, SPAN):
        d = dot(v_rows(j, SPAN), gm)
        for i in range(SPAN):
            part = d[i * TOK:(i + 1) * TOK]
            gs[blocks[j + i], cols] = (st[h, blocks[j + i], :] * inv * (part - delta)).astype(BF)
            yield
    dq_t[h] = dot(kt()[head], gs[:, cols]) * SCALE
    yield
    q_head, g_head = qt[head].astype(BF), gt[head].astype(BF)
    for j, rows in enumerate(blocks):
        b = j + 2 * view
        grads = dot(q_head, gs[rows, cols], NT) * SCALE, dot(g_head, pb[rows, cols], NT)
        for i, grad in enumerate(grads):
            if b in (3, 4):
                w = pl.ds((b - 3) * TOK, TOK)
                grad = grad if b - 3 == view else grad.astype(BF).astype(F32)
                own[i, head, w] = grad if view == 0 else own[i, head, w] + grad
            else:
                n, w = {0: (2, 0), 1: (0, 0), 2: (0, 1), 5: (1, 0), 6: (1, 1), 7: (2, 1)}[b]
                w = pl.ds(w * TOK, TOK)
                grad = grad.astype(BF)
                if b in (2, 5) and view == 1:
                    grad = (term[n, i, head, w].astype(F32) + grad.astype(F32)).astype(BF)
                term[n, i, head, w] = grad
        yield


def project(lat, w, s, p, k_s, v_s, q_s):
    span = PROJECT_ROWS
    first, count = 3 * lat.shape[1] // 8, lat.shape[1] // 4
    w_kv = w[:, pl.ds(pl.multiple_of(p * 384 + 128, 128), 256)]
    for r in range(lat.shape[1] // span):
        rows = pl.ds(r * span, span)
        kv = dot(lat[s, rows, :], w_kv).astype(BF)
        k_s[rows, :] = kv[:, :128]
        v_s[rows, :] = kv[:, 128:]
        yield
    q_s[...] = dot(lat[s, pl.ds(first, count), :], w[:, at(p * 384, 128)]).astype(BF)
    yield


def weave(threads):
    threads = list(threads)
    tick = 0
    while threads:
        for thread in list(threads):
            start, every, work = thread
            if tick >= start and (tick - start) % every == 0:
                try:
                    next(work)
                except StopIteration:
                    threads.remove(thread)
        tick += 1


def attend(bias, s, p, g_ref, k_s, v_s, q_s, st, pb, gs, att, dq, own, term, beside=()):
    kt = k_s[...].T
    vt = v_s[...].T
    threads = list(beside)
    results = []
    for view in range(2):
        rows = pl.ds(view * TOK, TOK)
        q = q_s[rows, :]
        g = g_ref[s, rows, at(p * 128, 128)]
        gt = g.astype(F32).T
        span = slice(2 * view * TOK, (2 * view + 6) * TOK)

        qt = q.astype(F32).T

        def rows_of(ref, view=view):
            return lambda j, n: ref[pl.ds((2 * view + j) * TOK, n * TOK), :]

        att_t, dq_t = {}, {}
        results.append((rows, att_t, dq_t))
        for h in range(2):
            threads.append((OFFSET * (2 * view + h), 1, head_pass(
                view, h, bias[view], qt, gt, rows_of(k_s), rows_of(v_s), lambda span=span: kt[:, span],
                lambda span=span: vt[:, span], st.at[view], pb.at[view], gs.at[view], att_t, dq_t, own, term)))
    weave(threads)
    for rows, att_t, dq_t in results:
        att[rows, :] = jnp.concatenate([att_t[0], att_t[1]], axis=0).T.astype(BF)
        dq[rows, :] = jnp.concatenate([dq_t[0], dq_t[1]], axis=0).T.astype(BF)


OFFSET, SPAN, PROJECT_ROWS = 10, 1, 512
STEPS, SLOTS = 8, 4
KINDS = ("a1u", "a1d", "bx", "a2u", "a2d", "b1u", "b1d", "ax", "b2u", "b2d")


def sample_and_pair(t):
    return t // 4, t % 4


def main_kernel(cycle_ref, cross_ref, lat_hbm, w_hbm, g_hbm, att_full, dw_out, dl_out,
                lat, w, g, k_s, v_s, q_s, st, pb, gs, att, own, out, inbox, gp, dwb, dl_out_s, dl_in,
                z1u, z1d, z2u, z2d, su, sd, zs, xin, xain, xa, q1u, q1d, q2u, q2d, qsu, qsd,
                whole, parts, fin, fing,
                local, tsend, trecv, rsend, rrecv, vsend, vrecv, dsend, drecv, gsend, grecv):
    me = Place()
    c, y, z, xh, xl = me.core, me.y, me.z, me.x_hi, me.x_lo
    zu, zd, zf = (z + 1) % 4, (z + 3) % 4, (z + 2) % 4
    width = 512
    strips, kept = [], []
    for p in range(4):
        for k in range(3):
            strips.append(pltpu.make_async_copy(
                w_hbm.at[:, at((2 * k + c) * width + p * 128, 128)],
                w.at[at(me.fsdp * 128, 128), pl.ds((3 * p + k) * 128, 128)], local.at[3 * p + k]))
    for s in range(2):
        kept.append(pltpu.make_async_copy(lat_hbm.at[s], lat.at[s, at((3 + c) * TOK, TOK)], local.at[12 + s]))
        kept.append(pltpu.make_async_copy(g_hbm.at[s, :, at(c * width, width)], g.at[s, at(c * TOK, TOK)], local.at[14 + s]))
    for copy in strips + kept:
        copy.start()
    chip = me.view // 2
    chips = [{"view": 2 * ((chip + d) % 8) + c, "fsdp": me.fsdp} for d in range(8)]
    others = [{"view": 2 * ((chip + d) % 8) + 1 - c, "fsdp": me.fsdp} for d in range(8)]
    greet((*chips[1:], *others, me.z_up, me.z_down, me.outer))

    def weight(link):
        return jnp.where(link > 0, 0.0, -1e30).astype(F32)

    a = me.view - c

    def cyc(v):
        return weight(cycle_ref[(v + 16) % 16])

    bias = [
        [weight(cross_ref[a % 8]), cyc(a - 2), 0.0, 0.0, 0.0, cyc(a)],
        [cyc(a - 1), 0.0, 0.0, 0.0, cyc(a + 1), weight(cross_ref[(a + 1) % 8])],
    ]
    first, last = y == 0, y == 3
    edge = jnp.logical_or(first, last)
    keep_down = jnp.where(first, 0.0, 1.0)
    keep_up = jnp.where(last, 0.0, 1.0)

    def mail(src, dst, send, recv, to):
        return pltpu.make_async_remote_copy(
            src_ref=src, dst_ref=dst, send_sem=send, recv_sem=recv, device_id=to, device_id_type=MESH)

    def up(t, i):
        return mail(out.at[t % SLOTS, 1, i], inbox.at[t, 1, i], tsend.at[i, t % SLOTS], trecv.at[i, t], me.up)

    def down(t, i):
        return mail(out.at[t % SLOTS, 0, i], inbox.at[t, 0, i], tsend.at[2 + i, t % SLOTS], trecv.at[2 + i, t], me.down)

    def across(t, i):
        return mail(out.at[t % SLOTS, 2, i], inbox.at[t, 2, i], tsend.at[4 + i, t % SLOTS], trecv.at[4 + i, t], me.pair)

    def columns(t):
        return at(c * width + sample_and_pair(t)[1] * 128, 128)

    def att_mate(t):
        return mail(att.at[t % SLOTS, at((1 - c) * TOK, TOK)], att_full.at[sample_and_pair(t)[0], :, columns(t)],
                    tsend.at[6, t % SLOTS], trecv.at[6, t], me.mate)

    def att_own(t):
        return pltpu.make_async_copy(
            att.at[t % SLOTS, at(c * TOK, TOK)], att_full.at[sample_and_pair(t)[0], :, columns(t)], tsend.at[7, t % SLOTS])

    def red(kind, p, src, dst, to):
        i = KINDS.index(kind)
        return mail(src, dst, rsend.at[i, p], rrecv.at[i, p], to)

    lo, hi, top, low = pl.ds(0, 32), pl.ds(32, 32), pl.ds(0, 64), pl.ds(64, 64)
    def a1u(p):
        return red("a1u", p, dwb.at[p, :, zf, lo], z1u.at[p], me.z_up)

    def a1d(p):
        return red("a1d", p, dwb.at[p, :, zf, hi], z1d.at[p], me.z_down)

    def bx(p):
        return red("bx", p, dwb.at[p, 1 - xh, :, low], xain.at[p], me.outer)

    def a2u(p):
        return red("a2u", p, su.at[p], z2u.at[p], me.z_up)

    def a2d(p):
        return red("a2d", p, sd.at[p], z2d.at[p], me.z_down)

    def b1u(p):
        return red("b1u", p, xa.at[p, zf, lo], q1u.at[p], me.z_up)

    def b1d(p):
        return red("b1d", p, xa.at[p, zf, hi], q1d.at[p], me.z_down)

    def ax(p):
        return red("ax", p, zs.at[p, 1 - xh], xin.at[p], me.outer)

    def b2u(p):
        return red("b2u", p, qsu.at[p], q2u.at[p], me.z_up)

    def b2d(p):
        return red("b2d", p, qsd.at[p], q2d.at[p], me.z_down)

    def scatter(group):
        return [mail(whole.at[pl.ds(2 * group, 2), at(((chip + d) % 8) * 16, 16)], parts.at[group, d - 1],
                     vsend.at[group, d - 1], vrecv.at[group, d - 1], chips[d]) for d in range(1, 8)]

    def spread(group):
        rows = at(chip * 16, 16)
        return [mail(fin.at[group], fing.at[c, pl.ds(2 * group, 2), rows], vsend.at[group, 7 + i], vrecv.at[group, 7 + i], to)
                for i, to in enumerate((*chips[1:], *others))]

    def f32(x):
        return x.astype(F32)

    def weight_grad(t):
        slot = t % SLOTS
        p = sample_and_pair(t)[1]

        def share(b):
            if b in (3, 4):
                part = own[slot, :, :, (b - 3) * TOK:(b - 2) * TOK].astype(BF)
            else:
                n, w = {0: (2, 0), 1: (0, 0), 2: (0, 1), 5: (1, 0), 6: (1, 1), 7: (2, 1)}[b]
                part = out[slot, n, :, :, w * TOK:(w + 1) * TOK]
            return part.reshape(256, TOK)

        mine = pl.ds(3 * TOK, 2 * TOK)
        queries = gp[p, pl.ds(512, 512), :128].astype(F32).T.astype(BF)
        sums = gp[p, pl.ds(0, 512), :].astype(F32).T.astype(BF)
        for f in range(4):
            cols = slice(f * 256, (f + 1) * 256)
            earlier = dot(sums, lat[0, mine, cols])
            total = earlier[128:]
            for b in range(8):
                total = total + dot(share(b), lat[1, pl.ds(b * TOK, TOK), cols])
            for k in range(2):
                half = slice(k * 128, (k + 1) * 128)
                block = dwb.at[p, f // 2, 2 * (f % 2) + k]
                block[:, :128] = (earlier[:128, half] + dot(queries, lat[1, mine, f * 256 + k * 128:f * 256 + (k + 1) * 128])).T.astype(BF)
                block[:, 128:] = total[:, half].T.astype(BF)

    def phase1(p):
        for make in (a1u, a1d, bx):
            make(p).start()

    def phase2(p):
        a1u(p).wait_recv()
        a1d(p).wait_recv()
        su[p, :, lo] = (f32(dwb[p, :, zu, lo]) + f32(z1u[p])).astype(BF)
        su[p, :, hi] = dwb[p, :, zu, hi]
        sd[p, :, lo] = dwb[p, :, zd, lo]
        sd[p, :, hi] = (f32(dwb[p, :, zd, hi]) + f32(z1d[p])).astype(BF)
        a2u(p).start()
        a2d(p).start()
        bx(p).wait_recv()
        xa[p] = (f32(dwb[p, xh, :, low]) + f32(xain[p])).astype(BF)
        b1u(p).start()
        b1d(p).start()

    def phase3(p):
        b1u(p).wait_recv()
        b1d(p).wait_recv()
        qsu[p, lo] = (f32(xa[p, zu, lo]) + f32(q1u[p])).astype(BF)
        qsu[p, hi] = xa[p, zu, hi]
        qsd[p, lo] = xa[p, zd, lo]
        qsd[p, hi] = (f32(xa[p, zd, hi]) + f32(q1d[p])).astype(BF)
        b2u(p).start()
        b2d(p).start()
        a2u(p).wait_recv()
        a2d(p).wait_recv()
        zs[p] = (f32(dwb[p, :, z, top]) + f32(z2u[p]) + f32(z2d[p])).astype(BF)
        ax(p).start()

    def phase4(p):
        b2u(p).wait_recv()
        b2d(p).wait_recv()
        whole[p, low] = (f32(xa[p, z]) + f32(q2u[p]) + f32(q2d[p])).astype(BF)
        ax(p).wait_recv()
        whole[p, top] = (f32(zs[p, xh]) + f32(xin[p])).astype(BF)
        if p % 2:
            copies = scatter(p // 2)
            for i in (5, 1, 2, 4, 6, 0, 3):
                copies[i].start()

    def phase5(p):
        if p % 2:
            group = p // 2
            total = f32(whole[2 * group:2 * group + 2, at(chip * 16, 16)])
            for d, copy in enumerate(scatter(group)):
                copy.wait_recv()
                total = total + f32(parts[group, d])
            fin[group] = total.astype(BF)
            fing[c, 2 * group:2 * group + 2, at(chip * 16, 16)] = total.astype(BF)
            copies = spread(group)
            for i in (5, 13, 1, 9, 2, 10, 4, 12, 6, 14, 0, 8, 3, 11, 7):
                copies[i].start()


    def gather_grads(t):
        across(t, 0).wait_recv()
        across(t, 1).wait_recv()
        s, p = sample_and_pair(t)
        for i in range(2):
            total = own[t % SLOTS, i] + f32(inbox[t, 2, i]) + f32(inbox[t, 1, i]) * keep_down + f32(inbox[t, 0, i]) * keep_up
            gp[p, at(s * 512, 512), (1 + i) * 128:(2 + i) * 128] = total.T.astype(BF)

    def join(u, i):
        up(u, i).wait_recv()
        down(u, i).wait_recv()

        @pl.when(first)
        def _():
            out[u % SLOTS, 2, i] = (f32(out[u % SLOTS, 2, i]) + f32(inbox[u, 1, i])).astype(BF)

        @pl.when(last)
        def _():
            out[u % SLOTS, 2, i] = (f32(out[u % SLOTS, 2, i]) + f32(inbox[u, 0, i])).astype(BF)

        pl.when(edge)(across(u, i).start)

    def service(t):
        def joins(first_step, count=1):
            for u in range(count):
                join(first_step + u, 0)
                join(first_step + u, 1)

        pl.when(both(t >= 2, t <= 4))(lambda: joins(t - 2))
        pl.when(t == 4)(lambda: joins(3))
        pl.when(t >= 5)(lambda: joins(t - 1))

        pl.when(t == 6)(lambda: phase2(0))
        pl.when(t == 7)(lambda: phase2(1))
        pl.when(t == 7)(lambda: phase3(0))

        pl.when(both(t >= 3, t <= 5))(lambda: gather_grads(t - 3))
        pl.when(t == 5)(lambda: gather_grads(3))
        pl.when(t >= 6)(lambda: gather_grads(t - 2))

    sent = []
    slots = iter(range(64))

    def post(src, dst, to, own=None):
        i = next(slots)
        made = mail(src, dst, gsend.at[i], grecv.at[i], to)
        sent.append(made)
        return made if own is None else (made, mail(own, dst, gsend.at[i], grecv.at[i], to))

    def rows_at(s, b, start=0, size=TOK):
        return lat.at[s, at(b * TOK + start, size)]

    def w_at(f, group, start=0, size=128):
        return w.at[at(f * 128 + start, size), pl.ds(1152, 384) if group else pl.ds(0, 1152)]

    cuts = {0: [(i * 64, 64) for i in range(4)], 1: [(0, TOK // 2), (TOK // 2, TOK // 2)]}
    to_pair, to_up, to_down, to_mate, relays, g_mate = {}, {}, {}, {}, {}, []
    for s in range(2):
        to_pair[s] = [post(lat_hbm.at[s, pl.ds(*cut)], rows_at(s, 7 * c, *cut), me.pair) for cut in cuts[s]]
        to_up[s] = [post(rows_at(s, 7 * c, *cut), rows_at(s, 1 + c, *cut), me.up, lat_hbm.at[s, pl.ds(*cut)]) for cut in cuts[s]]
        to_down[s] = [post(rows_at(s, 7 * c, *cut), rows_at(s, 5 + c, *cut), me.down, lat_hbm.at[s, pl.ds(*cut)]) for cut in cuts[s]]
        to_mate[s] = post(lat_hbm.at[s], rows_at(s, 3 + c), me.mate)
        relays[s] = [post(rows_at(s, b), rows_at(s, b), me.mate) for b in (7 * c, 1 + c, 5 + c)]
        g_mate.append(post(g_hbm.at[s, :, at((1 - c) * width, width)], g.at[s, at(c * TOK, TOK)], me.mate))
    f0, f_up, f_down, f_out, far = me.fsdp, me.f_up, me.f_down, me.f_outer, me.f_far
    w_mail = [dict(
        up=post(w_at(f0, grp), w_at(f0, grp), me.z_up),
        down=post(w_at(f0, grp), w_at(f0, grp), me.z_down),
        out=post(w_at(f0, grp), w_at(f0, grp), me.outer),
        up2=post(w_at(f_down, grp, 0, 64), w_at(f_down, grp, 0, 64), me.z_up),
        down2=post(w_at(f_up, grp, 64, 64), w_at(f_up, grp, 64, 64), me.z_down),
        out_up=post(w_at(f_out, grp), w_at(f_out, grp), me.z_up),
        out_down=post(w_at(f_out, grp), w_at(f_out, grp), me.z_down),
        far0=post(w_at(far, grp, 0, 64), w_at(far, grp, 0, 64), me.outer),
        far1=post(w_at(far, grp, 64, 64), w_at(far, grp, 64, 64), me.outer),
    ) for grp in range(2)]

    def w_first(grp):
        for copy in strips[9:] if grp else strips[:9]:
            copy.wait()
        for name in ("up", "down", "out"):
            w_mail[grp][name].start()

    def w_second(grp):
        m = w_mail[grp]
        m["up"].wait_recv()
        m["up2"].start()
        m["down"].wait_recv()
        m["down2"].start()
        m["out"].wait_recv()
        m["out_up"].start()
        m["out_down"].start()

    def w_third(grp):
        m = w_mail[grp]
        m["up2"].wait_recv()
        m["far0"].start()
        m["down2"].wait_recv()
        m["far1"].start()

    def w_last(grp):
        for name in ("out_up", "out_down", "far0", "far1"):
            w_mail[grp][name].wait_recv()

    def lat_first(s):
        for i in range(len(cuts[s])):
            pl.when(jnp.logical_not(last))(to_up[s][i][1].start)
            pl.when(jnp.logical_not(first))(to_down[s][i][1].start)
        to_mate[s].start()
        g_mate[s].start()

    def lat_wrap(s, i):
        to_pair[s][i].wait_recv()
        pl.when(last)(to_up[s][i][0].start)
        pl.when(first)(to_down[s][i][0].start)

    def lat_relay(s):
        for i in range(len(cuts[s])):
            to_up[s][i][0].wait_recv()
        relays[s][1].start()
        for i in range(len(cuts[s])):
            to_down[s][i][0].wait_recv()
        relays[s][2].start()

    def lat_last(s):
        for copy in (to_mate[s], g_mate[s], *relays[s]):
            copy.wait_recv()

    chunks = len(cuts[0])
    to_pair[0][0].start()
    to_pair[0][1].start()
    w_first(0)
    lat_first(0)
    for i in range(chunks):
        to_pair[0][i].wait_send()
        if i + 2 < chunks:
            to_pair[0][i + 2].start()
        lat_wrap(0, i)
        if i == 1:
            w_second(0)
            to_pair[1][0].start()
        if i == 2:
            w_third(0)
    relays[0][0].start()
    to_pair[1][1].start()
    w_first(1)
    lat_relay(0)
    lat_first(1)
    w_second(1)
    w_last(0)
    for copy in kept:
        copy.wait()
    lat_last(0)
    lat_wrap(1, 0)

    def projected(t, slot):
        for _ in project(lat, w, *sample_and_pair(t), k_s.at[slot], v_s.at[slot], q_s.at[slot]):
            pass

    projected(0, 0)

    def step(t, carry):
        s, p = sample_and_pair(t)

        @pl.when(t == 2)
        def _():
            w_last(1)

        @pl.when(t == 4)
        def _():
            lat_last(1)
            projected(4, 0)

        @pl.when(t >= SLOTS)
        def _():
            u = t - SLOTS
            for i in range(2):
                up(u, i).wait_send()
                down(u, i).wait_send()
                across(u, i).wait_send()
            att_mate(u).wait_send()
            att_own(u).wait()

        now, later = t % 2, (t + 1) % 2
        s_next, p_next = sample_and_pair(jnp.where(t == 3, 3, jnp.minimum(t + 1, STEPS - 1)))
        beside = project(lat, w, s_next, p_next, k_s.at[later], v_s.at[later], q_s.at[later])
        attend(bias, s, p, g, k_s.at[now], v_s.at[now], q_s.at[now], st, pb, gs, att.at[t % SLOTS],
               gp.at[p, at(s * 512, 512), pl.ds(0, 128)], own.at[t % SLOTS], out.at[t % SLOTS], [(4, 2, beside)])
        def send(i):
            up(t, i).start()
            down(t, i).start()
            pl.when(jnp.logical_not(edge))(across(t, i).start)

        send(0)
        att_mate(t).start()
        att_own(t).start()

        @pl.when(t >= 4)
        def _():
            weight_grad(t)
            phase1(t - 4)

        send(1)

        @pl.when(t == 0)
        def _():
            lat_wrap(1, 1)
            relays[1][0].start()
            w_third(1)

        @pl.when(t == 2)
        def _():
            lat_relay(1)

        service(t)
        return carry

    lax.fori_loop(0, STEPS, step, 0)

    def latent_grad(pairs):
        for n in range(4):
            for r in range(4):
                rows = pl.ds(r * 256, 256)
                total = None if pairs[0] == 0 else st[n // 2, n % 2, rows, :]
                for p in pairs:
                    part = dot(gp[p, rows, :], w[pl.ds(n * 256, 256), p * 384:(p + 1) * 384], NT)
                    total = part if total is None else total + part
                st[n // 2, n % 2, rows, :] = total

    def dl_mate():
        return mail(dl_out_s, dl_in, dsend.at[0], drecv.at[0], me.mate)

    def finish(group):
        for copy in spread(group):
            copy.wait_recv()
        for p in (2 * group, 2 * group + 1):
            for core in range(2):
                for k in range(3):
                    first_column = (2 * k + core) * width + p * 128
                    dw_out[:, first_column:first_column + 128] = f32(fing[core, p, :, k * 128:(k + 1) * 128])

    end = STEPS - 1
    join(end, 0)
    phase2(2)
    phase3(1)
    phase4(0)
    latent_grad((0,))
    join(end, 1)
    phase2(3)
    phase3(2)
    phase4(1)
    gather_grads(end - 1)
    latent_grad((1,))
    phase3(3)
    phase4(2)
    phase5(1)
    latent_grad((2,))
    phase4(3)
    gather_grads(end)
    latent_grad((3,))
    for s in range(2):
        for n in range(4):
            dl_out_s[s, :, n * 256:(n + 1) * 256] = st[n // 2, n % 2, at(s * 512 + (1 - c) * TOK, TOK), :].astype(BF)
    dl_mate().start()
    phase5(3)
    finish(0)
    dl_mate().wait_recv()
    for s in range(2):
        for n in range(4):
            cols = slice(n * 256, (n + 1) * 256)
            dl_out[s, :, cols] = (st[n // 2, n % 2, at(s * 512 + c * TOK, TOK), :] + f32(dl_in[s, :, cols])).astype(BF)
    finish(1)
    for t in range(STEPS - SLOTS, STEPS):
        for make in (up, down, across):
            make(t, 0).wait_send()
            make(t, 1).wait_send()
        att_mate(t).wait_send()
        att_own(t).wait()
    for t in range(STEPS):
        att_mate(t).wait_recv()
    dl_mate().wait_send()
    for p in range(4):
        for make in (a1u, a1d, bx, a2u, a2d, b1u, b1d, ax, b2u, b2d):
            make(p).wait_send()
    for group in range(2):
        for copy in scatter(group) + spread(group):
            copy.wait_send()
    for i, copy in enumerate(sent):
        if i >= chunks:
            copy.wait_send()


def hand_over_kernel(*refs):
    ins, outs, held, sems = refs[:3], refs[3:6], refs[6:9], refs[9]
    loads = [pltpu.make_async_copy(ins[i], held[i], sems.at[0, i]) for i in range(3)]
    stores = [pltpu.make_async_copy(held[i], outs[i], sems.at[1, i]) for i in range(3)]
    for load in loads:
        load.start()
    for load, store in zip(loads, stores):
        load.wait()
        store.start()
    for store in stores:
        store.wait()


def hand_over(arrays):
    ANY = pl.BlockSpec(memory_space=pl.ANY)
    return pl.pallas_call(
        hand_over_kernel,
        in_specs=[ANY] * 3,
        out_specs=[ANY] * 3,
        out_shape=[jax.ShapeDtypeStruct(a.shape, a.dtype) for a in arrays],
        scratch_shapes=[*[pltpu.VMEM(a.shape, a.dtype) for a in arrays], pltpu.SemaphoreType.DMA((2, 3))],
        compiler_params=pltpu.CompilerParams(vmem_limit_bytes=VMEM_LIMIT),
    )(*arrays)


def local(latents, w_qkv, cycle_links, cross_links, d_attended):
    _, _, samples, toks, model = latents.shape
    rows, wide = w_qkv.shape
    half = model // 2
    ANY = pl.BlockSpec(memory_space=pl.ANY)
    VM = pl.BlockSpec(memory_space=pltpu.VMEM)
    SM = pl.BlockSpec(memory_space=pltpu.SMEM)
    def vm(*shape, dtype=BF):
        return pltpu.VMEM(shape, dtype)

    W = 384
    att_full, dw_out, dl_out = pl.pallas_call(
        main_kernel,
        in_specs=[SM, SM, ANY, ANY, ANY],
        out_specs=[VM, VM, VM],
        out_shape=[
            jax.ShapeDtypeStruct((samples, toks, model), BF),
            jax.ShapeDtypeStruct((rows, wide), F32),
            jax.ShapeDtypeStruct((samples, toks, model), BF),
        ],
        scratch_shapes=[
            vm(samples, 8 * toks, model), vm(model, wide // 2), vm(samples, 2 * toks, half),
            vm(2, 8 * toks, 128), vm(2, 8 * toks, 128), vm(2, 2 * toks, 128),
            vm(2, 2, 6 * toks, toks, dtype=F32), vm(2, 6 * toks, 2 * toks), vm(2, 6 * toks, 2 * toks),
            vm(SLOTS, 2 * toks, 128), vm(SLOTS, 2, 128, 2 * toks, dtype=F32),
            vm(SLOTS, 3, 2, 128, 2 * toks), vm(STEPS, 3, 2, 128, 2 * toks),
            vm(4, samples * 2 * toks, W), vm(4, 2, 4, rows, W),
            vm(samples, toks, model), vm(samples, toks, model),
            vm(4, 2, 32, W), vm(4, 2, 32, W),
            vm(4, 2, 64, W), vm(4, 2, 64, W), vm(4, 2, 64, W), vm(4, 2, 64, W), vm(4, 2, 64, W),
            vm(4, 64, W), vm(4, 4, 64, W), vm(4, 4, 64, W),
            vm(4, 32, W), vm(4, 32, W),
            vm(4, 64, W), vm(4, 64, W), vm(4, 64, W), vm(4, 64, W),
            vm(4, rows, W), vm(2, 7, 2, 16, W), vm(2, 2, 16, W), vm(2, 4, rows, W),
            pltpu.SemaphoreType.DMA((16,)),
            pltpu.SemaphoreType.DMA((8, SLOTS)), pltpu.SemaphoreType.DMA((7, STEPS)),
            pltpu.SemaphoreType.DMA((len(KINDS), 4)), pltpu.SemaphoreType.DMA((len(KINDS), 4)),
            pltpu.SemaphoreType.DMA((2, 22)), pltpu.SemaphoreType.DMA((2, 22)),
            pltpu.SemaphoreType.DMA((1,)), pltpu.SemaphoreType.DMA((1,)),
            pltpu.SemaphoreType.DMA((64,)), pltpu.SemaphoreType.DMA((64,)),
        ],
        compiler_params=pltpu.CompilerParams(collective_id=0, has_side_effects=True, vmem_limit_bytes=63 * 2**20),
    )(cycle_links[0], cross_links[0], latents[0, 0], w_qkv, d_attended[0, 0])
    att_full, dl_out, dw_out = hand_over((att_full, dl_out, dw_out))
    return att_full[None, None], dl_out[None, None], dw_out


def solution(mesh):
    wide = P("fsdp", "view", None, None, None)
    rows = P("fsdp", None)
    return jax.shard_map(
        local,
        mesh=mesh,
        in_specs=(wide, rows, rows, rows, wide),
        out_specs=(wide, wide, rows),
        check_vma=False,
    )
```
